32 devices in a mesh: grp: 4 (over z), shard: 8 (over y, x, core).
Axes of the slice: x: 2, y: 2, z: 4, core: 2. Of those that a mesh axis runs over, the one named last changes fastest.
Arguments:
- inputs: bfloat16 [128, 192, 1024], P(('grp', 'shard')), may hold values from -6 to 6
- cotangent: bfloat16 [128, 192, 1024], P(('grp', 'shard')), may hold values from -6 to 6
- lengths: int32 [128], replicated, may hold values from 1 to 192, as said below
- dealing: int32 [128], replicated, may hold values from 0 to 127, as said below
- g_attn: bfloat16 [1024], P(('grp', 'shard')), may hold values from 0.099609375 to 1.8984375
- w_query: bfloat16 [1024, 512], P(('grp', 'shard')), may hold values from -0.1875 to 0.1875
- w_key: bfloat16 [1024, 512], P(('grp', 'shard')), may hold values from -0.1875 to 0.1875
- w_value: bfloat16 [1024, 1024], P(('grp', 'shard')), may hold values from -0.1875 to 0.1875
- w_outgate: bfloat16 [1024, 1024], P(('grp', 'shard')), may hold values from -0.1875 to 0.1875
- w_lowrank: bfloat16 [1024, 16], P(('grp', 'shard')), may hold values from -0.1875 to 0.1875
- w_forget: bfloat16 [16, 512], P(None, ('grp', 'shard')), may hold values from -0.75 to 0.75
- b_forget: bfloat16 [512], P(('grp', 'shard')), may hold values from -1 to 5
- g_head: bfloat16 [256], P(('grp', 'shard')), may hold values from 0.099609375 to 1.8984375
- w_output: bfloat16 [1024, 1024], P(('grp', 'shard')), may hold values from -0.25 to 0.25
- g_ffn: bfloat16 [1024], P(('grp', 'shard')), may hold values from 0.099609375 to 1.8984375
- w_gate: bfloat16 [1024, 2816], P(('grp', 'shard')), may hold values from -0.1875 to 0.1875
- w_up: bfloat16 [1024, 2816], P(('grp', 'shard')), may hold values from -0.1875 to 0.1875
- w_down: bfloat16 [2816, 1024], P(None, ('grp', 'shard')), may hold values from -0.15625 to 0.15625
Outputs:
- output: bfloat16 [128, 192, 1024], P(('grp', 'shard'))
- grad_input: bfloat16 [128, 192, 1024], P(('grp', 'shard'))
- dg_attn: float32 [1024], P(('grp', 'shard'))
- dw_query: float32 [1024, 512], P(('grp', 'shard'))
- dw_key: float32 [1024, 512], P(('grp', 'shard'))
- dw_value: float32 [1024, 1024], P(('grp', 'shard'))
- dw_outgate: float32 [1024, 1024], P(('grp', 'shard'))
- dw_lowrank: float32 [1024, 16], P(('grp', 'shard'))
- dw_forget: float32 [16, 512], P(None, ('grp', 'shard'))
- db_forget: float32 [512], P(('grp', 'shard'))
- dg_head: float32 [256], P(('grp', 'shard'))
- dw_output: float32 [1024, 1024], P(('grp', 'shard'))
- dg_ffn: float32 [1024], P(('grp', 'shard'))
- dw_gate: float32 [1024, 2816], P(('grp', 'shard'))
- dw_up: float32 [1024, 2816], P(('grp', 'shard'))
- dw_down: float32 [2816, 1024], P(None, ('grp', 'shard'))
The draws below stay inside these ranges and needn't reach their ends.
Inputs may be any that keep to these rules, and one draw needn't show every extreme that they name: dealing[q], for slot q = (m * 32 + r) * 2 + k, is the given position of the sequence that device r takes as its k-th in micro-batch m; a device's given positions are its 4 rows of inputs, and that sequence lies on a device with r's index along shard, at one of its given positions m * 2 to (m + 1) * 2 - 1. Each position is dealt once, and no device deals two sequences of one micro-batch to the same device. lengths[q] is the length of the sequence of slot q (slots as for dealing). Of the 2 slots of one device and micro-batch, exactly one holds 129 to 192 tokens, which take 3 blocks of 64 positions, and each other slot holds 1 to 64 tokens, one block; so the blocks of one device and micro-batch number 4 exactly. Some sequence has exactly 192 tokens.
All inputs are finite; a program needn't handle non-finite values.
Results may differ from the reference program's by a relative error of at most 0.02.
Values may be sent and summed in bfloat16 or wider, within the bound.
A program may use at most 192 MiB of HBM per device.

```python
import jax
import jax.numpy as jnp
from jax import lax

D = 1024
HEADS = 4
DK = 128
DV = 256
RANK = 16
FF = 2816
BLOCK = 64
SEQ_BIN = 2
MB = 2
KD = 512
VD = 1024
LMAX = 192
SEQ_DEV = 4
NSEQ = 128
N_GRP = 4
N_SHARD = 8


def draw_lengths(key, part):
    key = jax.random.fold_in(key, 5)
    bin_count = MB * N_GRP * N_SHARD
    longest = jax.random.randint(jax.random.fold_in(key, 1), (bin_count,), 0, SEQ_BIN, dtype=jnp.int32)
    shortfall = jax.random.randint(jax.random.fold_in(key, 2), (bin_count,), 0, BLOCK, dtype=jnp.int32)
    shortfall = jnp.where(jnp.arange(bin_count, dtype=jnp.int32) == 0, 0, shortfall)
    short_len = jax.random.randint(jax.random.fold_in(key, 3), (bin_count, SEQ_BIN), 1, BLOCK + 1, dtype=jnp.int32)
    is_long = jnp.arange(SEQ_BIN, dtype=jnp.int32)[None, :] == longest[:, None]
    return jnp.where(is_long, (LMAX - shortfall)[:, None], short_len).reshape(-1).astype(jnp.int32)


def group_order(key):
    return jax.random.permutation(key, N_GRP)


def slot_order(key):
    return jax.random.permutation(key, SEQ_BIN)


def draw_dealing(key, part):
    key = jax.random.fold_in(key, 7)
    columns = MB * N_SHARD
    grp_order = jax.vmap(group_order)(jax.random.split(jax.random.fold_in(key, 1), columns))
    shift_ids = jax.vmap(group_order)(jax.random.split(jax.random.fold_in(key, 2), columns))[:, :SEQ_BIN]
    slot_turns = jax.vmap(slot_order)(jax.random.split(jax.random.fold_in(key, 3), columns * N_GRP))
    slot_turns = slot_turns.reshape(columns, N_GRP, SEQ_BIN)
    micro_ids = jnp.arange(MB)[:, None, None, None]
    dest_ids = jnp.arange(N_GRP)[None, :, None, None]
    column_ids = jnp.arange(N_SHARD)[None, None, :, None]
    place_ids = jnp.arange(SEQ_BIN)[None, None, None, :]
    column_sel = micro_ids * N_SHARD + column_ids
    source_grp = grp_order[column_sel, (dest_ids + shift_ids[column_sel, place_ids]) % N_GRP]
    slot_ids = slot_turns[column_sel, source_grp, place_ids]
    given_pos = (source_grp * N_SHARD + column_ids) * (MB * SEQ_BIN) + micro_ids * SEQ_BIN + slot_ids
    return given_pos.reshape(-1).astype(jnp.int32)


def shard_levels(rng, extent, cuts, low, largest):
    def one(dim, parts):
        draws = jax.random.uniform(jax.random.fold_in(jax.random.fold_in(rng, 6), dim), (parts,), jnp.float32, low / len(cuts), largest / len(cuts))
        return jnp.repeat(jnp.exp(draws), extent[dim] // parts).reshape((-1,) + (1,) * (len(extent) - dim - 1))

    gain = one(*cuts[0])
    for cut in cuts[1:]:
        gain = gain * one(*cut)
    return gain


def gaussian(own_key, extent, scale, most, shards=(), kind=jnp.bfloat16):
    level = shard_levels(own_key, extent, shards, -0.22, 0.18) if shards else 1.0
    values = jax.random.normal(own_key, extent, jnp.float32) * scale * level
    return jnp.minimum(jnp.maximum(values, -most), most).astype(kind)


def setup_inputs(seed: int = 0) -> dict:
    keys = jax.random.split(jax.random.key(seed), 19)
    inputs = gaussian(keys[0], (NSEQ, LMAX, D), 1.0, 6.0, ((0, 32),))
    cotangent = gaussian(keys[1], (NSEQ, LMAX, D), 1.0, 6.0, ((0, 32),))
    lengths = draw_lengths(jax.random.fold_in(keys[18], 71), 0)
    dealing = draw_dealing(jax.random.fold_in(keys[18], 71), 0)
    g_attn = jnp.clip(1.0 + 0.18 * jax.random.normal(keys[4], (D,), jnp.float32), 0.099609375, 1.8984375).astype(jnp.bfloat16)
    w_query = gaussian(keys[5], (D, KD), D ** -0.5, 0.1875, ((0, 32),))
    w_key = gaussian(keys[6], (D, KD), D ** -0.5, 0.1875, ((0, 32),))
    w_value = gaussian(keys[7], (D, VD), D ** -0.5, 0.1875, ((0, 32),))
    w_outgate = gaussian(keys[8], (D, VD), D ** -0.5, 0.1875, ((0, 32),))
    w_lowrank = gaussian(keys[9], (D, RANK), D ** -0.5, 0.1875, ((0, 32),))
    w_forget = gaussian(keys[10], (RANK, KD), (4 * RANK) ** -0.5, 0.75, ((1, 32),))
    b_forget = jnp.clip(-1.0 + 6.0 * jax.random.uniform(keys[11], (KD,), jnp.float32) ** shard_levels(keys[11], (KD,), ((0, 32),), -0.2, 0.2), -1.0, 5.0).astype(jnp.bfloat16)
    g_head = jnp.clip(1.0 + 0.18 * jax.random.normal(keys[12], (DV,), jnp.float32), 0.099609375, 1.8984375).astype(jnp.bfloat16)
    w_output = gaussian(keys[13], (VD, D), (VD // 2) ** -0.5, 0.25, ((0, 32),))
    g_ffn = jnp.clip(1.0 + 0.18 * jax.random.normal(keys[14], (D,), jnp.float32), 0.099609375, 1.8984375).astype(jnp.bfloat16)
    w_gate = gaussian(keys[15], (D, FF), D ** -0.5, 0.1875, ((0, 32),))
    w_up = gaussian(keys[16], (D, FF), D ** -0.5, 0.1875, ((0, 32),))
    w_down = gaussian(keys[17], (FF, D), (FF // 2) ** -0.5, 0.15625, ((1, 32),))
    return {"inputs": inputs, "cotangent": cotangent, "lengths": lengths, "dealing": dealing, "g_attn": g_attn, "w_query": w_query, "w_key": w_key, "w_value": w_value, "w_outgate": w_outgate, "w_lowrank": w_lowrank, "w_forget": w_forget, "b_forget": b_forget, "g_head": g_head, "w_output": w_output, "g_ffn": g_ffn, "w_gate": w_gate, "w_up": w_up, "w_down": w_down}


@jax.custom_vjp
def low(v):
    return lax.optimization_barrier(v.astype(jnp.bfloat16)).astype(jnp.float32)

@jax.custom_vjp
def low_back(v):
    return v

def low_keep(v):
    return (low(v), None)

def low_pass(kept, grad):
    return (grad,)

def back_keep(v):
    return (v, None)

def back_low(kept, grad):
    return (low(grad),)
low.defvjp(low_keep, low_pass)
low_back.defvjp(back_keep, back_low)
EPS = 1e-05
HEAD_EPS = 1.0

def matmul(left_mat, right_mat):
    return jnp.dot(left_mat, right_mat, precision=lax.Precision.HIGHEST, preferred_element_type=jnp.float32)

def exact_einsum(form, left_mat, right_mat):
    return jnp.einsum(form, left_mat, right_mat, precision=lax.Precision.HIGHEST, preferred_element_type=jnp.float32)

def scaled_rows(rows_in, gain_vec, offset):
    return rows_in * lax.rsqrt(lax.optimization_barrier(jnp.mean(rows_in * rows_in, axis=-1, keepdims=True)) + offset) * gain_vec

def layer_forward(params, seq_rows):
    g_attn, w_query, w_key, w_value, w_outgate, w_lowrank, w_forget, b_forget, g_head, w_output, g_ffn, w_gate, w_up, w_down = params
    seq_count = seq_rows.shape[0]
    length = seq_rows.shape[1]
    row_count = seq_count * length
    blocks = length // BLOCK
    flat_rows = seq_rows.reshape(row_count, D)
    xn_one = low(scaled_rows(flat_rows, g_attn, EPS))
    queries = low_back(matmul(xn_one, w_query))
    key_rows = low_back(matmul(xn_one, w_key))
    values = low(low_back(matmul(xn_one, w_value)))
    gate_out = low_back(matmul(xn_one, w_outgate))
    lowrank = low(low_back(matmul(xn_one, w_lowrank)))
    forget = jax.nn.log_sigmoid(low_back(matmul(lowrank, w_forget)) + b_forget) / 16.0
    key_shape = (seq_count, blocks, BLOCK, HEADS, DK)
    val_shape = (seq_count, blocks, BLOCK, HEADS, DV)
    running = jnp.cumsum(forget.reshape(key_shape), axis=2)
    tail_sum = running[:, :, -1:]
    q_gate = low(queries.reshape(key_shape) * DK ** (-0.5) * jnp.exp(running))
    k_back = low(key_rows.reshape(key_shape) * jnp.exp(-running))
    k_tail = low(key_rows.reshape(key_shape) * jnp.exp(tail_sum - running))
    val_blocks = values.reshape(val_shape)
    spot_ids = jnp.arange(BLOCK, dtype=jnp.int32)
    causal = (spot_ids[:, None] >= spot_ids[None, :]).astype(jnp.float32)
    scores = exact_einsum('bcthd,bcshd->bchts', q_gate, k_back)
    attn_probs = low(low_back(scores * causal))
    intra_out = exact_einsum('bchts,bcshe->bcthe', attn_probs, val_blocks)
    update = low_back(exact_einsum('bcthd,bcthe->bchde', k_tail, val_blocks))
    decays = jnp.exp(tail_sum[:, :, 0])

    def advance(carried, block_item):
        factor, upd_block = block_item
        return (factor[..., None] * carried + upd_block, carried)
    zero_state = jnp.zeros((seq_count, HEADS, DK, DV), jnp.float32)
    _, before = lax.scan(advance, zero_state, (jnp.moveaxis(decays, 1, 0), jnp.moveaxis(update, 1, 0)))
    before = jnp.moveaxis(before, 0, 1)
    inter_out = exact_einsum('bcthd,bchde->bcthe', q_gate, low(before))
    mixed_out = low_back(intra_out + inter_out).reshape(row_count, HEADS, DV)
    normed = scaled_rows(mixed_out, g_head, HEAD_EPS).reshape(row_count, HEADS * DV)
    gated_out = low(normed * (gate_out * jax.nn.sigmoid(gate_out)))
    resid_one = flat_rows + low_back(matmul(gated_out, w_output))
    xn_two = low(scaled_rows(resid_one, g_ffn, EPS))
    pre_gate = low_back(matmul(xn_two, w_gate))
    pre_up = low_back(matmul(xn_two, w_up))
    hidden = low(jax.nn.silu(pre_gate) * pre_up)
    return (resid_one + low_back(matmul(hidden, w_down))).reshape(seq_count, length, D)

def reference(inputs, cotangent, lengths, dealing, g_attn, w_query, w_key, w_value, w_outgate, w_lowrank, w_forget, b_forget, g_head, w_output, g_ffn, w_gate, w_up, w_down):
    params = tuple((weight.astype(jnp.float32) for weight in (g_attn, w_query, w_key, w_value, w_outgate, w_lowrank, w_forget, b_forget, g_head, w_output, g_ffn, w_gate, w_up, w_down)))
    given_len = jnp.zeros((NSEQ,), jnp.int32).at[dealing.astype(jnp.int32)].set(lengths.astype(jnp.int32))
    live = (jnp.arange(LMAX, dtype=jnp.int32)[None, :] < given_len[:, None]).astype(jnp.float32)
    groups = NSEQ // SEQ_DEV

    def visit(totals, group_item):
        seq_rows, seq_back, seq_live = group_item
        keep = seq_live[..., None]
        rows_f = seq_rows.astype(jnp.float32) * keep
        back_f = seq_back.astype(jnp.float32) * keep
        result, pull = jax.vjp(layer_forward, params, rows_f)
        grads, grad_rows = pull(back_f)
        totals = tuple((acc_part + new_part for acc_part, new_part in zip(totals, grads)))
        return (totals, ((result * keep).astype(jnp.bfloat16), (grad_rows * keep).astype(jnp.bfloat16)))
    start = tuple((jnp.zeros(weight.shape, jnp.float32) for weight in params))
    totals, (outs, grads_in) = lax.scan(visit, start, (inputs.reshape(groups, SEQ_DEV, LMAX, D), cotangent.reshape(groups, SEQ_DEV, LMAX, D), live.reshape(groups, SEQ_DEV, LMAX)))
    return (outs.reshape(NSEQ, LMAX, D), grads_in.reshape(NSEQ, LMAX, D), totals[0], totals[1], totals[2], totals[3], totals[4], totals[5], totals[6], totals[7], totals[8], totals[9], totals[10], totals[11], totals[12], totals[13])
```

```python
import jax
import jax.numpy as jnp
from jax import lax
from jax.sharding import PartitionSpec as P

D = 1024
HEADS = 4
BLOCK = 64


EPS = 1e-05
HEAD_EPS = 1.0


def matmul(left_mat, right_mat):
    return jnp.dot(left_mat, right_mat, preferred_element_type=jnp.float32)


def rows_contract(left_mat, right_mat):
    return lax.dot_general(
        left_mat, right_mat, (((0,), (0,)), ((), ())), preferred_element_type=jnp.float32
    )


def right_transpose(left_mat, right_mat):
    return lax.dot_general(
        left_mat, right_mat, (((1,), (1,)), ((), ())), preferred_element_type=jnp.float32
    )


def scaled_rows(rows_in, gain_vec):
    return rows_in * lax.rsqrt(jnp.mean(rows_in * rows_in, axis=-1, keepdims=True) + EPS) * gain_vec


def head_rows(rows_in, gain_vec):
    return (
        rows_in
        * lax.rsqrt(jnp.mean(rows_in * rows_in, axis=-1, keepdims=True) + HEAD_EPS)
        * gain_vec
    )


def forget_rate(logits):
    return jax.nn.log_sigmoid(logits) / 16.0


def swiglu_core(pre_gate, pre_up):
    return jax.nn.silu(pre_gate) * pre_up


def head_gate(mixed_out, gate_out, head_gain):
    normed = head_rows(mixed_out, head_gain)
    active = gate_out * jax.nn.sigmoid(gate_out)
    return normed.reshape(active.shape) * active


def block_gates(queries, key_rows, forget):
    running = jnp.cumsum(forget, axis=1)
    tail_sum = running[:, -1:]
    q_gate = queries * queries.shape[-1] ** (-0.5) * jnp.exp(running)
    k_back = key_rows * jnp.exp(-running)
    k_tail = key_rows * jnp.exp(tail_sum - running)
    return (q_gate, k_back, k_tail, jnp.exp(tail_sum[:, 0]))


def layer_pass(weights, rows_in, back_in, seq_count):
    (
        g_attn,
        w_query,
        w_key,
        w_value,
        w_outgate,
        w_lowrank,
        w_forget,
        b_forget,
        g_head,
        w_output,
        g_ffn,
        w_gate,
        w_up,
        w_down,
    ) = weights
    row_count = rows_in.shape[0]
    blocks = row_count // BLOCK
    key_dim = w_query.shape[1] // HEADS
    val_dim = w_value.shape[1] // HEADS
    key_shape = (blocks, BLOCK, HEADS, key_dim)
    val_shape = (blocks, BLOCK, HEADS, val_dim)
    flat_rows = rows_in.astype(jnp.float32)
    norm_one, pull_one = jax.vjp(scaled_rows, flat_rows, g_attn.astype(jnp.float32))
    xn_one = norm_one.astype(jnp.bfloat16)
    queries = matmul(xn_one, w_query)
    key_rows = matmul(xn_one, w_key)
    values = matmul(xn_one, w_value).astype(jnp.bfloat16)
    gate_out = matmul(xn_one, w_outgate)
    lowrank = matmul(xn_one, w_lowrank).astype(jnp.bfloat16)
    logits = matmul(lowrank, w_forget) + b_forget.astype(jnp.float32)
    forget, pull_forget = jax.vjp(forget_rate, logits)
    gate_vals, pull_gates = jax.vjp(
        block_gates,
        queries.reshape(key_shape),
        key_rows.reshape(key_shape),
        forget.reshape(key_shape),
    )
    q_gate = gate_vals[0].astype(jnp.bfloat16)
    k_back = gate_vals[1].astype(jnp.bfloat16)
    k_tail = gate_vals[2].astype(jnp.bfloat16)
    decays = gate_vals[3]
    val_blocks = values.reshape(val_shape)
    spot_ids = jnp.arange(BLOCK)
    causal = (spot_ids[:, None] >= spot_ids[None, :]).astype(jnp.float32)
    scores = jnp.einsum("cthd,cshd->chts", q_gate, k_back, preferred_element_type=jnp.float32)
    attn_probs = (scores * causal).astype(jnp.bfloat16)
    intra_out = jnp.einsum(
        "chts,cshe->cthe", attn_probs, val_blocks, preferred_element_type=jnp.float32
    )
    update = jnp.einsum("cthd,cthe->chde", k_tail, val_blocks, preferred_element_type=jnp.float32)

    per_seq = blocks // seq_count
    seq_blocks = (seq_count, per_seq) + update.shape[1:]
    upd_seq = update.reshape(seq_blocks)
    decay_seq = decays.reshape((seq_count, per_seq) + decays.shape[1:])
    carried = jnp.zeros_like(upd_seq[:, 0])
    before_list = []
    for idx in range(per_seq):
        before_list.append(carried)
        carried = decay_seq[:, idx][..., None] * carried + upd_seq[:, idx]
    before_seq = jnp.stack(before_list, axis=1)
    before_low = before_seq.reshape(update.shape).astype(jnp.bfloat16)
    inter_out = jnp.einsum(
        "cthd,chde->cthe", q_gate, before_low, preferred_element_type=jnp.float32
    )
    mixed_out = (intra_out + inter_out).reshape(row_count, HEADS, val_dim)
    gated_f, pull_head = jax.vjp(head_gate, mixed_out, gate_out, g_head.astype(jnp.float32))
    gated_out = gated_f.astype(jnp.bfloat16)
    resid_one = flat_rows + matmul(gated_out, w_output)
    norm_two, pull_two = jax.vjp(scaled_rows, resid_one, g_ffn.astype(jnp.float32))
    xn_two = norm_two.astype(jnp.bfloat16)
    pre_gate = matmul(xn_two, w_gate)
    pre_up = matmul(xn_two, w_up)
    hidden_f, pull_ffn = jax.vjp(swiglu_core, pre_gate, pre_up)
    hidden = hidden_f.astype(jnp.bfloat16)
    output = (resid_one + matmul(hidden, w_down)).astype(jnp.bfloat16)
    back_f = back_in.astype(jnp.float32)
    dw_down = rows_contract(hidden, back_in)
    d_hidden = right_transpose(back_in, w_down)
    d_pre_gate, d_pre_up = pull_ffn(d_hidden)
    d_gate_low = d_pre_gate.astype(jnp.bfloat16)
    d_up_low = d_pre_up.astype(jnp.bfloat16)
    dw_gate = rows_contract(xn_two, d_gate_low)
    dw_up = rows_contract(xn_two, d_up_low)
    d_norm_two = right_transpose(d_gate_low, w_gate) + right_transpose(d_up_low, w_up)
    d_resid_part, dg_ffn = pull_two(d_norm_two)
    d_resid = back_f + d_resid_part
    d_attn = d_resid.astype(jnp.bfloat16)
    dw_output = rows_contract(gated_out, d_attn)
    d_gated = right_transpose(d_attn, w_output)
    d_mixed_f, d_gate_out_f, dg_head = pull_head(d_gated)
    d_mixed = d_mixed_f.astype(jnp.bfloat16).reshape(val_shape)
    d_scores = jnp.einsum(
        "cthe,cshe->chts", d_mixed, val_blocks, preferred_element_type=jnp.float32
    )
    d_probs = (d_scores * causal).astype(jnp.bfloat16)
    d_q_gate = jnp.einsum(
        "chts,cshd->cthd", d_probs, k_back, preferred_element_type=jnp.float32
    ) + jnp.einsum("cthe,chde->cthd", d_mixed, before_low, preferred_element_type=jnp.float32)
    d_k_back = jnp.einsum("chts,cthd->cshd", d_probs, q_gate, preferred_element_type=jnp.float32)
    d_val_intra = jnp.einsum(
        "chts,cthe->cshe", attn_probs, d_mixed, preferred_element_type=jnp.float32
    )
    d_before = jnp.einsum("cthd,cthe->chde", q_gate, d_mixed, preferred_element_type=jnp.float32)

    d_before_seq = d_before.reshape(seq_blocks)
    d_after = jnp.zeros_like(upd_seq[:, 0])
    d_update_list = []
    d_decay_list = []
    for idx in reversed(range(per_seq)):
        d_update_list.append(d_after)
        d_decay_list.append(jnp.sum(d_after * before_seq[:, idx], axis=-1))
        d_after = d_before_seq[:, idx] + decay_seq[:, idx][..., None] * d_after
    d_update = jnp.stack(d_update_list[::-1], axis=1).reshape(update.shape)
    d_decays = jnp.stack(d_decay_list[::-1], axis=1).reshape(decays.shape)
    d_update_low = d_update.astype(jnp.bfloat16)
    d_k_tail = jnp.einsum(
        "cthe,chde->cthd", val_blocks, d_update_low, preferred_element_type=jnp.float32
    )
    d_values = (
        (
            d_val_intra
            + jnp.einsum(
                "cthd,chde->cthe", k_tail, d_update_low, preferred_element_type=jnp.float32
            )
        )
        .reshape(row_count, -1)
        .astype(jnp.bfloat16)
    )
    d_query_f, d_key_f, d_forget = pull_gates((d_q_gate, d_k_back, d_k_tail, d_decays))
    d_queries = d_query_f.reshape(row_count, -1).astype(jnp.bfloat16)
    d_keys = d_key_f.reshape(row_count, -1).astype(jnp.bfloat16)
    (d_logits,) = pull_forget(d_forget.reshape(row_count, -1))
    db_forget = jnp.sum(d_logits, axis=0)
    d_logit_low = d_logits.astype(jnp.bfloat16)
    dw_forget = rows_contract(lowrank, d_logit_low)
    d_lowrank = right_transpose(d_logit_low, w_forget).astype(jnp.bfloat16)
    d_gate_out = d_gate_out_f.astype(jnp.bfloat16)
    dw_query = rows_contract(xn_one, d_queries)
    dw_key = rows_contract(xn_one, d_keys)
    dw_value = rows_contract(xn_one, d_values)
    dw_outgate = rows_contract(xn_one, d_gate_out)
    dw_lowrank = rows_contract(xn_one, d_lowrank)
    d_norm_one = (
        right_transpose(d_queries, w_query)
        + right_transpose(d_keys, w_key)
        + right_transpose(d_values, w_value)
        + right_transpose(d_gate_out, w_outgate)
        + right_transpose(d_lowrank, w_lowrank)
    )
    d_flat, dg_attn = pull_one(d_norm_one)
    grad_rows = (d_resid + d_flat).astype(jnp.bfloat16)
    grads = (
        dg_attn,
        dw_query,
        dw_key,
        dw_value,
        dw_outgate,
        dw_lowrank,
        dw_forget,
        db_forget,
        dg_head,
        dw_output,
        dg_ffn,
        dw_gate,
        dw_up,
        dw_down,
    )
    return (output, grad_rows, grads)


def shards(
    inputs,
    cotangent,
    lengths,
    dealing,
    g_attn,
    w_query,
    w_key,
    w_value,
    w_outgate,
    w_lowrank,
    w_forget,
    b_forget,
    g_head,
    w_output,
    g_ffn,
    w_gate,
    w_up,
    w_down,
):
    axes = ("grp", "shard")
    shard_count = lax.axis_size("shard")
    self_index = lax.axis_index("grp") * shard_count + lax.axis_index("shard")
    seq_dev, max_len, _ = inputs.shape
    own_given = self_index * seq_dev + jnp.arange(seq_dev, dtype=jnp.int32)
    own_len = jnp.sum(jnp.where(dealing[None, :] == own_given[:, None], lengths[None, :], 0), axis=1)
    live = jnp.arange(max_len, dtype=jnp.int32)[None, :] < own_len[:, None]
    zero_low = jnp.zeros((), jnp.bfloat16)
    rows_in = jnp.where(live[..., None], inputs, zero_low).reshape(seq_dev * max_len, D)
    back_in = jnp.where(live[..., None], cotangent, zero_low).reshape(seq_dev * max_len, D)
    shard_weights = (
        g_attn,
        w_query,
        w_key,
        w_value,
        w_outgate,
        w_lowrank,
        w_forget,
        b_forget,
        g_head,
        w_output,
        g_ffn,
        w_gate,
        w_up,
        w_down,
    )
    grad_dims = (0, 0, 0, 0, 0, 0, 1, 0, 0, 0, 0, 0, 0, 1)
    gathered = tuple(
        lax.all_gather(weight, axes, axis=dim, tiled=True)
        for weight, dim in zip(shard_weights, grad_dims)
    )
    out_rows, grad_rows, grads = layer_pass(gathered, rows_in, back_in, seq_dev)
    reduced = tuple(
        lax.psum_scatter(
            grad.astype(jnp.bfloat16), axes, scatter_dimension=dim, tiled=True
        ).astype(jnp.float32)
        for grad, dim in zip(grads, grad_dims)
    )
    return (out_rows.reshape(inputs.shape), grad_rows.reshape(inputs.shape)) + reduced


def solution(mesh):
    return jax.shard_map(
        shards,
        mesh=mesh,
        in_specs=(
            P(("grp", "shard"), None, None),
            P(("grp", "shard"), None, None),
            P(),
            P(),
            P(("grp", "shard")),
            P(("grp", "shard"), None),
            P(("grp", "shard"), None),
            P(("grp", "shard"), None),
            P(("grp", "shard"), None),
            P(("grp", "shard"), None),
            P(None, ("grp", "shard")),
            P(("grp", "shard")),
            P(("grp", "shard")),
            P(("grp", "shard"), None),
            P(("grp", "shard")),
            P(("grp", "shard"), None),
            P(("grp", "shard"), None),
            P(None, ("grp", "shard")),
        ),
        out_specs=(
            P(("grp", "shard"), None, None),
            P(("grp", "shard"), None, None),
            P(("grp", "shard")),
            P(("grp", "shard"), None),
            P(("grp", "shard"), None),
            P(("grp", "shard"), None),
            P(("grp", "shard"), None),
            P(("grp", "shard"), None),
            P(None, ("grp", "shard")),
            P(("grp", "shard")),
            P(("grp", "shard")),
            P(("grp", "shard"), None),
            P(("grp", "shard")),
            P(("grp", "shard"), None),
            P(("grp", "shard"), None),
            P(None, ("grp", "shard")),
        ),
        check_vma=False,
    )
```

```python
import jax
import jax.numpy as jnp
from jax import lax
from jax.experimental import pallas as pl
from jax.experimental.pallas import tpu as pltpu
from jax.sharding import PartitionSpec as P

D = 1024
HEADS = 4
BLOCK = 64


EPS = 1e-05
HEAD_EPS = 1.0

MESH = pl.DeviceIdType.MESH
DMA = pltpu.SemaphoreType.DMA
GRP = 4
SHARD = 8
ROWS = 32
WIDE = 768
FF_CUT = 256
SLOTS = 6
MISC = 128


def matmul(left_mat, right_mat):
    return jnp.dot(left_mat, right_mat, preferred_element_type=jnp.float32)


def rows_contract(left_mat, right_mat):
    return lax.dot_general(
        left_mat, right_mat, (((0,), (0,)), ((), ())), preferred_element_type=jnp.float32
    )


def right_transpose(left_mat, right_mat):
    return lax.dot_general(
        left_mat, right_mat, (((1,), (1,)), ((), ())), preferred_element_type=jnp.float32
    )


def scaled_rows(rows_in, gain_vec):
    return rows_in * lax.rsqrt(jnp.mean(rows_in * rows_in, axis=-1, keepdims=True) + EPS) * gain_vec


def head_rows(rows_in, gain_vec):
    return (
        rows_in
        * lax.rsqrt(jnp.mean(rows_in * rows_in, axis=-1, keepdims=True) + HEAD_EPS)
        * gain_vec
    )


def forget_rate(logits):
    return jax.nn.log_sigmoid(logits) / 16.0


def swiglu_core(pre_gate, pre_up):
    return jax.nn.silu(pre_gate) * pre_up


def head_gate(mixed_out, gate_out, head_gain):
    normed = head_rows(mixed_out, head_gain)
    active = gate_out * jax.nn.sigmoid(gate_out)
    return normed.reshape(active.shape) * active


def block_gates(queries, key_rows, forget):
    running = jnp.cumsum(forget, axis=1)
    tail_sum = running[:, -1:]
    q_gate = queries * queries.shape[-1] ** (-0.5) * jnp.exp(running)
    k_back = key_rows * jnp.exp(-running)
    k_tail = key_rows * jnp.exp(tail_sum - running)
    return (q_gate, k_back, k_tail, jnp.exp(tail_sum[:, 0]))


def layer_pass(weights, rows_in, back_in, seq_count):
    (
        g_attn,
        w_query,
        w_key,
        w_value,
        w_outgate,
        w_lowrank,
        w_forget,
        b_forget,
        g_head,
        w_output,
        g_ffn,
        w_gate,
        w_up,
        w_down,
    ) = weights
    row_count = rows_in.shape[0]
    blocks = row_count // BLOCK
    key_dim = w_query.shape[1] // HEADS
    val_dim = w_value.shape[1] // HEADS
    key_shape = (blocks, BLOCK, HEADS, key_dim)
    val_shape = (blocks, BLOCK, HEADS, val_dim)
    flat_rows = rows_in.astype(jnp.float32)
    norm_one, pull_one = jax.vjp(scaled_rows, flat_rows, g_attn.astype(jnp.float32))
    xn_one = norm_one.astype(jnp.bfloat16)
    queries = matmul(xn_one, w_query)
    key_rows = matmul(xn_one, w_key)
    values = matmul(xn_one, w_value).astype(jnp.bfloat16)
    gate_out = matmul(xn_one, w_outgate)
    lowrank = matmul(xn_one, w_lowrank).astype(jnp.bfloat16)
    logits = matmul(lowrank, w_forget) + b_forget.astype(jnp.float32)
    forget, pull_forget = jax.vjp(forget_rate, logits)
    gate_vals, pull_gates = jax.vjp(
        block_gates,
        queries.reshape(key_shape),
        key_rows.reshape(key_shape),
        forget.reshape(key_shape),
    )
    q_gate = gate_vals[0].astype(jnp.bfloat16)
    k_back = gate_vals[1].astype(jnp.bfloat16)
    k_tail = gate_vals[2].astype(jnp.bfloat16)
    decays = gate_vals[3]
    val_blocks = values.reshape(val_shape)
    spot_ids = jnp.arange(BLOCK)
    causal = (spot_ids[:, None] >= spot_ids[None, :]).astype(jnp.float32)
    scores = jnp.einsum("cthd,cshd->chts", q_gate, k_back, preferred_element_type=jnp.float32)
    attn_probs = (scores * causal).astype(jnp.bfloat16)
    intra_out = jnp.einsum(
        "chts,cshe->cthe", attn_probs, val_blocks, preferred_element_type=jnp.float32
    )
    update = jnp.einsum("cthd,cthe->chde", k_tail, val_blocks, preferred_element_type=jnp.float32)

    per_seq = blocks // seq_count
    seq_blocks = (seq_count, per_seq) + update.shape[1:]
    upd_seq = update.reshape(seq_blocks)
    decay_seq = decays.reshape((seq_count, per_seq) + decays.shape[1:])
    carried = jnp.zeros_like(upd_seq[:, 0])
    before_list = []
    for idx in range(per_seq):
        before_list.append(carried)
        carried = decay_seq[:, idx][..., None] * carried + upd_seq[:, idx]
    before_seq = jnp.stack(before_list, axis=1)
    before_low = before_seq.reshape(update.shape).astype(jnp.bfloat16)
    inter_out = jnp.einsum(
        "cthd,chde->cthe", q_gate, before_low, preferred_element_type=jnp.float32
    )
    mixed_out = (intra_out + inter_out).reshape(row_count, HEADS, val_dim)
    gated_f, pull_head = jax.vjp(head_gate, mixed_out, gate_out, g_head.astype(jnp.float32))
    gated_out = gated_f.astype(jnp.bfloat16)
    resid_one = flat_rows + matmul(gated_out, w_output)
    norm_two, pull_two = jax.vjp(scaled_rows, resid_one, g_ffn.astype(jnp.float32))
    xn_two = norm_two.astype(jnp.bfloat16)
    pre_gate = matmul(xn_two, w_gate)
    pre_up = matmul(xn_two, w_up)
    hidden_f, pull_ffn = jax.vjp(swiglu_core, pre_gate, pre_up)
    hidden = hidden_f.astype(jnp.bfloat16)
    output = (resid_one + matmul(hidden, w_down)).astype(jnp.bfloat16)
    back_f = back_in.astype(jnp.float32)
    dw_down = rows_contract(hidden, back_in)
    d_hidden = right_transpose(back_in, w_down)
    d_pre_gate, d_pre_up = pull_ffn(d_hidden)
    d_gate_low = d_pre_gate.astype(jnp.bfloat16)
    d_up_low = d_pre_up.astype(jnp.bfloat16)
    dw_gate = rows_contract(xn_two, d_gate_low)
    dw_up = rows_contract(xn_two, d_up_low)
    d_norm_two = right_transpose(d_gate_low, w_gate) + right_transpose(d_up_low, w_up)
    d_resid_part, dg_ffn = pull_two(d_norm_two)
    d_resid = back_f + d_resid_part
    d_attn = d_resid.astype(jnp.bfloat16)
    dw_output = rows_contract(gated_out, d_attn)
    d_gated = right_transpose(d_attn, w_output)
    d_mixed_f, d_gate_out_f, dg_head = pull_head(d_gated)
    d_mixed = d_mixed_f.astype(jnp.bfloat16).reshape(val_shape)
    d_scores = jnp.einsum(
        "cthe,cshe->chts", d_mixed, val_blocks, preferred_element_type=jnp.float32
    )
    d_probs = (d_scores * causal).astype(jnp.bfloat16)
    d_q_gate = jnp.einsum(
        "chts,cshd->cthd", d_probs, k_back, preferred_element_type=jnp.float32
    ) + jnp.einsum("cthe,chde->cthd", d_mixed, before_low, preferred_element_type=jnp.float32)
    d_k_back = jnp.einsum("chts,cthd->cshd", d_probs, q_gate, preferred_element_type=jnp.float32)
    d_val_intra = jnp.einsum(
        "chts,cthe->cshe", attn_probs, d_mixed, preferred_element_type=jnp.float32
    )
    d_before = jnp.einsum("cthd,cthe->chde", q_gate, d_mixed, preferred_element_type=jnp.float32)

    d_before_seq = d_before.reshape(seq_blocks)
    d_after = jnp.zeros_like(upd_seq[:, 0])
    d_update_list = []
    d_decay_list = []
    for idx in reversed(range(per_seq)):
        d_update_list.append(d_after)
        d_decay_list.append(jnp.sum(d_after * before_seq[:, idx], axis=-1))
        d_after = d_before_seq[:, idx] + decay_seq[:, idx][..., None] * d_after
    d_update = jnp.stack(d_update_list[::-1], axis=1).reshape(update.shape)
    d_decays = jnp.stack(d_decay_list[::-1], axis=1).reshape(decays.shape)
    d_update_low = d_update.astype(jnp.bfloat16)
    d_k_tail = jnp.einsum(
        "cthe,chde->cthd", val_blocks, d_update_low, preferred_element_type=jnp.float32
    )
    d_values = (
        (
            d_val_intra
            + jnp.einsum(
                "cthd,chde->cthe", k_tail, d_update_low, preferred_element_type=jnp.float32
            )
        )
        .reshape(row_count, -1)
        .astype(jnp.bfloat16)
    )
    d_query_f, d_key_f, d_forget = pull_gates((d_q_gate, d_k_back, d_k_tail, d_decays))
    d_queries = d_query_f.reshape(row_count, -1).astype(jnp.bfloat16)
    d_keys = d_key_f.reshape(row_count, -1).astype(jnp.bfloat16)
    (d_logits,) = pull_forget(d_forget.reshape(row_count, -1))
    db_forget = jnp.sum(d_logits, axis=0)
    d_logit_low = d_logits.astype(jnp.bfloat16)
    dw_forget = rows_contract(lowrank, d_logit_low)
    d_lowrank = right_transpose(d_logit_low, w_forget).astype(jnp.bfloat16)
    d_gate_out = d_gate_out_f.astype(jnp.bfloat16)
    dw_query = rows_contract(xn_one, d_queries)
    dw_key = rows_contract(xn_one, d_keys)
    dw_value = rows_contract(xn_one, d_values)
    dw_outgate = rows_contract(xn_one, d_gate_out)
    dw_lowrank = rows_contract(xn_one, d_lowrank)
    d_norm_one = (
        right_transpose(d_queries, w_query)
        + right_transpose(d_keys, w_key)
        + right_transpose(d_values, w_value)
        + right_transpose(d_gate_out, w_outgate)
        + right_transpose(d_lowrank, w_lowrank)
    )
    d_flat, dg_attn = pull_one(d_norm_one)
    grad_rows = (d_resid + d_flat).astype(jnp.bfloat16)
    grads = (
        dg_attn,
        dw_query,
        dw_key,
        dw_value,
        dw_outgate,
        dw_lowrank,
        dw_forget,
        db_forget,
        dg_head,
        dw_output,
        dg_ffn,
        dw_gate,
        dw_up,
        dw_down,
    )
    return (output, grad_rows, grads)


def flip(index, bit):
    return index + bit - 2 * bit * lax.rem(index // bit, 2)


def remote(src, dst, send_sem, recv_sem, device):
    return pltpu.make_async_remote_copy(
        src_ref=src,
        dst_ref=dst,
        send_sem=send_sem,
        recv_sem=recv_sem,
        device_id=device,
        device_id_type=MESH,
    )


def start_all(copies):
    for copy in copies:
        copy.start()


def recv_all(copies):
    for copy in copies:
        copy.wait_recv()


def sent_all(copies):
    for copy in copies:
        copy.wait_send()


class Place:
    def __init__(self):
        self.z = lax.axis_index("grp")
        self.s = lax.axis_index("shard")
        self.sib = flip(self.s, 1)
        self.xn = flip(self.s, 2)
        self.yn = flip(self.s, 4)
        self.dg = flip(self.xn, 4)
        self.sets = [self.s, self.xn, self.yn, self.dg]
        self.z_peers = [lax.rem(self.z + step, GRP) for step in range(1, GRP)]
        self.z_from = [lax.rem(self.z + GRP - step, GRP) for step in range(1, GRP)]

    def greet(self):
        barrier = pltpu.get_barrier_semaphore()
        peers = [(peer, self.s) for peer in self.z_peers]
        peers += [(self.z, self.sib), (self.z, self.xn), (self.z, self.yn)]
        for peer in peers:
            pl.semaphore_signal(barrier, inc=1, device_id=peer, device_id_type=MESH)
        return (barrier, len(peers))


class Gather:
    def __init__(self, place, src, full, sems):
        self.p = place
        self.src = src
        self.full = full
        (
            self.ls,
            self.zs,
            self.zr,
            self.xs,
            self.xr,
            self.ds,
            self.dr,
            self.ss,
            self.sr,
        ) = sems

    def local(self, c):
        p = self.p
        return pltpu.make_async_copy(self.src.at[c], self.full.at[c, p.z, p.s], self.ls.at[c])

    def line(self, c):
        p = self.p
        return [
            remote(
                self.src.at[c],
                self.full.at[c, p.z, p.s],
                self.zs.at[c, k],
                self.zr.at[c, k],
                (p.z_peers[k], p.s),
            )
            for k in range(GRP - 1)
        ]

    def line_in(self, c):
        p = self.p
        return [
            remote(
                self.src.at[c],
                self.full.at[c, p.z_from[k], p.s],
                self.zs.at[c, k],
                self.zr.at[c, k],
                (p.z_peers[k], p.s),
            )
            for k in range(GRP - 1)
        ]

    def moved(self, c, set_id, part, send, recv, k, device):
        view = self.full.at[c, part, set_id]
        return remote(view, view, send.at[c, k], recv.at[c, k], device)

    def plane(self, c):
        p = self.p
        whole = pl.ds(0, GRP)
        return [
            self.moved(c, p.s, whole, self.xs, self.xr, 0, (p.z, p.xn)),
            self.moved(c, p.s, whole, self.xs, self.xr, 1, (p.z, p.yn)),
        ]

    def plane_in(self, c):
        p = self.p
        whole = pl.ds(0, GRP)
        return [
            self.moved(c, p.xn, whole, self.xs, self.xr, 0, (p.z, p.xn)),
            self.moved(c, p.yn, whole, self.xs, self.xr, 1, (p.z, p.yn)),
        ]

    def corner(self, c):
        p = self.p
        low, high = pl.ds(0, 2), pl.ds(2, 2)
        return [
            self.moved(c, p.xn, low, self.ds, self.dr, 0, (p.z, p.yn)),
            self.moved(c, p.yn, high, self.ds, self.dr, 1, (p.z, p.xn)),
        ]

    def corner_in(self, c):
        p = self.p
        low, high = pl.ds(0, 2), pl.ds(2, 2)
        return [
            self.moved(c, p.dg, low, self.ds, self.dr, 0, (p.z, p.yn)),
            self.moved(c, p.dg, high, self.ds, self.dr, 1, (p.z, p.xn)),
        ]

    def other(self, c, k):
        p = self.p
        return self.moved(c, p.sets[k], pl.ds(0, GRP), self.ss, self.sr, k, (p.z, p.sib))

    def other_in(self, c):
        p = self.p
        return [
            self.moved(c, flip(p.sets[k], 1), pl.ds(0, GRP), self.ss, self.sr, k, (p.z, p.sib))
            for k in range(4)
        ]

    def step(self, t, chunks, ahead):
        if t + ahead < chunks:
            start_all(self.line(t + ahead))
        if t < chunks:
            self.local(t).wait()
            recv_all(self.line_in(t))
            start_all(self.plane(t))
            self.other(t, 0).start()
        if 0 <= t - 1 < chunks:
            recv_all(self.plane_in(t - 1))
            start_all(self.corner(t - 1))
            self.other(t - 1, 1).start()
            self.other(t - 1, 2).start()
        if 0 <= t - 2 < chunks:
            recv_all(self.corner_in(t - 2))
            self.other(t - 2, 3).start()
        if 0 <= t - 3 < chunks:
            recv_all(self.other_in(t - 3))

    def drain(self, c):
        sent_all(self.line(c) + self.plane(c) + self.corner(c))
        sent_all([self.other(c, k) for k in range(4)])


def gather_sems(chunks):
    counts = (3, 3, 2, 2, 2, 2, 4, 4)
    return [DMA((chunks,))] + [DMA((chunks, count)) for count in counts]


def gather_kernel(src, full, *sems):
    chunks = src.shape[0]
    place = Place()
    barrier, greeted = place.greet()
    gather = Gather(place, src, full, sems)
    start_all([gather.local(c) for c in range(chunks)])
    pl.semaphore_wait(barrier, greeted)
    ahead = 3
    for c in range(ahead):
        start_all(gather.line(c))
    for t in range(chunks + 3):
        gather.step(t, chunks, ahead)
    for c in range(chunks):
        gather.drain(c)


def gather_call(src):
    chunks = src.shape[0]
    return pl.pallas_call(
        gather_kernel,
        out_shape=jax.ShapeDtypeStruct((chunks, GRP, SHARD, ROWS, WIDE), jnp.bfloat16),
        in_specs=[pl.BlockSpec(memory_space=pl.ANY)],
        out_specs=pl.BlockSpec(memory_space=pl.ANY),
        scratch_shapes=gather_sems(chunks),
        compiler_params=pltpu.CompilerParams(
            collective_id=0, has_side_effects=True, vmem_limit_bytes=32 << 20
        ),
    )(src)


class Reduce:
    def __init__(self, place, src, out, bufs, sems):
        self.p = place
        self.src = src
        self.out = out
        self.own, self.b1, self.b2, self.b3, self.b4 = bufs
        (
            self.ls,
            self.s1,
            self.r1,
            self.s2,
            self.r2,
            self.s3,
            self.r3,
            self.s4,
            self.r4,
        ) = sems

    def local(self, c):
        p, k = self.p, c % SLOTS
        return [
            pltpu.make_async_copy(
                self.src.at[c, :, p.sets[j]], self.own.at[k, j], self.ls.at[k, j]
            )
            for j in range(4)
        ]

    def other(self, c):
        p, k = self.p, c % SLOTS
        return [
            remote(
                self.src.at[c, :, flip(p.sets[j], 1)],
                self.b1.at[k, j],
                self.s1.at[k, j],
                self.r1.at[k, j],
                (p.z, p.sib),
            )
            for j in range(4)
        ]

    def corner(self, c):
        p, k = self.p, c % SLOTS
        peers = [(p.z, p.xn), (p.z, p.yn)]
        return [
            remote(
                self.own.at[k, 3, pl.ds(2 * i, 2)],
                self.b2.at[k, i],
                self.s2.at[k, i],
                self.r2.at[k, i],
                peers[i],
            )
            for i in range(2)
        ]

    def plane(self, c):
        p, k = self.p, c % SLOTS
        peers = [(p.z, p.xn), (p.z, p.yn)]
        return [
            remote(
                self.own.at[k, 1 + i],
                self.b3.at[k, i],
                self.s3.at[k, i],
                self.r3.at[k, i],
                peers[i],
            )
            for i in range(2)
        ]

    def line(self, c):
        p, k = self.p, c % SLOTS
        return [
            remote(
                self.own.at[k, 0, p.z_peers[i]],
                self.b4.at[k, i],
                self.s4.at[k, i],
                self.r4.at[k, i],
                (p.z_peers[i], p.s),
            )
            for i in range(GRP - 1)
        ]

    def drain(self, c):
        sent_all(self.other(c) + self.corner(c) + self.plane(c) + self.line(c))

    def enter(self, c):
        if c >= SLOTS:
            self.drain(c - SLOTS)
        start_all(self.local(c))
        start_all(self.other(c))

    def add_other(self, c):
        k = c % SLOTS
        for copy in self.local(c):
            copy.wait()
        recv_all(self.other(c))
        for j in (3, 2, 1, 0):
            total = self.own[k, j].astype(jnp.float32) + self.b1[k, j].astype(jnp.float32)
            self.own[k, j] = total.astype(jnp.bfloat16)
            if j == 3:
                start_all(self.corner(c))

    def add_corner(self, c):
        k = c % SLOTS
        recv_all(self.corner(c))
        for j, lo, i in ((2, 0, 0), (1, 2, 1)):
            total = self.own[k, j, lo : lo + 2].astype(jnp.float32) + self.b2[k, i].astype(
                jnp.float32
            )
            self.own[k, j, lo : lo + 2] = total.astype(jnp.bfloat16)
        start_all(self.plane(c))

    def add_plane(self, c):
        k = c % SLOTS
        recv_all(self.plane(c))
        total = self.own[k, 0].astype(jnp.float32)
        total += self.b3[k, 0].astype(jnp.float32)
        total += self.b3[k, 1].astype(jnp.float32)
        self.own[k, 0] = total.astype(jnp.bfloat16)
        start_all(self.line(c))

    def finish(self, c):
        k = c % SLOTS
        recv_all(self.line(c))
        total = self.own[k, 0, self.p.z].astype(jnp.float32)
        for i in range(GRP - 1):
            total += self.b4[k, i].astype(jnp.float32)
        self.out[c] = total

    def step(self, t, chunks):
        if t + 1 < chunks:
            self.enter(t + 1)
        if t < chunks:
            self.add_other(t)
        if 0 <= t - 1 < chunks:
            self.add_corner(t - 1)
        if 0 <= t - 2 < chunks:
            self.add_plane(t - 2)
        if 0 <= t - 3 < chunks:
            self.finish(t - 3)


def reduce_scratch():
    def buf(*shape):
        return pltpu.VMEM((SLOTS,) + shape + (ROWS, WIDE), jnp.bfloat16)

    bufs = [buf(4, GRP), buf(4, GRP), buf(2, 2), buf(2, GRP), buf(GRP - 1)]
    counts = (4, 4, 4, 2, 2, 2, 2, 3, 3)
    return bufs + [DMA((SLOTS, count)) for count in counts]


def reduce_kernel(src, out, *scratch):
    chunks = src.shape[0]
    place = Place()
    barrier, greeted = place.greet()
    red = Reduce(place, src, out, scratch[:5], scratch[5:])
    pl.semaphore_wait(barrier, greeted)
    red.enter(0)
    for t in range(chunks + 3):
        red.step(t, chunks)
    for c in range(max(0, chunks - SLOTS), chunks):
        red.drain(c)


def reduce_call(src):
    chunks = src.shape[0]
    return pl.pallas_call(
        reduce_kernel,
        out_shape=jax.ShapeDtypeStruct((chunks, ROWS, WIDE), jnp.float32),
        in_specs=[pl.BlockSpec(memory_space=pl.ANY)],
        scratch_shapes=reduce_scratch(),
        compiler_params=pltpu.CompilerParams(
            collective_id=1, has_side_effects=True, vmem_limit_bytes=48 << 20
        ),
    )(src)


def pad_cols(mat, width):
    return jnp.pad(mat, ((0, 0), (0, width - mat.shape[1])))


def pad_rows(mat, rows):
    return jnp.pad(mat, ((0, rows - mat.shape[0]), (0, 0)))


def pack(parts, rows):
    (
        g_attn,
        w_query,
        w_key,
        w_value,
        w_outgate,
        w_lowrank,
        forget_t,
        b_forget,
        g_head,
        w_output,
        g_ffn,
        w_gate,
        w_up,
        down_t,
    ) = parts
    devs = rows // ROWS

    def spread(mat):
        cut = mat.reshape(devs, -1, mat.shape[1])
        return jnp.pad(cut, ((0, 0), (0, ROWS - cut.shape[1]), (0, 0))).reshape(rows, -1)

    misc = jnp.concatenate(
        [
            w_lowrank,
            g_attn[:, None],
            g_ffn[:, None],
            spread(g_head[:, None]),
            jnp.zeros((rows, 13), w_lowrank.dtype),
            spread(forget_t),
            spread(b_forget[:, None]),
        ],
        axis=1,
    )
    mixer = jnp.concatenate(
        [pad_cols(misc, MISC), w_query, w_key, w_value, w_outgate, w_output], axis=1
    )
    heads = -(-mixer.shape[1] // WIDE)
    mixer = pad_cols(mixer, heads * WIDE).reshape(rows, heads, WIDE)
    cuts = w_gate.shape[1] // FF_CUT
    ffn = jnp.concatenate(
        [mat.reshape(rows, cuts, FF_CUT) for mat in (w_gate, w_up, down_t)], axis=2
    )
    return jnp.swapaxes(jnp.concatenate([mixer, ffn], axis=1), 0, 1)


def unpack(chunks, sizes):
    rows = chunks.shape[1]
    devs = rows // ROWS
    key_wide, val_wide, rank, forget_rows, head_rows, model = sizes
    heads = -(-(MISC + 2 * key_wide + 2 * val_wide + model) // WIDE)
    flat = jnp.swapaxes(chunks[:heads], 0, 1).reshape(rows, heads * WIDE)
    at = MISC
    mats = []
    for wide in (key_wide, key_wide, val_wide, val_wide, model):
        mats.append(flat[:, at : at + wide])
        at += wide

    def gathered(lo, hi, keep):
        return flat[:, lo:hi].reshape(devs, ROWS, hi - lo)[:, :keep].reshape(devs * keep, hi - lo)

    ffn = chunks[heads:]
    ffn = [
        jnp.swapaxes(ffn[:, :, i * FF_CUT : (i + 1) * FF_CUT], 0, 1).reshape(rows, -1)
        for i in range(3)
    ]
    return (
        flat[:, rank],
        mats[0],
        mats[1],
        mats[2],
        mats[3],
        flat[:, :rank],
        gathered(32, 32 + rank, forget_rows),
        gathered(48, 49, forget_rows)[:, 0],
        gathered(18, 19, head_rows)[:, 0],
        mats[4],
        flat[:, rank + 1],
        ffn[0],
        ffn[1],
        ffn[2],
    )


def plain_shards(
    inputs,
    cotangent,
    lengths,
    dealing,
    g_attn,
    w_query,
    w_key,
    w_value,
    w_outgate,
    w_lowrank,
    w_forget,
    b_forget,
    g_head,
    w_output,
    g_ffn,
    w_gate,
    w_up,
    w_down,
):
    axes = ("grp", "shard")
    shard_count = lax.axis_size("shard")
    self_index = lax.axis_index("grp") * shard_count + lax.axis_index("shard")
    seq_dev, max_len, _ = inputs.shape
    own_given = self_index * seq_dev + jnp.arange(seq_dev, dtype=jnp.int32)
    own_len = jnp.sum(jnp.where(dealing[None, :] == own_given[:, None], lengths[None, :], 0), axis=1)
    live = jnp.arange(max_len, dtype=jnp.int32)[None, :] < own_len[:, None]
    zero_low = jnp.zeros((), jnp.bfloat16)
    rows_in = jnp.where(live[..., None], inputs, zero_low).reshape(seq_dev * max_len, D)
    back_in = jnp.where(live[..., None], cotangent, zero_low).reshape(seq_dev * max_len, D)
    shard_weights = (
        g_attn,
        w_query,
        w_key,
        w_value,
        w_outgate,
        w_lowrank,
        w_forget,
        b_forget,
        g_head,
        w_output,
        g_ffn,
        w_gate,
        w_up,
        w_down,
    )
    grad_dims = (0, 0, 0, 0, 0, 0, 1, 0, 0, 0, 0, 0, 0, 1)
    gathered = tuple(
        lax.all_gather(weight, axes, axis=dim, tiled=True)
        for weight, dim in zip(shard_weights, grad_dims)
    )
    out_rows, grad_rows, grads = layer_pass(gathered, rows_in, back_in, seq_dev)
    reduced = tuple(
        lax.psum_scatter(
            grad.astype(jnp.bfloat16), axes, scatter_dimension=dim, tiled=True
        ).astype(jnp.float32)
        for grad, dim in zip(grads, grad_dims)
    )
    return (out_rows.reshape(inputs.shape), grad_rows.reshape(inputs.shape)) + reduced


def kernel_shards(
    inputs,
    cotangent,
    lengths,
    dealing,
    g_attn,
    w_query,
    w_key,
    w_value,
    w_outgate,
    w_lowrank,
    w_forget,
    b_forget,
    g_head,
    w_output,
    g_ffn,
    w_gate,
    w_up,
    w_down,
):
    self_index = lax.axis_index("grp") * SHARD + lax.axis_index("shard")
    seq_dev, max_len, _ = inputs.shape
    own_given = self_index * seq_dev + jnp.arange(seq_dev, dtype=jnp.int32)
    own_len = jnp.sum(jnp.where(dealing[None, :] == own_given[:, None], lengths[None, :], 0), axis=1)
    live = jnp.arange(max_len, dtype=jnp.int32)[None, :] < own_len[:, None]
    zero_low = jnp.zeros((), jnp.bfloat16)
    rows_in = jnp.where(live[..., None], inputs, zero_low).reshape(seq_dev * max_len, D)
    back_in = jnp.where(live[..., None], cotangent, zero_low).reshape(seq_dev * max_len, D)
    shard_weights = (
        g_attn,
        w_query,
        w_key,
        w_value,
        w_outgate,
        w_lowrank,
        w_forget.T,
        b_forget,
        g_head,
        w_output,
        g_ffn,
        w_gate,
        w_up,
        w_down.T,
    )
    sizes = (
        w_query.shape[1],
        w_value.shape[1],
        w_lowrank.shape[1],
        b_forget.shape[0],
        g_head.shape[0],
        D,
    )
    full = gather_call(pack(shard_weights, ROWS))
    full = full.reshape(full.shape[0], GRP * SHARD * ROWS, WIDE)
    weights = list(unpack(full, sizes))
    weights[6] = weights[6].T
    weights[13] = weights[13].T
    out_rows, grad_rows, grads = layer_pass(weights, rows_in, back_in, seq_dev)
    grads = [grad.astype(jnp.bfloat16) for grad in grads]
    grads[6] = grads[6].T
    grads[13] = grads[13].T
    packed = pack(grads, GRP * SHARD * ROWS)
    reduced = list(unpack(reduce_call(packed.reshape(packed.shape[0], GRP, SHARD, ROWS, WIDE)), sizes))
    reduced[6] = reduced[6].T
    reduced[13] = reduced[13].T
    return (out_rows.reshape(inputs.shape), grad_rows.reshape(inputs.shape)) + tuple(reduced)


def solution(mesh):
    small = mesh.shape["grp"] == GRP and mesh.shape["shard"] == SHARD
    return jax.shard_map(
        kernel_shards if small else plain_shards,
        mesh=mesh,
        in_specs=(
            P(("grp", "shard"), None, None),
            P(("grp", "shard"), None, None),
            P(),
            P(),
            P(("grp", "shard")),
            P(("grp", "shard"), None),
            P(("grp", "shard"), None),
            P(("grp", "shard"), None),
            P(("grp", "shard"), None),
            P(("grp", "shard"), None),
            P(None, ("grp", "shard")),
            P(("grp", "shard")),
            P(("grp", "shard")),
            P(("grp", "shard"), None),
            P(("grp", "shard")),
            P(("grp", "shard"), None),
            P(("grp", "shard"), None),
            P(None, ("grp", "shard")),
        ),
        out_specs=(
            P(("grp", "shard"), None, None),
            P(("grp", "shard"), None, None),
            P(("grp", "shard")),
            P(("grp", "shard"), None),
            P(("grp", "shard"), None),
            P(("grp", "shard"), None),
            P(("grp", "shard"), None),
            P(("grp", "shard"), None),
            P(None, ("grp", "shard")),
            P(("grp", "shard")),
            P(("grp", "shard")),
            P(("grp", "shard"), None),
            P(("grp", "shard")),
            P(("grp", "shard"), None),
            P(("grp", "shard"), None),
            P(None, ("grp", "shard")),
        ),
        check_vma=False,
    )
```

```python
import jax
import jax.numpy as jnp
from jax import lax
from jax.experimental import pallas as pl
from jax.experimental.pallas import tpu as pltpu
from jax.sharding import PartitionSpec as P

D = 1024
HEADS = 4
BLOCK = 64


EPS = 1e-05
HEAD_EPS = 1.0

MESH = pl.DeviceIdType.MESH
DMA = pltpu.SemaphoreType.DMA
GRP = 4
SHARD = 8
ROWS = 32
WIDE = 768
FF_CUT = 256
SLOTS = 4
MISC = 128
DEVICES = 32
RANK = 16
KEY_WIDE = 512
VAL_WIDE = 1024
HEAD_KEY = 128
HEAD_VAL = 256
SCALE = 128 ** (-0.5)
SEQS = 4
SEQ = 192
BLOCKS = 3
LIVE = SEQS * SEQ
Q_AT = MISC
K_AT = Q_AT + KEY_WIDE
V_AT = K_AT + KEY_WIDE
G_AT = V_AT + VAL_WIDE
O_AT = G_AT + VAL_WIDE
PROJ = O_AT
GATE_AT = V_AT
MIX_CHUNKS = 6
FF_CHUNKS = 11
CHUNKS = MIX_CHUNKS + FF_CHUNKS
LAST_WIDE = O_AT + D - (MIX_CHUNKS - 1) * WIDE
AHEAD = 3
RED_FROM = 7
VMEM_LIMIT = 63 << 20
HALVES = (slice(0, LIVE // 2), slice(LIVE // 2, LIVE))


def matmul(left_mat, right_mat):
    return jnp.dot(left_mat, right_mat, preferred_element_type=jnp.float32)


def rows_contract(left_mat, right_mat):
    return lax.dot_general(
        left_mat, right_mat, (((0,), (0,)), ((), ())), preferred_element_type=jnp.float32
    )


def right_transpose(left_mat, right_mat):
    return lax.dot_general(
        left_mat, right_mat, (((1,), (1,)), ((), ())), preferred_element_type=jnp.float32
    )


def scaled_rows(rows_in, gain_vec):
    return rows_in * lax.rsqrt(jnp.mean(rows_in * rows_in, axis=-1, keepdims=True) + EPS) * gain_vec


def head_rows(rows_in, gain_vec):
    return (
        rows_in
        * lax.rsqrt(jnp.mean(rows_in * rows_in, axis=-1, keepdims=True) + HEAD_EPS)
        * gain_vec
    )


def forget_rate(logits):
    return jax.nn.log_sigmoid(logits) / 16.0


def swiglu_core(pre_gate, pre_up):
    return jax.nn.silu(pre_gate) * pre_up


def head_gate(mixed_out, gate_out, head_gain):
    normed = head_rows(mixed_out, head_gain)
    active = gate_out * jax.nn.sigmoid(gate_out)
    return normed.reshape(active.shape) * active


def block_gates(queries, key_rows, forget):
    running = jnp.cumsum(forget, axis=1)
    tail_sum = running[:, -1:]
    q_gate = queries * queries.shape[-1] ** (-0.5) * jnp.exp(running)
    k_back = key_rows * jnp.exp(-running)
    k_tail = key_rows * jnp.exp(tail_sum - running)
    return (q_gate, k_back, k_tail, jnp.exp(tail_sum[:, 0]))


def layer_pass(weights, rows_in, back_in, seq_count):
    (
        g_attn,
        w_query,
        w_key,
        w_value,
        w_outgate,
        w_lowrank,
        w_forget,
        b_forget,
        g_head,
        w_output,
        g_ffn,
        w_gate,
        w_up,
        w_down,
    ) = weights
    row_count = rows_in.shape[0]
    blocks = row_count // BLOCK
    key_dim = w_query.shape[1] // HEADS
    val_dim = w_value.shape[1] // HEADS
    key_shape = (blocks, BLOCK, HEADS, key_dim)
    val_shape = (blocks, BLOCK, HEADS, val_dim)
    flat_rows = rows_in.astype(jnp.float32)
    norm_one, pull_one = jax.vjp(scaled_rows, flat_rows, g_attn.astype(jnp.float32))
    xn_one = norm_one.astype(jnp.bfloat16)
    queries = matmul(xn_one, w_query)
    key_rows = matmul(xn_one, w_key)
    values = matmul(xn_one, w_value).astype(jnp.bfloat16)
    gate_out = matmul(xn_one, w_outgate)
    lowrank = matmul(xn_one, w_lowrank).astype(jnp.bfloat16)
    logits = matmul(lowrank, w_forget) + b_forget.astype(jnp.float32)
    forget, pull_forget = jax.vjp(forget_rate, logits)
    gate_vals, pull_gates = jax.vjp(
        block_gates,
        queries.reshape(key_shape),
        key_rows.reshape(key_shape),
        forget.reshape(key_shape),
    )
    q_gate = gate_vals[0].astype(jnp.bfloat16)
    k_back = gate_vals[1].astype(jnp.bfloat16)
    k_tail = gate_vals[2].astype(jnp.bfloat16)
    decays = gate_vals[3]
    val_blocks = values.reshape(val_shape)
    spot_ids = jnp.arange(BLOCK)
    causal = (spot_ids[:, None] >= spot_ids[None, :]).astype(jnp.float32)
    scores = jnp.einsum("cthd,cshd->chts", q_gate, k_back, preferred_element_type=jnp.float32)
    attn_probs = (scores * causal).astype(jnp.bfloat16)
    intra_out = jnp.einsum(
        "chts,cshe->cthe", attn_probs, val_blocks, preferred_element_type=jnp.float32
    )
    update = jnp.einsum("cthd,cthe->chde", k_tail, val_blocks, preferred_element_type=jnp.float32)

    per_seq = blocks // seq_count
    seq_blocks = (seq_count, per_seq) + update.shape[1:]
    upd_seq = update.reshape(seq_blocks)
    decay_seq = decays.reshape((seq_count, per_seq) + decays.shape[1:])
    carried = jnp.zeros_like(upd_seq[:, 0])
    before_list = []
    for idx in range(per_seq):
        before_list.append(carried)
        carried = decay_seq[:, idx][..., None] * carried + upd_seq[:, idx]
    before_seq = jnp.stack(before_list, axis=1)
    before_low = before_seq.reshape(update.shape).astype(jnp.bfloat16)
    inter_out = jnp.einsum(
        "cthd,chde->cthe", q_gate, before_low, preferred_element_type=jnp.float32
    )
    mixed_out = (intra_out + inter_out).reshape(row_count, HEADS, val_dim)
    gated_f, pull_head = jax.vjp(head_gate, mixed_out, gate_out, g_head.astype(jnp.float32))
    gated_out = gated_f.astype(jnp.bfloat16)
    resid_one = flat_rows + matmul(gated_out, w_output)
    norm_two, pull_two = jax.vjp(scaled_rows, resid_one, g_ffn.astype(jnp.float32))
    xn_two = norm_two.astype(jnp.bfloat16)
    pre_gate = matmul(xn_two, w_gate)
    pre_up = matmul(xn_two, w_up)
    hidden_f, pull_ffn = jax.vjp(swiglu_core, pre_gate, pre_up)
    hidden = hidden_f.astype(jnp.bfloat16)
    output = (resid_one + matmul(hidden, w_down)).astype(jnp.bfloat16)
    back_f = back_in.astype(jnp.float32)
    dw_down = rows_contract(hidden, back_in)
    d_hidden = right_transpose(back_in, w_down)
    d_pre_gate, d_pre_up = pull_ffn(d_hidden)
    d_gate_low = d_pre_gate.astype(jnp.bfloat16)
    d_up_low = d_pre_up.astype(jnp.bfloat16)
    dw_gate = rows_contract(xn_two, d_gate_low)
    dw_up = rows_contract(xn_two, d_up_low)
    d_norm_two = right_transpose(d_gate_low, w_gate) + right_transpose(d_up_low, w_up)
    d_resid_part, dg_ffn = pull_two(d_norm_two)
    d_resid = back_f + d_resid_part
    d_attn = d_resid.astype(jnp.bfloat16)
    dw_output = rows_contract(gated_out, d_attn)
    d_gated = right_transpose(d_attn, w_output)
    d_mixed_f, d_gate_out_f, dg_head = pull_head(d_gated)
    d_mixed = d_mixed_f.astype(jnp.bfloat16).reshape(val_shape)
    d_scores = jnp.einsum(
        "cthe,cshe->chts", d_mixed, val_blocks, preferred_element_type=jnp.float32
    )
    d_probs = (d_scores * causal).astype(jnp.bfloat16)
    d_q_gate = jnp.einsum(
        "chts,cshd->cthd", d_probs, k_back, preferred_element_type=jnp.float32
    ) + jnp.einsum("cthe,chde->cthd", d_mixed, before_low, preferred_element_type=jnp.float32)
    d_k_back = jnp.einsum("chts,cthd->cshd", d_probs, q_gate, preferred_element_type=jnp.float32)
    d_val_intra = jnp.einsum(
        "chts,cthe->cshe", attn_probs, d_mixed, preferred_element_type=jnp.float32
    )
    d_before = jnp.einsum("cthd,cthe->chde", q_gate, d_mixed, preferred_element_type=jnp.float32)

    d_before_seq = d_before.reshape(seq_blocks)
    d_after = jnp.zeros_like(upd_seq[:, 0])
    d_update_list = []
    d_decay_list = []
    for idx in reversed(range(per_seq)):
        d_update_list.append(d_after)
        d_decay_list.append(jnp.sum(d_after * before_seq[:, idx], axis=-1))
        d_after = d_before_seq[:, idx] + decay_seq[:, idx][..., None] * d_after
    d_update = jnp.stack(d_update_list[::-1], axis=1).reshape(update.shape)
    d_decays = jnp.stack(d_decay_list[::-1], axis=1).reshape(decays.shape)
    d_update_low = d_update.astype(jnp.bfloat16)
    d_k_tail = jnp.einsum(
        "cthe,chde->cthd", val_blocks, d_update_low, preferred_element_type=jnp.float32
    )
    d_values = (
        (
            d_val_intra
            + jnp.einsum(
                "cthd,chde->cthe", k_tail, d_update_low, preferred_element_type=jnp.float32
            )
        )
        .reshape(row_count, -1)
        .astype(jnp.bfloat16)
    )
    d_query_f, d_key_f, d_forget = pull_gates((d_q_gate, d_k_back, d_k_tail, d_decays))
    d_queries = d_query_f.reshape(row_count, -1).astype(jnp.bfloat16)
    d_keys = d_key_f.reshape(row_count, -1).astype(jnp.bfloat16)
    (d_logits,) = pull_forget(d_forget.reshape(row_count, -1))
    db_forget = jnp.sum(d_logits, axis=0)
    d_logit_low = d_logits.astype(jnp.bfloat16)
    dw_forget = rows_contract(lowrank, d_logit_low)
    d_lowrank = right_transpose(d_logit_low, w_forget).astype(jnp.bfloat16)
    d_gate_out = d_gate_out_f.astype(jnp.bfloat16)
    dw_query = rows_contract(xn_one, d_queries)
    dw_key = rows_contract(xn_one, d_keys)
    dw_value = rows_contract(xn_one, d_values)
    dw_outgate = rows_contract(xn_one, d_gate_out)
    dw_lowrank = rows_contract(xn_one, d_lowrank)
    d_norm_one = (
        right_transpose(d_queries, w_query)
        + right_transpose(d_keys, w_key)
        + right_transpose(d_values, w_value)
        + right_transpose(d_gate_out, w_outgate)
        + right_transpose(d_lowrank, w_lowrank)
    )
    d_flat, dg_attn = pull_one(d_norm_one)
    grad_rows = (d_resid + d_flat).astype(jnp.bfloat16)
    grads = (
        dg_attn,
        dw_query,
        dw_key,
        dw_value,
        dw_outgate,
        dw_lowrank,
        dw_forget,
        db_forget,
        dg_head,
        dw_output,
        dg_ffn,
        dw_gate,
        dw_up,
        dw_down,
    )
    return (output, grad_rows, grads)


def when(cond, do):
    if isinstance(cond, bool):
        if cond:
            do()
    else:
        pl.when(cond)(do)


def columns(ref, lo, hi):
    return ref[:, :, :, lo:hi].reshape(D, hi - lo)


def put_columns(ref, lo, hi, value):
    ref[:, :, :, lo:hi] = value.reshape(GRP, SHARD, ROWS, hi - lo)


def flip(index, bit):
    return index + bit - 2 * bit * lax.rem(index // bit, 2)


def remote(src, dst, send_sem, recv_sem, device):
    return pltpu.make_async_remote_copy(
        src_ref=src,
        dst_ref=dst,
        send_sem=send_sem,
        recv_sem=recv_sem,
        device_id=device,
        device_id_type=MESH,
    )


def start_all(copies):
    for copy in copies:
        copy.start()


def recv_all(copies):
    for copy in copies:
        copy.wait_recv()


def sent_all(copies):
    for copy in copies:
        copy.wait_send()


class Place:
    def __init__(self):
        self.z = lax.axis_index("grp")
        self.s = lax.axis_index("shard")
        self.sib = flip(self.s, 1)
        self.xn = flip(self.s, 2)
        self.yn = flip(self.s, 4)
        self.dg = flip(self.xn, 4)
        self.sets = [self.s, self.xn, self.yn, self.dg]
        self.z_peers = [lax.rem(self.z + step, GRP) for step in range(1, GRP)]
        self.z_from = [lax.rem(self.z + GRP - step, GRP) for step in range(1, GRP)]

    def greet(self):
        barrier = pltpu.get_barrier_semaphore()
        peers = [(peer, self.s) for peer in self.z_peers]
        peers += [(self.z, self.sib), (self.z, self.xn), (self.z, self.yn)]
        for peer in peers:
            pl.semaphore_signal(barrier, inc=1, device_id=peer, device_id_type=MESH)
        return (barrier, len(peers))


class Gather:
    def __init__(self, place, src, full, sems):
        self.p = place
        self.src = src
        self.full = full
        (
            self.ls,
            self.zs,
            self.zr,
            self.xs,
            self.xr,
            self.ds,
            self.dr,
            self.ss,
            self.sr,
        ) = sems

    def local(self, c):
        p = self.p
        return pltpu.make_async_copy(
            self.src.at[c, :, self.cols(c)], self.full.at[c, p.z, p.s, :, self.cols(c)], self.ls.at[c]
        )

    def line(self, c):
        p = self.p
        return [
            remote(
                self.src.at[c, :, self.cols(c)],
                self.full.at[c, p.z, p.s, :, self.cols(c)],
                self.zs.at[c, k],
                self.zr.at[c, k],
                (p.z_peers[k], p.s),
            )
            for k in range(GRP - 1)
        ]

    def line_in(self, c):
        p = self.p
        return [
            remote(
                self.src.at[c, :, self.cols(c)],
                self.full.at[c, p.z_from[k], p.s, :, self.cols(c)],
                self.zs.at[c, k],
                self.zr.at[c, k],
                (p.z_peers[k], p.s),
            )
            for k in range(GRP - 1)
        ]

    def cols(self, c):
        narrow = isinstance(c, int) and c == MIX_CHUNKS - 1
        return pl.ds(0, LAST_WIDE if narrow else WIDE)

    def moved(self, c, set_id, part, send, recv, k, device):
        view = self.full.at[c, part, set_id, :, self.cols(c)]
        return remote(view, view, send.at[c, k], recv.at[c, k], device)

    def plane(self, c):
        p = self.p
        whole = pl.ds(0, GRP)
        return [
            self.moved(c, p.s, whole, self.xs, self.xr, 0, (p.z, p.xn)),
            self.moved(c, p.s, whole, self.xs, self.xr, 1, (p.z, p.yn)),
        ]

    def plane_in(self, c):
        p = self.p
        whole = pl.ds(0, GRP)
        return [
            self.moved(c, p.xn, whole, self.xs, self.xr, 0, (p.z, p.xn)),
            self.moved(c, p.yn, whole, self.xs, self.xr, 1, (p.z, p.yn)),
        ]

    def corner(self, c):
        p = self.p
        low, high = pl.ds(0, 2), pl.ds(2, 2)
        return [
            self.moved(c, p.xn, low, self.ds, self.dr, 0, (p.z, p.yn)),
            self.moved(c, p.yn, high, self.ds, self.dr, 1, (p.z, p.xn)),
        ]

    def corner_in(self, c):
        p = self.p
        low, high = pl.ds(0, 2), pl.ds(2, 2)
        return [
            self.moved(c, p.dg, low, self.ds, self.dr, 0, (p.z, p.yn)),
            self.moved(c, p.dg, high, self.ds, self.dr, 1, (p.z, p.xn)),
        ]

    def other(self, c, k):
        p = self.p
        return self.moved(c, p.sets[k], pl.ds(0, GRP), self.ss, self.sr, k, (p.z, p.sib))

    def other_in(self, c):
        p = self.p
        return [
            self.moved(c, flip(p.sets[k], 1), pl.ds(0, GRP), self.ss, self.sr, k, (p.z, p.sib))
            for k in range(4)
        ]

    def line_stage(self, c):
        self.local(c).wait()
        recv_all(self.line_in(c))
        start_all(self.plane(c))
        self.other(c, 0).start()

    def plane_stage(self, c):
        recv_all(self.plane_in(c))
        start_all(self.corner(c))
        self.other(c, 1).start()
        self.other(c, 2).start()

    def corner_stage(self, c):
        recv_all(self.corner_in(c))
        self.other(c, 3).start()

    def step(self, t):
        def some(c, do):
            if isinstance(c, int):
                when(0 <= c < CHUNKS, lambda: do(c))
            else:
                when(c < CHUNKS, lambda: do(c))

        some(t + AHEAD, lambda c: start_all(self.line(c)))
        some(t, self.line_stage)
        some(t - 1, self.plane_stage)
        some(t - 2, self.corner_stage)
        some(t - 3, lambda c: recv_all(self.other_in(c)))

    def drain(self, c):
        sent_all(self.line(c) + self.plane(c) + self.corner(c))
        sent_all([self.other(c, k) for k in range(4)])


class Reduce:
    def __init__(self, place, src, out, bufs, sems):
        self.p = place
        self.src = src
        self.out = out
        self.own, self.b1, self.b2, self.b3, self.b4, self.stage = bufs
        (
            self.ls,
            self.s1,
            self.r1,
            self.s2,
            self.r2,
            self.s3,
            self.r3,
            self.s4,
            self.r4,
            self.out_sem,
        ) = sems

    def slot(self, c):
        return c % SLOTS if isinstance(c, int) else lax.rem(c, SLOTS)

    def wide(self, c):
        return LAST_WIDE if isinstance(c, int) and c == CHUNKS - 1 else WIDE

    def local(self, c):
        p, k = self.p, self.slot(c)
        n = pl.ds(0, self.wide(c))
        return [
            pltpu.make_async_copy(
                self.src.at[c, :, p.sets[j], :, n],
                self.own.at[k, j, :, :, n],
                self.ls.at[k, j],
            )
            for j in range(4)
        ]

    def other(self, c):
        p, k = self.p, self.slot(c)
        n = pl.ds(0, self.wide(c))
        return [
            remote(
                self.src.at[c, :, flip(p.sets[j], 1), :, n],
                self.b1.at[k, j, :, :, n],
                self.s1.at[k, j],
                self.r1.at[k, j],
                (p.z, p.sib),
            )
            for j in range(4)
        ]

    def corner(self, c):
        p, k = self.p, self.slot(c)
        n = pl.ds(0, self.wide(c))
        peers = [(p.z, p.xn), (p.z, p.yn)]
        return [
            remote(
                self.own.at[k, 3, pl.ds(2 * i, 2), :, n],
                self.b2.at[k, i, :, :, n],
                self.s2.at[k, i],
                self.r2.at[k, i],
                peers[i],
            )
            for i in range(2)
        ]

    def plane(self, c):
        p, k = self.p, self.slot(c)
        n = pl.ds(0, self.wide(c))
        peers = [(p.z, p.xn), (p.z, p.yn)]
        return [
            remote(
                self.own.at[k, 1 + i, :, :, n],
                self.b3.at[k, i, :, :, n],
                self.s3.at[k, i],
                self.r3.at[k, i],
                peers[i],
            )
            for i in range(2)
        ]

    def line(self, c):
        p, k = self.p, self.slot(c)
        n = pl.ds(0, self.wide(c))
        return [
            remote(
                self.own.at[k, 0, p.z_peers[i], :, n],
                self.b4.at[k, i, :, n],
                self.s4.at[k, i],
                self.r4.at[k, i],
                (p.z_peers[i], p.s),
            )
            for i in range(GRP - 1)
        ]

    def drain(self, c):
        sent_all(self.other(c) + self.corner(c) + self.plane(c) + self.line(c))

    def enter(self, c):
        when(c >= SLOTS, lambda: self.drain(c - SLOTS))
        start_all(self.local(c))
        start_all(self.other(c))

    def add_other(self, c):
        k, n = self.slot(c), slice(0, self.wide(c))
        for copy in self.local(c):
            copy.wait()
        recv_all(self.other(c))
        for j in (3, 2, 1, 0):
            total = wide_type(self.own[k, j, :, :, n]) + wide_type(self.b1[k, j, :, :, n])
            self.own[k, j, :, :, n] = low_type(total)
            if j == 3:
                start_all(self.corner(c))

    def add_corner(self, c):
        k, n = self.slot(c), slice(0, self.wide(c))
        recv_all(self.corner(c))
        for j, lo, i in ((2, 0, 0), (1, 2, 1)):
            cut = slice(lo, lo + 2)
            total = wide_type(self.own[k, j, cut, :, n]) + wide_type(self.b2[k, i, :, :, n])
            self.own[k, j, cut, :, n] = low_type(total)
        start_all(self.plane(c))

    def add_plane(self, c):
        k, n = self.slot(c), slice(0, self.wide(c))
        recv_all(self.plane(c))
        total = wide_type(self.own[k, 0, :, :, n])
        total += wide_type(self.b3[k, 0, :, :, n])
        total += wide_type(self.b3[k, 1, :, :, n])
        self.own[k, 0, :, :, n] = low_type(total)
        start_all(self.line(c))

    def finish(self, c):
        k, n = self.slot(c), slice(0, self.wide(c))
        recv_all(self.line(c))
        total = wide_type(self.own[k, 0, self.p.z, :, n])
        for i in range(GRP - 1):
            total += wide_type(self.b4[k, i, :, n])
        when(c >= SLOTS, lambda: self.leave(c - SLOTS).wait())
        self.stage[k, :, n] = total
        self.leave(c).start()

    def leave(self, c):
        k, n = self.slot(c), pl.ds(0, self.wide(c))
        return pltpu.make_async_copy(
            self.stage.at[k, :, n], self.out.at[c, :, n], self.out_sem.at[k]
        )

    def step(self, t):
        def some(c, do):
            if isinstance(c, int):
                when(0 <= c < CHUNKS, lambda: do(c))
            else:
                when(c >= 0, lambda: do(c))

        some(t - 3, self.finish)
        some(t + 1, self.enter)
        some(t, self.add_other)
        some(t - 1, self.add_corner)
        some(t - 2, self.add_plane)


def reduce_scratch():
    def buf(*shape):
        return pltpu.VMEM((SLOTS,) + shape + (ROWS, WIDE), jnp.bfloat16)

    bufs = [buf(4, GRP), buf(4, GRP), buf(2, 2), buf(2, GRP), buf(GRP - 1)]
    counts = (4, 4, 4, 2, 2, 2, 2, 3, 3)
    bufs.append(pltpu.VMEM((SLOTS, ROWS, WIDE), jnp.float32))
    return bufs + [DMA((SLOTS, count)) for count in counts] + [DMA((SLOTS,))]


def mm_nn(left_mat, right_mat):
    return jnp.dot(left_mat, right_mat, preferred_element_type=jnp.float32)


def mm_nt(left_mat, right_mat):
    return right_transpose(left_mat, right_mat)


def mm_tn(left_mat, right_mat):
    return rows_contract(left_mat, right_mat)


def low_type(value):
    return value.astype(jnp.bfloat16)


def wide_type(value):
    return value.astype(jnp.float32)


def exact_sum(zero_one, value):
    high = low_type(value)
    rest = value - wide_type(high)
    mid = low_type(rest)
    last = low_type(rest - wide_type(mid))
    return mm_nn(zero_one, high) + mm_nn(zero_one, mid) + mm_nn(zero_one, last)


def iota(shape, dim):
    return lax.broadcasted_iota(jnp.int32, shape, dim)


def place_matrix(keep, columns):
    row = iota((D, columns), 0)
    col = iota((D, columns), 1)
    hit = (row // ROWS == col // keep) & (row % ROWS == col % keep)
    return low_type(jnp.where(hit, 1.0, 0.0))


def unit_matrix(size):
    return low_type(jnp.where(iota((size, size), 0) == iota((size, size), 1), 1.0, 0.0))


def row_rsqrt(value, eps):
    return lax.rsqrt(jnp.mean(value * value, axis=-1, keepdims=True) + eps)


class Layer:
    def __init__(self, refs):
        self.__dict__.update(refs)

    def rows(self, i):
        return pl.ds(pl.multiple_of(i * SEQ, SEQ), SEQ)

    def prepare(self):
        misc = columns(self.wm.at[0], 0, MISC)
        turned = mm_nt(unit_matrix(MISC), misc)
        self.gains[0:1, :] = turned[RANK : RANK + 1]
        self.gains[1:2, :] = turned[RANK + 1 : RANK + 2]
        picked = mm_tn(misc, place_matrix(KEY_WIDE // DEVICES, KEY_WIDE))
        self.wf[...] = jnp.zeros_like(self.wf)
        self.wf[0:RANK, :] = low_type(picked[32 : 32 + RANK])
        self.bias[0:1, :] = picked[48:49]
        heads = mm_tn(misc, place_matrix(HEAD_VAL // DEVICES, HEAD_VAL))
        self.ghead[0:1, :] = heads[18:19]
        for i in range(SEQS):
            r = pl.ds(i * SEQ, SEQ)
            value = wide_type(self.x[r, :])
            self.xn1[r, :] = low_type(value * row_rsqrt(value, EPS) * self.gains[0:1, :])

    def project(self, c):
        lo, hi = c * WIDE, min((c + 1) * WIDE, PROJ)
        for r in HALVES:
            value = mm_nn(self.xn1[r, :], columns(self.wm.at[c], 0, hi - lo))
            for ref, at, first, last in self.pieces(lo, hi):
                ref[r, at : at + last - first] = value[:, first:last].astype(ref.dtype)

    def pieces(self, lo, hi):
        found = []
        for ref, start, end, at in (
            (self.proj, 0, V_AT, 0),
            (self.pval, V_AT, G_AT, 0),
            (self.proj, G_AT, PROJ, GATE_AT),
        ):
            a, b = max(lo, start), min(hi, end)
            if a < b:
                found.append((ref, at + a - start, a - lo, b - lo))
        return found

    def gates(self, r):
        lane = iota((SEQ, MISC), 1)
        lowrank = low_type(jnp.where(lane < RANK, self.proj[r, 0:MISC], 0.0))
        logits = mm_nn(lowrank, self.wf[...]) + self.bias[0:1, :]
        forget = (jnp.minimum(logits, 0.0) - jnp.log1p(jnp.exp(-jnp.abs(logits)))) * (1.0 / 16.0)
        row, col = iota((SEQ, SEQ), 0), iota((SEQ, SEQ), 1)
        same = row // BLOCK == col // BLOCK
        causal = same & (col <= row)
        running = exact_sum(low_type(jnp.where(causal, 1.0, 0.0)), forget)
        tails = [running[b * BLOCK + BLOCK - 1 : (b + 1) * BLOCK] for b in range(BLOCKS)]
        tail = jnp.concatenate(
            [jnp.broadcast_to(one, (BLOCK, KEY_WIDE)) for one in tails], axis=0
        )
        return (lowrank, logits, running, tails, tail, same, causal)

    def attend(self, i):
        r = self.rows(i)
        _, _, running, tails, tail, _, causal = self.gates(r)
        grow = jnp.exp(running)
        fade = jnp.exp(-running)
        late = jnp.exp(tail - running)
        for h in range(HEADS):
            k = slice(h * HEAD_KEY, (h + 1) * HEAD_KEY)
            queries = self.proj[r, Q_AT + h * HEAD_KEY : Q_AT + (h + 1) * HEAD_KEY]
            key_rows = self.proj[r, K_AT + h * HEAD_KEY : K_AT + (h + 1) * HEAD_KEY]
            values = self.pval[r, h * HEAD_VAL : (h + 1) * HEAD_VAL]
            q_gate = low_type(queries * SCALE * grow[:, k])
            k_back = low_type(key_rows * fade[:, k])
            k_tail = low_type(key_rows * late[:, k])
            probs = low_type(jnp.where(causal, mm_nt(q_gate, k_back), 0.0))
            mixed = mm_nn(probs, values)
            state = mm_tn(values[0:BLOCK], k_tail[0:BLOCK])
            parts = [mixed[0:BLOCK]]
            for b in range(1, BLOCKS):
                cut = slice(b * BLOCK, (b + 1) * BLOCK)
                parts.append(mixed[cut] + mm_nt(q_gate[cut], low_type(state)))
                if b + 1 < BLOCKS:
                    state = state * jnp.exp(tails[b][:, k]) + mm_tn(values[cut], k_tail[cut])
            self.mixed[r, h * HEAD_VAL : (h + 1) * HEAD_VAL] = jnp.concatenate(parts, axis=0)

    def gate_rows(self, i):
        r = self.rows(i)
        for h in range(HEADS):
            v = slice(h * HEAD_VAL, (h + 1) * HEAD_VAL)
            mixed = self.mixed[r, v]
            gate = self.proj[r, GATE_AT + h * HEAD_VAL : GATE_AT + (h + 1) * HEAD_VAL]
            normed = mixed * row_rsqrt(mixed, HEAD_EPS) * self.ghead[0:1, :]
            self.gated[r, v] = low_type(normed * (gate * jax.nn.sigmoid(gate)))

    def mix_out(self):
        cut = WIDE - O_AT % WIDE
        first = O_AT // WIDE
        lo = O_AT % WIDE
        for i in range(SEQS):
            r = pl.ds(i * SEQ, SEQ)
            self.out_sum[r, 0:cut] = wide_type(self.x[r, 0:cut]) + mm_nn(
                self.gated[r, :], columns(self.wm.at[first], lo, WIDE)
            )
            self.out_sum[r, cut:D] = wide_type(self.x[r, cut:D]) + mm_nn(
                self.gated[r, :], columns(self.wl, 0, D - cut)
            )

    def second_norm(self):
        for i in range(SEQS):
            r = pl.ds(i * SEQ, SEQ)
            value = self.out_sum[r, :]
            self.xn2[r, :] = low_type(value * row_rsqrt(value, EPS) * self.gains[1:2, :])
        self.dx_sum[...] = jnp.zeros_like(self.dx_sum)
        self.turn(self.xn2, self.turn_a)
        self.turn(self.cot, self.turn_b)

    def turn(self, src, dst):
        for i in range(LIVE // 256):
            dst[:, i * 256 : (i + 1) * 256] = src[i * 256 : (i + 1) * 256, :].T

    def ffn(self, w_ref, g_ref):
        c = FF_CUT
        for r in HALVES:
            pre = mm_nn(self.xn2[r, :], columns(w_ref, 0, 2 * c))
            d_hidden = mm_nn(self.cot[r, :], columns(w_ref, 2 * c, 3 * c))
            pre_gate, pre_up = pre[:, 0:c], pre[:, c : 2 * c]
            sig = jax.nn.sigmoid(pre_gate)
            silu = pre_gate * sig
            self.hid[r, :] = low_type(silu * pre_up)
            self.dpre[r, 0:c] = low_type(d_hidden * pre_up * sig * (1.0 + pre_gate * (1.0 - sig)))
            self.dpre[r, c : 2 * c] = low_type(d_hidden * silu)
            self.out_sum[r, :] += mm_nt(self.hid[r, :], columns(w_ref, 2 * c, 3 * c))
            self.dx_sum[r, :] += mm_nt(self.dpre[r, :], columns(w_ref, 0, 2 * c))
        put_columns(g_ref, 0, 2 * c, low_type(mm_nn(self.turn_a[...], self.dpre[...])))
        put_columns(g_ref, 2 * c, 3 * c, low_type(mm_nn(self.turn_b[...], self.hid[...])))

    def norm_back(self, value, d_out, gain, eps):
        rs = row_rsqrt(value, eps)
        scaled = gain * d_out
        mean = jnp.mean(value * scaled, axis=-1, keepdims=True)
        d_gain = jnp.sum(d_out * value * rs, axis=0, keepdims=True)
        return (rs * scaled - value * (rs * rs * rs * mean), d_gain)

    def after_ffn(self):
        cut = WIDE - O_AT % WIDE
        first = O_AT // WIDE
        lo = O_AT % WIDE
        total = jnp.zeros((1, D), jnp.float32)
        for i in range(SEQS):
            r = pl.ds(i * SEQ, SEQ)
            resid = wide_type(self.x[r, :]) + jnp.concatenate(
                [
                    mm_nn(self.gated[r, :], columns(self.wm.at[first], lo, WIDE)),
                    mm_nn(self.gated[r, :], columns(self.wl, 0, D - cut)),
                ],
                axis=1,
            )
            d_val, d_gain = self.norm_back(
                resid, self.dx_sum[r, :], self.gains[1:2, :], EPS
            )
            total += d_gain
            d_resid = wide_type(self.cot[r, :]) + d_val
            self.dx_sum[r, :] = d_resid
            self.xn2[r, :] = low_type(d_resid)
        self.dgains[1:2, :] = total
        self.turn(self.gated, self.turn_a)
        self.turn(self.xn1, self.turn_b)
        self.gated[...] = low_type(self.out_sum[...])
        self.dwf[...] = jnp.zeros_like(self.dwf)
        self.dbias[...] = jnp.zeros_like(self.dbias)
        self.dghead[...] = jnp.zeros_like(self.dghead)

    def retreat(self, i):
        r = self.rows(i)
        cut = WIDE - O_AT % WIDE
        first = O_AT // WIDE
        lo = O_AT % WIDE
        d_attn = self.xn2[r, :]
        d_gated = mm_nt(d_attn[:, 0:cut], columns(self.wm.at[first], lo, WIDE))
        d_gated += mm_nt(d_attn[:, cut:D], columns(self.wl, 0, D - cut))
        lowrank, logits, running, tails, tail, same, causal = self.gates(r)
        grow = jnp.exp(running)
        fade = jnp.exp(-running)
        late = jnp.exp(tail - running)
        d_forget_parts = []
        tail_parts = []
        d_ghead = jnp.zeros((1, HEAD_VAL), jnp.float32)
        for h in range(HEADS):
            k = slice(h * HEAD_KEY, (h + 1) * HEAD_KEY)
            v = slice(h * HEAD_VAL, (h + 1) * HEAD_VAL)
            q_cols = slice(Q_AT + h * HEAD_KEY, Q_AT + (h + 1) * HEAD_KEY)
            k_cols = slice(K_AT + h * HEAD_KEY, K_AT + (h + 1) * HEAD_KEY)
            g_cols = slice(GATE_AT + h * HEAD_VAL, GATE_AT + (h + 1) * HEAD_VAL)
            mixed = self.mixed[r, v]
            gate = self.proj[r, g_cols]
            sig = jax.nn.sigmoid(gate)
            act = gate * sig
            rs = row_rsqrt(mixed, HEAD_EPS)
            unit = mixed * rs
            gain = self.ghead[0:1, :]
            d_out = d_gated[:, v]
            d_normed = d_out * act
            d_gate = d_out * (unit * gain) * sig * (1.0 + gate * (1.0 - sig))
            self.proj[r, g_cols] = wide_type(low_type(d_gate))
            d_ghead += jnp.sum(d_normed * unit, axis=0, keepdims=True)
            scaled = gain * d_normed
            mean = jnp.mean(mixed * scaled, axis=-1, keepdims=True)
            d_mixed = low_type(rs * scaled - mixed * (rs * rs * rs * mean))

            q_full = self.proj[r, q_cols] * SCALE * grow[:, k]
            key_rows = self.proj[r, k_cols]
            kb_full = key_rows * fade[:, k]
            kt_full = key_rows * late[:, k]
            values = self.pval[r, v]
            q_gate, k_back, k_tail = low_type(q_full), low_type(kb_full), low_type(kt_full)
            probs = low_type(jnp.where(causal, mm_nt(q_gate, k_back), 0.0))
            d_probs = low_type(jnp.where(causal, mm_nt(d_mixed, values), 0.0))
            d_q = mm_nn(d_probs, k_back)
            d_kb = mm_tn(d_probs, q_gate)
            d_v = mm_tn(probs, d_mixed)
            cuts = [slice(b * BLOCK, (b + 1) * BLOCK) for b in range(BLOCKS)]
            before = [None, mm_tn(values[cuts[0]], k_tail[cuts[0]])]
            decay = [jnp.exp(tails[b][:, k]) for b in range(BLOCKS)]
            for b in range(2, BLOCKS):
                before.append(
                    before[b - 1] * decay[b - 1] + mm_tn(values[cuts[b - 1]], k_tail[cuts[b - 1]])
                )
            after = [None] * BLOCKS
            for b in range(BLOCKS - 1, 0, -1):
                d_before = mm_tn(d_mixed[cuts[b]], q_gate[cuts[b]])
                after[b - 1] = d_before if after[b] is None else d_before + decay[b] * after[b]
            q_parts, t_parts, v_parts, e_parts = [], [], [], []
            for b in range(BLOCKS):
                cut_b = cuts[b]
                part = d_q[cut_b]
                if b > 0:
                    part = part + mm_nn(d_mixed[cut_b], low_type(before[b]))
                q_parts.append(part)
                if after[b] is None:
                    t_parts.append(jnp.zeros((BLOCK, HEAD_KEY), jnp.float32))
                    v_parts.append(d_v[cut_b])
                    e_parts.append(jnp.zeros((1, HEAD_KEY), jnp.float32))
                    continue
                after_low = low_type(after[b])
                d_kt = mm_nn(values[cut_b], after_low)
                t_parts.append(d_kt)
                v_parts.append(d_v[cut_b] + mm_nt(k_tail[cut_b], after_low))
                extra = jnp.sum(d_kt * kt_full[cut_b], axis=0, keepdims=True)
                if b > 0:
                    extra += jnp.sum(after[b] * before[b], axis=0, keepdims=True) * decay[b]
                e_parts.append(extra)
            d_q = jnp.concatenate(q_parts, axis=0)
            d_kt = jnp.concatenate(t_parts, axis=0)
            d_v = jnp.concatenate(v_parts, axis=0)
            self.pval[r, v] = low_type(d_v)
            self.proj[r, q_cols] = wide_type(low_type(d_q * SCALE * grow[:, k]))
            self.proj[r, k_cols] = wide_type(low_type(d_kb * fade[:, k] + d_kt * late[:, k]))
            d_forget_parts.append(d_q * q_full - d_kb * kb_full - d_kt * kt_full)
            tail_parts.append(
                jnp.concatenate(
                    [jnp.broadcast_to(one, (BLOCK, HEAD_KEY)) for one in e_parts], axis=0
                )
            )
        self.dghead[0:1, :] += d_ghead
        d_running = jnp.concatenate(d_forget_parts, axis=1)
        row, col = iota((SEQ, SEQ), 0), iota((SEQ, SEQ), 1)
        later = low_type(jnp.where(same & (col >= row), 1.0, 0.0))
        d_forget = exact_sum(later, d_running) + jnp.concatenate(tail_parts, axis=1)
        d_logits = d_forget * jax.nn.sigmoid(-logits) * (1.0 / 16.0)
        self.dbias[0:1, :] += jnp.sum(d_logits, axis=0, keepdims=True)
        d_logit_low = low_type(d_logits)
        self.dwf[...] += mm_tn(lowrank, d_logit_low)
        self.proj[r, 0:MISC] = wide_type(low_type(mm_nt(d_logit_low, self.wf[...])))

    def d_proj(self, c, rows=slice(None)):
        lo, hi = c * WIDE, min((c + 1) * WIDE, PROJ)
        parts = [
            low_type(ref[rows, at : at + last - first])
            for ref, at, first, last in self.pieces(lo, hi)
        ]
        return parts[0] if len(parts) == 1 else jnp.concatenate(parts, axis=1)

    def first_norm_back(self):
        for c in range(-(-PROJ // WIDE)):
            for r in HALVES:
                d_proj = self.d_proj(c, r)
                part = mm_nt(d_proj, columns(self.wm.at[c], 0, d_proj.shape[1]))
                self.out_sum[r, :] = part if c == 0 else self.out_sum[r, :] + part
        total = jnp.zeros((1, D), jnp.float32)
        for i in range(SEQS):
            r = pl.ds(i * SEQ, SEQ)
            d_val, d_gain = self.norm_back(
                wide_type(self.x[r, :]), self.out_sum[r, :], self.gains[0:1, :], EPS
            )
            total += d_gain
            self.xn1[r, :] = low_type(self.dx_sum[r, :] + d_val)
        self.dgains[0:1, :] = total

    def mixer_grad(self, c, g_ref):
        first = O_AT // WIDE
        lo = O_AT % WIDE
        cut = WIDE - lo
        if c == first + 1:
            put_columns(g_ref, 0, D - cut, low_type(mm_nn(self.turn_a[...], self.xn2[:, cut:D])))
            return
        d_proj = self.d_proj(c)
        grad = mm_nn(self.turn_b[...], d_proj)
        if c == first:
            put_columns(g_ref, lo, WIDE, low_type(mm_nn(self.turn_a[...], self.xn2[:, 0:cut])))
            put_columns(g_ref, 0, lo, low_type(grad))
            return
        if c > 0:
            put_columns(g_ref, 0, WIDE, low_type(grad))
            return
        zero = jnp.zeros
        gains = jnp.concatenate(
            [zero((RANK, D), jnp.float32), self.dgains[...], zero((MISC - RANK - 8, D), jnp.float32)],
            axis=0,
        )
        small = mm_tn(low_type(gains), unit_matrix(MISC))
        keyed = jnp.concatenate(
            [
                zero((32, KEY_WIDE), jnp.float32),
                self.dwf[0:RANK, :],
                self.dbias[...],
                zero((MISC - 56, KEY_WIDE), jnp.float32),
            ],
            axis=0,
        )
        small += mm_nt(place_matrix(KEY_WIDE // DEVICES, KEY_WIDE), low_type(keyed))
        lane = iota((MISC, HEAD_VAL), 0)
        headed = jnp.where(lane == 18, jnp.broadcast_to(self.dghead[0:1, :], (MISC, HEAD_VAL)), 0.0)
        small += mm_nt(place_matrix(HEAD_VAL // DEVICES, HEAD_VAL), low_type(headed))
        put_columns(g_ref, 0, MISC, low_type(grad[:, 0:MISC] + small))
        put_columns(g_ref, MISC, WIDE, low_type(grad[:, MISC:WIDE]))


LAYER_SCRATCH = (
    ("xn1", (LIVE, D), jnp.bfloat16),
    ("proj", (LIVE, GATE_AT + VAL_WIDE), jnp.float32),
    ("pval", (LIVE, VAL_WIDE), jnp.bfloat16),
    ("wm", (MIX_CHUNKS - 1, GRP, SHARD, ROWS, WIDE), jnp.bfloat16),
    ("wl", (GRP, SHARD, ROWS, LAST_WIDE), jnp.bfloat16),
    ("gains", (8, D), jnp.float32),
    ("wf", (MISC, KEY_WIDE), jnp.bfloat16),
    ("bias", (8, KEY_WIDE), jnp.float32),
    ("ghead", (8, HEAD_VAL), jnp.float32),
    ("mixed", (LIVE, D), jnp.float32),
    ("gated", (LIVE, D), jnp.bfloat16),
    ("xn2", (LIVE, D), jnp.bfloat16),
    ("out_sum", (LIVE, D), jnp.float32),
    ("dx_sum", (LIVE, D), jnp.float32),
    ("turn_a", (D, LIVE), jnp.bfloat16),
    ("turn_b", (D, LIVE), jnp.bfloat16),
    ("hid", (LIVE, FF_CUT), jnp.bfloat16),
    ("dpre", (LIVE, 2 * FF_CUT), jnp.bfloat16),
    ("dgains", (8, D), jnp.float32),
    ("dwf", (MISC, KEY_WIDE), jnp.float32),
    ("dbias", (8, KEY_WIDE), jnp.float32),
    ("dghead", (8, HEAD_VAL), jnp.float32),
    ("wb", (2, GRP, SHARD, ROWS, WIDE), jnp.bfloat16),
    ("gb", (2, GRP, SHARD, ROWS, WIDE), jnp.bfloat16),
)
SEM_COUNTS = (3, 3, 2, 2, 2, 2, 4, 4)


def layer_kernel(src, x, cot, out, grad, red, full, grads, *scratch):
    count = len(LAYER_SCRATCH)
    refs = {name: ref for (name, _, _), ref in zip(LAYER_SCRATCH, scratch[:count])}
    scratch = scratch[count:]
    g_sems, scratch = scratch[: 1 + len(SEM_COUNTS)], scratch[1 + len(SEM_COUNTS) :]
    load_sem, store_sem, out_sem = scratch[:3]
    bufs, r_sems = scratch[3:9], scratch[9:]

    place = Place()
    barrier, greeted = place.greet()
    gather = Gather(place, src, full, g_sems)
    red_op = Reduce(place, grads, red, bufs, r_sems)
    work = Layer(dict(refs, x=x, cot=cot))

    def load(c, ref, k):
        return pltpu.make_async_copy(full.at[c], ref, load_sem.at[k])

    def load_ffn(f):
        k = f % 2 if isinstance(f, int) else lax.rem(f, 2)
        return load(MIX_CHUNKS + f, work.wb.at[k], k)

    def load_mixer(c):
        if c == MIX_CHUNKS - 1:
            half = pl.ds(0, LAST_WIDE)
            return pltpu.make_async_copy(
                full.at[c, :, :, :, half], work.wl, load_sem.at[0]
            )
        return load(c, work.wm.at[c], 0)

    def store(o, k):
        if isinstance(o, int) and o == CHUNKS - 1:
            half = pl.ds(0, LAST_WIDE)
            return pltpu.make_async_copy(
                work.gb.at[k, :, :, :, half], grads.at[o, :, :, :, half], store_sem.at[k]
            )
        return pltpu.make_async_copy(work.gb.at[k], grads.at[o], store_sem.at[k])

    def fetch_mixer(c):
        copy = load_mixer(c)
        copy.start()
        copy.wait()

    start_all([gather.local(c) for c in range(CHUNKS)])
    work.dgains[...] = jnp.zeros_like(work.dgains)
    pl.semaphore_wait(barrier, greeted)
    for c in range(AHEAD):
        start_all(gather.line(c))
    for t in range(4):
        gather.step(t)
    fetch_mixer(0)
    work.prepare()
    work.project(0)
    for c in (1, 2, 3):
        gather.step(3 + c)
        fetch_mixer(c)
        work.project(c)
    work.attend(0)
    work.attend(1)
    gather.step(7)
    fetch_mixer(4)
    work.project(4)
    work.attend(2)
    work.attend(3)
    gather.step(8)
    fetch_mixer(5)
    for i in range(SEQS):
        work.gate_rows(i)
    work.mix_out()
    gather.step(9)
    load_ffn(0).start()
    work.second_norm()

    def ffn_step(f, reduce_too):
        k = lax.rem(f, 2)
        gather.step(10 + f)
        load_ffn(f).wait()
        when(f + 1 < FF_CHUNKS, lambda: load_ffn(f + 1).start())
        when(f >= 2, lambda: store(f - 2, k).wait())
        work.ffn(work.wb.at[k], work.gb.at[k])
        store(f, k).start()
        if reduce_too:
            red_op.step(f - RED_FROM)
        return 0

    def ffn_first(f, carry):
        return ffn_step(f, False)

    def ffn_last(f, carry):
        return ffn_step(f, True)

    lax.fori_loop(0, RED_FROM, ffn_first, 0)
    red_op.enter(0)
    lax.fori_loop(RED_FROM, FF_CHUNKS, ffn_last, 0)
    for f in (FF_CHUNKS - 2, FF_CHUNKS - 1):
        store(f, f % 2).wait()
    o = FF_CHUNKS - RED_FROM
    work.after_ffn()
    out_copy = pltpu.make_async_copy(work.gated, out, out_sem.at[0])
    out_copy.start()
    red_op.step(o)
    for i in range(SEQS):
        work.retreat(i)
        red_op.step(o + 1 + i)
    work.first_norm_back()
    grad_copy = pltpu.make_async_copy(work.xn1, grad, out_sem.at[1])
    grad_copy.start()
    o += 1 + SEQS
    order = [4, 3, 2, 1, 0, 5]
    for n, c in enumerate(order):
        work.mixer_grad(c, work.gb.at[n % 2])
        copy = store(FF_CHUNKS + n, n % 2)
        copy.start()
        copy.wait()
        while o + 1 < FF_CHUNKS + n + 1:
            red_op.step(o)
            o += 1
    while o < CHUNKS + 3:
        red_op.step(o)
        o += 1
    out_copy.wait()
    grad_copy.wait()
    for c in range(CHUNKS):
        gather.drain(c)
    for c in range(CHUNKS - SLOTS, CHUNKS):
        red_op.drain(c)
        red_op.leave(c).wait()


def layer_call(src, x, cot):
    any_spec = pl.BlockSpec(memory_space=pl.ANY)
    vmem = pl.BlockSpec(memory_space=pltpu.VMEM)
    chunk = (CHUNKS, GRP, SHARD, ROWS, WIDE)
    rows = jax.ShapeDtypeStruct((LIVE, D), jnp.bfloat16)
    scratch = [pltpu.VMEM(shape, kind) for _, shape, kind in LAYER_SCRATCH]
    scratch += [DMA((CHUNKS,))] + [DMA((CHUNKS, count)) for count in SEM_COUNTS]
    scratch += [DMA((2,)), DMA((2,)), DMA((2,))]
    scratch += reduce_scratch()
    result = pl.pallas_call(
        layer_kernel,
        out_shape=(
            rows,
            rows,
            jax.ShapeDtypeStruct((CHUNKS, ROWS, WIDE), jnp.float32),
            jax.ShapeDtypeStruct(chunk, jnp.bfloat16),
            jax.ShapeDtypeStruct(chunk, jnp.bfloat16),
        ),
        in_specs=[any_spec, vmem, vmem],
        out_specs=(any_spec,) * 5,
        scratch_shapes=scratch,
        compiler_params=pltpu.CompilerParams(
            collective_id=0, has_side_effects=True, vmem_limit_bytes=VMEM_LIMIT
        ),
    )(src, x, cot)
    return result[:3]


def pad_cols(mat, width):
    return jnp.pad(mat, ((0, 0), (0, width - mat.shape[1])))


def pad_rows(mat, rows):
    return jnp.pad(mat, ((0, rows - mat.shape[0]), (0, 0)))


def pack(parts, rows):
    (
        g_attn,
        w_query,
        w_key,
        w_value,
        w_outgate,
        w_lowrank,
        forget_t,
        b_forget,
        g_head,
        w_output,
        g_ffn,
        w_gate,
        w_up,
        down_t,
    ) = parts
    devs = rows // ROWS

    def spread(mat):
        cut = mat.reshape(devs, -1, mat.shape[1])
        return jnp.pad(cut, ((0, 0), (0, ROWS - cut.shape[1]), (0, 0))).reshape(rows, -1)

    misc = jnp.concatenate(
        [
            w_lowrank,
            g_attn[:, None],
            g_ffn[:, None],
            spread(g_head[:, None]),
            jnp.zeros((rows, 13), w_lowrank.dtype),
            spread(forget_t),
            spread(b_forget[:, None]),
        ],
        axis=1,
    )
    mixer = jnp.concatenate(
        [pad_cols(misc, MISC), w_query, w_key, w_value, w_outgate, w_output], axis=1
    )
    heads = -(-mixer.shape[1] // WIDE)
    mixer = pad_cols(mixer, heads * WIDE).reshape(rows, heads, WIDE)
    cuts = w_gate.shape[1] // FF_CUT
    ffn = jnp.concatenate(
        [mat.reshape(rows, cuts, FF_CUT) for mat in (w_gate, w_up, down_t)], axis=2
    )
    return jnp.swapaxes(jnp.concatenate([mixer, ffn], axis=1), 0, 1)


def unpack(chunks, sizes):
    rows = chunks.shape[1]
    devs = rows // ROWS
    key_wide, val_wide, rank, forget_rows, head_rows, model = sizes
    heads = -(-(MISC + 2 * key_wide + 2 * val_wide + model) // WIDE)
    flat = jnp.swapaxes(chunks[:heads], 0, 1).reshape(rows, heads * WIDE)
    at = MISC
    mats = []
    for wide in (key_wide, key_wide, val_wide, val_wide, model):
        mats.append(flat[:, at : at + wide])
        at += wide

    def gathered(lo, hi, keep):
        return flat[:, lo:hi].reshape(devs, ROWS, hi - lo)[:, :keep].reshape(devs * keep, hi - lo)

    ffn = chunks[heads:]
    ffn = [
        jnp.swapaxes(ffn[:, :, i * FF_CUT : (i + 1) * FF_CUT], 0, 1).reshape(rows, -1)
        for i in range(3)
    ]
    return (
        flat[:, rank],
        mats[0],
        mats[1],
        mats[2],
        mats[3],
        flat[:, :rank],
        gathered(32, 32 + rank, forget_rows),
        gathered(48, 49, forget_rows)[:, 0],
        gathered(18, 19, head_rows)[:, 0],
        mats[4],
        flat[:, rank + 1],
        ffn[0],
        ffn[1],
        ffn[2],
    )


def plain_shards(
    inputs,
    cotangent,
    lengths,
    dealing,
    g_attn,
    w_query,
    w_key,
    w_value,
    w_outgate,
    w_lowrank,
    w_forget,
    b_forget,
    g_head,
    w_output,
    g_ffn,
    w_gate,
    w_up,
    w_down,
):
    axes = ("grp", "shard")
    shard_count = lax.axis_size("shard")
    self_index = lax.axis_index("grp") * shard_count + lax.axis_index("shard")
    seq_dev, max_len, _ = inputs.shape
    own_given = self_index * seq_dev + jnp.arange(seq_dev, dtype=jnp.int32)
    own_len = jnp.sum(jnp.where(dealing[None, :] == own_given[:, None], lengths[None, :], 0), axis=1)
    live = jnp.arange(max_len, dtype=jnp.int32)[None, :] < own_len[:, None]
    zero_low = jnp.zeros((), jnp.bfloat16)
    rows_in = jnp.where(live[..., None], inputs, zero_low).reshape(seq_dev * max_len, D)
    back_in = jnp.where(live[..., None], cotangent, zero_low).reshape(seq_dev * max_len, D)
    shard_weights = (
        g_attn,
        w_query,
        w_key,
        w_value,
        w_outgate,
        w_lowrank,
        w_forget,
        b_forget,
        g_head,
        w_output,
        g_ffn,
        w_gate,
        w_up,
        w_down,
    )
    grad_dims = (0, 0, 0, 0, 0, 0, 1, 0, 0, 0, 0, 0, 0, 1)
    gathered = tuple(
        lax.all_gather(weight, axes, axis=dim, tiled=True)
        for weight, dim in zip(shard_weights, grad_dims)
    )
    out_rows, grad_rows, grads = layer_pass(gathered, rows_in, back_in, seq_dev)
    reduced = tuple(
        lax.psum_scatter(
            grad.astype(jnp.bfloat16), axes, scatter_dimension=dim, tiled=True
        ).astype(jnp.float32)
        for grad, dim in zip(grads, grad_dims)
    )
    return (out_rows.reshape(inputs.shape), grad_rows.reshape(inputs.shape)) + reduced


def kernel_shards(
    inputs,
    cotangent,
    lengths,
    dealing,
    g_attn,
    w_query,
    w_key,
    w_value,
    w_outgate,
    w_lowrank,
    w_forget,
    b_forget,
    g_head,
    w_output,
    g_ffn,
    w_gate,
    w_up,
    w_down,
):
    self_index = lax.axis_index("grp") * SHARD + lax.axis_index("shard")
    seq_dev, max_len, _ = inputs.shape
    own_given = self_index * seq_dev + jnp.arange(seq_dev, dtype=jnp.int32)
    own_len = jnp.sum(jnp.where(dealing[None, :] == own_given[:, None], lengths[None, :], 0), axis=1)
    live = jnp.arange(max_len, dtype=jnp.int32)[None, :] < own_len[:, None]
    zero_low = jnp.zeros((), jnp.bfloat16)
    rows_in = jnp.where(live[..., None], inputs, zero_low).reshape(seq_dev * max_len, D)
    back_in = jnp.where(live[..., None], cotangent, zero_low).reshape(seq_dev * max_len, D)
    shard_weights = (
        g_attn,
        w_query,
        w_key,
        w_value,
        w_outgate,
        w_lowrank,
        w_forget.T,
        b_forget,
        g_head,
        w_output,
        g_ffn,
        w_gate,
        w_up,
        w_down.T,
    )
    sizes = (
        w_query.shape[1],
        w_value.shape[1],
        w_lowrank.shape[1],
        b_forget.shape[0],
        g_head.shape[0],
        D,
    )
    out_rows, grad_rows, red = layer_call(pack(shard_weights, ROWS), rows_in, back_in)
    order = [15, 14, 13, 12, 11, 16] + list(range(FF_CHUNKS))
    reduced = list(unpack(jnp.stack([red[o] for o in order]), sizes))
    reduced[6] = reduced[6].T
    reduced[13] = reduced[13].T
    return (out_rows.reshape(inputs.shape), grad_rows.reshape(inputs.shape)) + tuple(reduced)


def solution(mesh):
    small = mesh.shape["grp"] == GRP and mesh.shape["shard"] == SHARD
    return jax.shard_map(
        kernel_shards if small else plain_shards,
        mesh=mesh,
        in_specs=(
            P(("grp", "shard"), None, None),
            P(("grp", "shard"), None, None),
            P(),
            P(),
            P(("grp", "shard")),
            P(("grp", "shard"), None),
            P(("grp", "shard"), None),
            P(("grp", "shard"), None),
            P(("grp", "shard"), None),
            P(("grp", "shard"), None),
            P(None, ("grp", "shard")),
            P(("grp", "shard")),
            P(("grp", "shard")),
            P(("grp", "shard"), None),
            P(("grp", "shard")),
            P(("grp", "shard"), None),
            P(("grp", "shard"), None),
            P(None, ("grp", "shard")),
        ),
        out_specs=(
            P(("grp", "shard"), None, None),
            P(("grp", "shard"), None, None),
            P(("grp", "shard")),
            P(("grp", "shard"), None),
            P(("grp", "shard"), None),
            P(("grp", "shard"), None),
            P(("grp", "shard"), None),
            P(("grp", "shard"), None),
            P(None, ("grp", "shard")),
            P(("grp", "shard")),
            P(("grp", "shard")),
            P(("grp", "shard"), None),
            P(("grp", "shard")),
            P(("grp", "shard"), None),
            P(("grp", "shard"), None),
            P(None, ("grp", "shard")),
        ),
        check_vma=False,
    )
```

```python
import jax
import jax.numpy as jnp
from jax import lax
from jax.experimental import pallas as pl
from jax.experimental.pallas import tpu as pltpu
from jax.sharding import PartitionSpec as P

D = 1024
HEADS = 4
BLOCK = 64


EPS = 1e-05
HEAD_EPS = 1.0

MESH = pl.DeviceIdType.MESH
DMA = pltpu.SemaphoreType.DMA
GRP = 4
SHARD = 8
ROWS = 32
WIDE = 768
FF_CUT = 256
SLOTS = 4
MISC = 128
DEVICES = 32
RANK = 16
KEY_WIDE = 512
VAL_WIDE = 1024
HEAD_KEY = 128
HEAD_VAL = 256
SCALE = 128 ** (-0.5)
SEQS = 4
SEQ = 192
BLOCKS = 3
LIVE = SEQS * SEQ
Q_AT = MISC
K_AT = Q_AT + KEY_WIDE
V_AT = K_AT + KEY_WIDE
G_AT = V_AT + VAL_WIDE
O_AT = G_AT + VAL_WIDE
PROJ = O_AT
GATE_AT = V_AT
MIX_CHUNKS = 6
FF_CHUNKS = 11
CHUNKS = MIX_CHUNKS + FF_CHUNKS
LAST_WIDE = O_AT + D - (MIX_CHUNKS - 1) * WIDE
AHEAD = 6
RED_FROM = 5
SQUARE = 4
CORES = 2
SPREAD = (15, 16)
LINES = 15
VMEM_LIMIT = 63 << 20
HALVES = (slice(0, LIVE // 2), slice(LIVE // 2, LIVE))


def matmul(left_mat, right_mat):
    return jnp.dot(left_mat, right_mat, preferred_element_type=jnp.float32)


def rows_contract(left_mat, right_mat):
    return lax.dot_general(
        left_mat, right_mat, (((0,), (0,)), ((), ())), preferred_element_type=jnp.float32
    )


def right_transpose(left_mat, right_mat):
    return lax.dot_general(
        left_mat, right_mat, (((1,), (1,)), ((), ())), preferred_element_type=jnp.float32
    )


def scaled_rows(rows_in, gain_vec):
    return rows_in * lax.rsqrt(jnp.mean(rows_in * rows_in, axis=-1, keepdims=True) + EPS) * gain_vec


def head_rows(rows_in, gain_vec):
    return (
        rows_in
        * lax.rsqrt(jnp.mean(rows_in * rows_in, axis=-1, keepdims=True) + HEAD_EPS)
        * gain_vec
    )


def forget_rate(logits):
    return jax.nn.log_sigmoid(logits) / 16.0


def swiglu_core(pre_gate, pre_up):
    return jax.nn.silu(pre_gate) * pre_up


def head_gate(mixed_out, gate_out, head_gain):
    normed = head_rows(mixed_out, head_gain)
    active = gate_out * jax.nn.sigmoid(gate_out)
    return normed.reshape(active.shape) * active


def block_gates(queries, key_rows, forget):
    running = jnp.cumsum(forget, axis=1)
    tail_sum = running[:, -1:]
    q_gate = queries * queries.shape[-1] ** (-0.5) * jnp.exp(running)
    k_back = key_rows * jnp.exp(-running)
    k_tail = key_rows * jnp.exp(tail_sum - running)
    return (q_gate, k_back, k_tail, jnp.exp(tail_sum[:, 0]))


def layer_pass(weights, rows_in, back_in, seq_count):
    (
        g_attn,
        w_query,
        w_key,
        w_value,
        w_outgate,
        w_lowrank,
        w_forget,
        b_forget,
        g_head,
        w_output,
        g_ffn,
        w_gate,
        w_up,
        w_down,
    ) = weights
    row_count = rows_in.shape[0]
    blocks = row_count // BLOCK
    key_dim = w_query.shape[1] // HEADS
    val_dim = w_value.shape[1] // HEADS
    key_shape = (blocks, BLOCK, HEADS, key_dim)
    val_shape = (blocks, BLOCK, HEADS, val_dim)
    flat_rows = rows_in.astype(jnp.float32)
    norm_one, pull_one = jax.vjp(scaled_rows, flat_rows, g_attn.astype(jnp.float32))
    xn_one = norm_one.astype(jnp.bfloat16)
    queries = matmul(xn_one, w_query)
    key_rows = matmul(xn_one, w_key)
    values = matmul(xn_one, w_value).astype(jnp.bfloat16)
    gate_out = matmul(xn_one, w_outgate)
    lowrank = matmul(xn_one, w_lowrank).astype(jnp.bfloat16)
    logits = matmul(lowrank, w_forget) + b_forget.astype(jnp.float32)
    forget, pull_forget = jax.vjp(forget_rate, logits)
    gate_vals, pull_gates = jax.vjp(
        block_gates,
        queries.reshape(key_shape),
        key_rows.reshape(key_shape),
        forget.reshape(key_shape),
    )
    q_gate = gate_vals[0].astype(jnp.bfloat16)
    k_back = gate_vals[1].astype(jnp.bfloat16)
    k_tail = gate_vals[2].astype(jnp.bfloat16)
    decays = gate_vals[3]
    val_blocks = values.reshape(val_shape)
    spot_ids = jnp.arange(BLOCK)
    causal = (spot_ids[:, None] >= spot_ids[None, :]).astype(jnp.float32)
    scores = jnp.einsum("cthd,cshd->chts", q_gate, k_back, preferred_element_type=jnp.float32)
    attn_probs = (scores * causal).astype(jnp.bfloat16)
    intra_out = jnp.einsum(
        "chts,cshe->cthe", attn_probs, val_blocks, preferred_element_type=jnp.float32
    )
    update = jnp.einsum("cthd,cthe->chde", k_tail, val_blocks, preferred_element_type=jnp.float32)

    per_seq = blocks // seq_count
    seq_blocks = (seq_count, per_seq) + update.shape[1:]
    upd_seq = update.reshape(seq_blocks)
    decay_seq = decays.reshape((seq_count, per_seq) + decays.shape[1:])
    carried = jnp.zeros_like(upd_seq[:, 0])
    before_list = []
    for idx in range(per_seq):
        before_list.append(carried)
        carried = decay_seq[:, idx][..., None] * carried + upd_seq[:, idx]
    before_seq = jnp.stack(before_list, axis=1)
    before_low = before_seq.reshape(update.shape).astype(jnp.bfloat16)
    inter_out = jnp.einsum(
        "cthd,chde->cthe", q_gate, before_low, preferred_element_type=jnp.float32
    )
    mixed_out = (intra_out + inter_out).reshape(row_count, HEADS, val_dim)
    gated_f, pull_head = jax.vjp(head_gate, mixed_out, gate_out, g_head.astype(jnp.float32))
    gated_out = gated_f.astype(jnp.bfloat16)
    resid_one = flat_rows + matmul(gated_out, w_output)
    norm_two, pull_two = jax.vjp(scaled_rows, resid_one, g_ffn.astype(jnp.float32))
    xn_two = norm_two.astype(jnp.bfloat16)
    pre_gate = matmul(xn_two, w_gate)
    pre_up = matmul(xn_two, w_up)
    hidden_f, pull_ffn = jax.vjp(swiglu_core, pre_gate, pre_up)
    hidden = hidden_f.astype(jnp.bfloat16)
    output = (resid_one + matmul(hidden, w_down)).astype(jnp.bfloat16)
    back_f = back_in.astype(jnp.float32)
    dw_down = rows_contract(hidden, back_in)
    d_hidden = right_transpose(back_in, w_down)
    d_pre_gate, d_pre_up = pull_ffn(d_hidden)
    d_gate_low = d_pre_gate.astype(jnp.bfloat16)
    d_up_low = d_pre_up.astype(jnp.bfloat16)
    dw_gate = rows_contract(xn_two, d_gate_low)
    dw_up = rows_contract(xn_two, d_up_low)
    d_norm_two = right_transpose(d_gate_low, w_gate) + right_transpose(d_up_low, w_up)
    d_resid_part, dg_ffn = pull_two(d_norm_two)
    d_resid = back_f + d_resid_part
    d_attn = d_resid.astype(jnp.bfloat16)
    dw_output = rows_contract(gated_out, d_attn)
    d_gated = right_transpose(d_attn, w_output)
    d_mixed_f, d_gate_out_f, dg_head = pull_head(d_gated)
    d_mixed = d_mixed_f.astype(jnp.bfloat16).reshape(val_shape)
    d_scores = jnp.einsum(
        "cthe,cshe->chts", d_mixed, val_blocks, preferred_element_type=jnp.float32
    )
    d_probs = (d_scores * causal).astype(jnp.bfloat16)
    d_q_gate = jnp.einsum(
        "chts,cshd->cthd", d_probs, k_back, preferred_element_type=jnp.float32
    ) + jnp.einsum("cthe,chde->cthd", d_mixed, before_low, preferred_element_type=jnp.float32)
    d_k_back = jnp.einsum("chts,cthd->cshd", d_probs, q_gate, preferred_element_type=jnp.float32)
    d_val_intra = jnp.einsum(
        "chts,cthe->cshe", attn_probs, d_mixed, preferred_element_type=jnp.float32
    )
    d_before = jnp.einsum("cthd,cthe->chde", q_gate, d_mixed, preferred_element_type=jnp.float32)

    d_before_seq = d_before.reshape(seq_blocks)
    d_after = jnp.zeros_like(upd_seq[:, 0])
    d_update_list = []
    d_decay_list = []
    for idx in reversed(range(per_seq)):
        d_update_list.append(d_after)
        d_decay_list.append(jnp.sum(d_after * before_seq[:, idx], axis=-1))
        d_after = d_before_seq[:, idx] + decay_seq[:, idx][..., None] * d_after
    d_update = jnp.stack(d_update_list[::-1], axis=1).reshape(update.shape)
    d_decays = jnp.stack(d_decay_list[::-1], axis=1).reshape(decays.shape)
    d_update_low = d_update.astype(jnp.bfloat16)
    d_k_tail = jnp.einsum(
        "cthe,chde->cthd", val_blocks, d_update_low, preferred_element_type=jnp.float32
    )
    d_values = (
        (
            d_val_intra
            + jnp.einsum(
                "cthd,chde->cthe", k_tail, d_update_low, preferred_element_type=jnp.float32
            )
        )
        .reshape(row_count, -1)
        .astype(jnp.bfloat16)
    )
    d_query_f, d_key_f, d_forget = pull_gates((d_q_gate, d_k_back, d_k_tail, d_decays))
    d_queries = d_query_f.reshape(row_count, -1).astype(jnp.bfloat16)
    d_keys = d_key_f.reshape(row_count, -1).astype(jnp.bfloat16)
    (d_logits,) = pull_forget(d_forget.reshape(row_count, -1))
    db_forget = jnp.sum(d_logits, axis=0)
    d_logit_low = d_logits.astype(jnp.bfloat16)
    dw_forget = rows_contract(lowrank, d_logit_low)
    d_lowrank = right_transpose(d_logit_low, w_forget).astype(jnp.bfloat16)
    d_gate_out = d_gate_out_f.astype(jnp.bfloat16)
    dw_query = rows_contract(xn_one, d_queries)
    dw_key = rows_contract(xn_one, d_keys)
    dw_value = rows_contract(xn_one, d_values)
    dw_outgate = rows_contract(xn_one, d_gate_out)
    dw_lowrank = rows_contract(xn_one, d_lowrank)
    d_norm_one = (
        right_transpose(d_queries, w_query)
        + right_transpose(d_keys, w_key)
        + right_transpose(d_values, w_value)
        + right_transpose(d_gate_out, w_outgate)
        + right_transpose(d_lowrank, w_lowrank)
    )
    d_flat, dg_attn = pull_one(d_norm_one)
    grad_rows = (d_resid + d_flat).astype(jnp.bfloat16)
    grads = (
        dg_attn,
        dw_query,
        dw_key,
        dw_value,
        dw_outgate,
        dw_lowrank,
        dw_forget,
        db_forget,
        dg_head,
        dw_output,
        dg_ffn,
        dw_gate,
        dw_up,
        dw_down,
    )
    return (output, grad_rows, grads)


def when(cond, do):
    if isinstance(cond, bool):
        if cond:
            do()
    else:
        pl.when(cond)(do)


def columns(ref, lo, hi):
    return ref[:, :, :, :, lo:hi].reshape(D, hi - lo)


def put_columns(ref, lo, hi, value):
    ref[:, :, :, :, lo:hi] = value.reshape(GRP, SQUARE, CORES, ROWS, hi - lo)


def flip(index, bit):
    return index + bit - 2 * bit * lax.rem(index // bit, 2)


def remote(src, dst, send_sem, recv_sem, device):
    return pltpu.make_async_remote_copy(
        src_ref=src,
        dst_ref=dst,
        send_sem=send_sem,
        recv_sem=recv_sem,
        device_id=device,
        device_id_type=MESH,
    )


def start_all(copies):
    for copy in copies:
        copy.start()


def recv_all(copies):
    for copy in copies:
        copy.wait_recv()


def sent_all(copies):
    for copy in copies:
        copy.wait_send()


class Place:
    def __init__(self):
        self.z = lax.axis_index("grp")
        self.s = lax.axis_index("shard")
        self.core = lax.rem(self.s, CORES)
        self.q = self.s // CORES
        self.qx = flip(self.q, 1)
        self.qy = flip(self.q, 2)
        self.qd = flip(self.qx, 2)
        self.z_peers = [lax.rem(self.z + step, GRP) for step in range(1, GRP)]
        self.z_from = [lax.rem(self.z + GRP - step, GRP) for step in range(1, GRP)]
        self.line_to = [(peer, self.s) for peer in self.z_peers]
        self.sib = (self.z, flip(self.s, 1))
        self.xn = (self.z, flip(self.s, CORES))
        self.yn = (self.z, flip(self.s, 2 * CORES))

    def greet(self):
        barrier = pltpu.get_barrier_semaphore()
        peers = self.line_to + [self.sib, self.xn, self.yn]
        for peer in peers:
            pl.semaphore_signal(barrier, inc=1, device_id=peer, device_id_type=MESH)
        return (barrier, len(peers))


class Gather:
    def __init__(self, place, parts, full, sems):
        self.p = place
        self.parts = parts
        self.full = full
        self.ls, self.zs, self.zr, self.xs, self.xr, self.ds, self.dr, self.ss, self.sr = sems

    def cols(self, c):
        narrow = isinstance(c, int) and c == MIX_CHUNKS - 1
        return pl.ds(0, LAST_WIDE if narrow else WIDE)

    def mine(self, c):
        return self.parts.at[c // 16, c % 16 // SQUARE, c % SQUARE, :, self.cols(c)]

    def locals(self):
        p = self.p
        groups = [(g, pl.ds(g * SQUARE, SQUARE)) for g in range(16 // SQUARE)]
        copies = [
            pltpu.make_async_copy(
                self.parts.at[0, g], self.full.at[chunks, p.z, p.q, p.core], self.ls.at[g]
            )
            for g, chunks in groups
        ]
        last = pltpu.make_async_copy(
            self.parts.at[1, 0, 0], self.full.at[16, p.z, p.q, p.core], self.ls.at[4]
        )
        return copies + [last]

    def view(self, c, z, q):
        return self.full.at[c, z, q, self.p.core, :, self.cols(c)]

    def line(self, c):
        p = self.p
        there = self.view(c, p.z, p.q)
        return [
            remote(self.mine(c), there, self.zs.at[c, k], self.zr.at[c, k], p.line_to[k])
            for k in range(GRP - 1)
        ]

    def line_in(self, c):
        p = self.p
        return [
            remote(
                self.view(c, p.z, p.q),
                self.view(c, p.z_from[k], p.q),
                self.zs.at[c, k],
                self.zr.at[c, k],
                p.line_to[k],
            )
            for k in range(GRP - 1)
        ]

    def z_part(self, c):
        return self.p.z if isinstance(c, int) and c in SPREAD else pl.ds(0, GRP)

    def plane(self, c):
        p = self.p
        there = self.view(c, self.z_part(c), p.q)
        here = self.mine(c) if isinstance(c, int) and c in SPREAD else there
        return [
            remote(here, there, self.xs.at[c, k], self.xr.at[c, k], to)
            for k, to in enumerate((p.xn, p.yn))
        ]

    def plane_in(self, c):
        p = self.p
        return [
            remote(view, view, self.xs.at[c, k], self.xr.at[c, k], to)
            for k, (view, to) in enumerate(
                (
                    (self.view(c, self.z_part(c), p.qx), p.xn),
                    (self.view(c, self.z_part(c), p.qy), p.yn),
                )
            )
        ]

    def halves(self, c, q_low, q_high):
        if isinstance(c, int) and c in SPREAD:
            half = ROWS // 2
            return (
                self.full.at[c, self.p.z, q_low, self.p.core, pl.ds(0, half)],
                self.full.at[c, self.p.z, q_high, self.p.core, pl.ds(half, half)],
            )
        return (self.view(c, pl.ds(0, 2), q_low), self.view(c, pl.ds(2, 2), q_high))

    def corner(self, c):
        p = self.p
        low, high = self.halves(c, p.qx, p.qy)
        return [
            remote(low, low, self.ds.at[c, 0], self.dr.at[c, 0], p.yn),
            remote(high, high, self.ds.at[c, 1], self.dr.at[c, 1], p.xn),
        ]

    def corner_in(self, c):
        p = self.p
        low, high = self.halves(c, p.qd, p.qd)
        return [
            remote(low, low, self.ds.at[c, 0], self.dr.at[c, 0], p.yn),
            remote(high, high, self.ds.at[c, 1], self.dr.at[c, 1], p.xn),
        ]

    def spread(self, c):
        p = self.p
        own = self.full.at[c, p.z, :, p.core]
        return [
            remote(own, own, self.zs.at[c, k], self.zr.at[c, k], p.line_to[k])
            for k in range(GRP - 1)
        ]

    def spread_in(self, c):
        p = self.p
        return [
            remote(
                self.full.at[c, p.z, :, p.core],
                self.full.at[c, p.z_from[k], :, p.core],
                self.zs.at[c, k],
                self.zr.at[c, k],
                p.line_to[k],
            )
            for k in range(GRP - 1)
        ]

    def other(self, c, core):
        view = self.full.at[c, :, :, core, :, self.cols(c)]
        return remote(view, view, self.ss.at[c], self.sr.at[c], self.p.sib)

    def other_in(self, c):
        self.other(c, 1 - self.p.core).wait_recv()

    def other_out(self, c):
        self.other(c, self.p.core).start()

    def line_out(self, c):
        start_all(self.line(c))

    def line_stage(self, c):
        recv_all(self.line_in(c))
        start_all(self.plane(c))

    def plane_stage(self, c):
        recv_all(self.plane_in(c))
        start_all(self.corner(c))

    def corner_stage(self, c):
        recv_all(self.corner_in(c))
        self.other_out(c)

    def spread_first(self, c):
        start_all(self.plane(c))

    def spread_out(self, c):
        recv_all(self.corner_in(c))
        start_all(self.spread(c))

    def spread_last(self, c):
        recv_all(self.spread_in(c))
        self.other_out(c)

    def step(self, t):
        def some(c, do):
            when(0 <= c < LINES, lambda: do(c))

        some(t + AHEAD, self.line_out)
        some(t, self.line_stage)
        some(t - 1, self.plane_stage)
        some(t - 2, self.corner_stage)
        some(t - 3, self.other_in)
        if t == 1:
            for c in SPREAD:
                self.plane_stage(c)
        if t == LINES - AHEAD - 1:
            self.spread_out(SPREAD[0])
        if t == LINES - AHEAD:
            self.spread_out(SPREAD[1])

    def mid_step(self, t):
        self.line_stage(t)
        self.plane_stage(t - 1)
        self.corner_stage(t - 2)
        self.other_in(t - 3)

    def late_step(self, t):
        when(t == LINES, lambda: self.plane_stage(LINES - 1))
        when(t <= LINES + 1, lambda: self.corner_stage(t - 2))
        when(t <= LINES + 2, lambda: self.other_in(t - 3))
        when(t == LINES + 2, lambda: self.spread_last(SPREAD[0]))
        when(t == LINES + 3, lambda: self.other_in(SPREAD[0]))
        when(t == LINES + 3, lambda: self.spread_last(SPREAD[1]))
        when(t == LINES + 4, lambda: self.other_in(SPREAD[1]))

    def drain_parts(self):
        for c in range(LINES):
            sent_all(self.line(c))
        for c in SPREAD:
            sent_all(self.plane(c))

    def drain(self, c):
        along = self.spread(c) if c in SPREAD else self.plane(c)
        sent_all(along + self.corner(c) + [self.other(c, self.p.core)])


class Reduce:
    def __init__(self, place, src, out, bufs, sems):
        self.p = place
        self.src = src
        self.out = out
        self.own, self.b1, self.b2, self.b3, self.b4, self.stage = bufs
        (
            self.ls,
            self.s1,
            self.r1,
            self.s2,
            self.r2,
            self.s3,
            self.r3,
            self.s4,
            self.r4,
            self.out_sem,
        ) = sems

    def slot(self, c):
        return c % SLOTS if isinstance(c, int) else lax.rem(c, SLOTS)

    def wide(self, c):
        return LAST_WIDE if isinstance(c, int) and c == CHUNKS - 1 else WIDE

    def local(self, c):
        k, n = self.slot(c), pl.ds(0, self.wide(c))
        return pltpu.make_async_copy(
            self.src.at[c, :, :, self.p.core, :, n], self.own.at[k, :, :, :, n], self.ls.at[k]
        )

    def other(self, c):
        k, n = self.slot(c), pl.ds(0, self.wide(c))
        return remote(
            self.src.at[c, :, :, 1 - self.p.core, :, n],
            self.b1.at[k, :, :, :, n],
            self.s1.at[k],
            self.r1.at[k],
            self.p.sib,
        )

    def corner(self, c):
        p, k, n = self.p, self.slot(c), pl.ds(0, self.wide(c))
        return [
            remote(
                self.own.at[k, pl.ds(2 * i, 2), p.qd, :, n],
                self.b2.at[k, i, :, :, n],
                self.s2.at[k, i],
                self.r2.at[k, i],
                to,
            )
            for i, to in enumerate((p.xn, p.yn))
        ]

    def plane(self, c):
        p, k, n = self.p, self.slot(c), pl.ds(0, self.wide(c))
        return [
            remote(
                self.own.at[k, :, q, :, n],
                self.b3.at[k, i, :, :, n],
                self.s3.at[k, i],
                self.r3.at[k, i],
                to,
            )
            for i, (q, to) in enumerate(((p.qx, p.xn), (p.qy, p.yn)))
        ]

    def line(self, c):
        p, k, n = self.p, self.slot(c), pl.ds(0, self.wide(c))
        return [
            remote(
                self.own.at[k, p.z_peers[i], p.q, :, n],
                self.b4.at[k, i, :, n],
                self.s4.at[k, i],
                self.r4.at[k, i],
                p.line_to[i],
            )
            for i in range(GRP - 1)
        ]

    def drain(self, c):
        sent_all([self.other(c)] + self.corner(c) + self.plane(c) + self.line(c))

    def enter(self, c):
        when(c >= SLOTS, lambda: self.drain(c - SLOTS))
        self.local(c).start()
        self.other(c).start()

    def add_other(self, c):
        p, k, n = self.p, self.slot(c), slice(0, self.wide(c))
        self.local(c).wait()
        self.other(c).wait_recv()
        for q in (p.qd, p.qx, p.qy, p.q):
            total = wide_type(self.own[k, :, q, :, n]) + wide_type(self.b1[k, :, q, :, n])
            self.own[k, :, q, :, n] = low_type(total)
            if q is p.qd:
                start_all(self.corner(c))

    def add_corner(self, c):
        p, k, n = self.p, self.slot(c), slice(0, self.wide(c))
        recv_all(self.corner(c))
        for q, cut, i in ((p.qy, slice(0, 2), 0), (p.qx, slice(2, 4), 1)):
            total = wide_type(self.own[k, cut, q, :, n]) + wide_type(self.b2[k, i, :, :, n])
            self.own[k, cut, q, :, n] = low_type(total)
        start_all(self.plane(c))

    def add_plane(self, c):
        p, k, n = self.p, self.slot(c), slice(0, self.wide(c))
        recv_all(self.plane(c))
        total = wide_type(self.own[k, :, p.q, :, n])
        total += wide_type(self.b3[k, 0, :, :, n])
        total += wide_type(self.b3[k, 1, :, :, n])
        self.own[k, :, p.q, :, n] = low_type(total)
        start_all(self.line(c))

    def finish(self, c):
        p, k, n = self.p, self.slot(c), slice(0, self.wide(c))
        recv_all(self.line(c))
        total = wide_type(self.own[k, p.z, p.q, :, n])
        for i in range(GRP - 1):
            total += wide_type(self.b4[k, i, :, n])
        when(c >= SLOTS, lambda: self.leave(c - SLOTS).wait())
        self.stage[k, :, n] = total
        self.leave(c).start()

    def leave(self, c):
        k, n = self.slot(c), pl.ds(0, self.wide(c))
        return pltpu.make_async_copy(
            self.stage.at[k, :, n], self.out.at[c, :, n], self.out_sem.at[k]
        )

    def step(self, t):
        def some(c, do):
            if isinstance(c, int):
                when(0 <= c < CHUNKS, lambda: do(c))
            else:
                when(c >= 0, lambda: do(c))

        some(t - 3, self.finish)
        some(t + 1, self.enter)
        some(t, self.add_other)
        some(t - 1, self.add_corner)
        some(t - 2, self.add_plane)


def reduce_scratch():
    def buf(*shape):
        return pltpu.VMEM((SLOTS,) + shape + (ROWS, WIDE), jnp.bfloat16)

    bufs = [buf(GRP, SQUARE), buf(GRP, SQUARE), buf(2, 2), buf(2, GRP), buf(GRP - 1)]
    bufs.append(pltpu.VMEM((SLOTS, ROWS, WIDE), jnp.float32))
    sems = [DMA((SLOTS,))] * 3 + [DMA((SLOTS, count)) for count in (2, 2, 2, 2, 3, 3)]
    return bufs + sems + [DMA((SLOTS,))]


def mm_nn(left_mat, right_mat):
    return jnp.dot(left_mat, right_mat, preferred_element_type=jnp.float32)


def mm_nt(left_mat, right_mat):
    return right_transpose(left_mat, right_mat)


def mm_tn(left_mat, right_mat):
    return rows_contract(left_mat, right_mat)


def low_type(value):
    return value.astype(jnp.bfloat16)


def wide_type(value):
    return value.astype(jnp.float32)


def exact_sum(zero_one, value):
    high = low_type(value)
    rest = value - wide_type(high)
    mid = low_type(rest)
    last = low_type(rest - wide_type(mid))
    return mm_nn(zero_one, high) + mm_nn(zero_one, mid) + mm_nn(zero_one, last)


def iota(shape, dim):
    return lax.broadcasted_iota(jnp.int32, shape, dim)


def place_matrix(keep, columns):
    row = iota((D, columns), 0)
    col = iota((D, columns), 1)
    hit = (row // ROWS == col // keep) & (row % ROWS == col % keep)
    return low_type(jnp.where(hit, 1.0, 0.0))


def unit_matrix(size):
    return low_type(jnp.where(iota((size, size), 0) == iota((size, size), 1), 1.0, 0.0))


def row_rsqrt(value, eps):
    return lax.rsqrt(jnp.mean(value * value, axis=-1, keepdims=True) + eps)


class Layer:
    def __init__(self, refs):
        self.__dict__.update(refs)

    def rows(self, i):
        return pl.ds(pl.multiple_of(i * SEQ, SEQ), SEQ)

    def mask(self, lengths, dealing, first_seq):
        held = wide_type(lengths[...])
        for i in range(SEQS):
            r = pl.ds(i * SEQ, SEQ)
            match = dealing[...] == first_seq + i
            length = jnp.sum(jnp.where(match, held, 0.0), axis=1, keepdims=True)
            live = wide_type(iota((SEQ, 1), 0)) < length
            self.x[r, :] = jnp.where(live, self.x[r, :], jnp.zeros((), jnp.bfloat16))
            self.cot[r, :] = jnp.where(live, self.cot[r, :], jnp.zeros((), jnp.bfloat16))

    def prepare(self):
        misc = columns(self.wm.at[0], 0, MISC)
        turned = mm_nt(unit_matrix(MISC), misc)
        self.gains[0:1, :] = turned[RANK : RANK + 1]
        self.gains[1:2, :] = turned[RANK + 1 : RANK + 2]
        picked = mm_tn(misc, place_matrix(KEY_WIDE // DEVICES, KEY_WIDE))
        self.wf[...] = jnp.zeros_like(self.wf)
        self.wf[0:RANK, :] = low_type(picked[32 : 32 + RANK])
        self.bias[0:1, :] = picked[48:49]
        heads = mm_tn(misc, place_matrix(HEAD_VAL // DEVICES, HEAD_VAL))
        self.ghead[0:1, :] = heads[18:19]
        for i in range(SEQS):
            r = pl.ds(i * SEQ, SEQ)
            value = wide_type(self.x[r, :])
            self.xn1[r, :] = low_type(value * row_rsqrt(value, EPS) * self.gains[0:1, :])

    def project(self, c):
        lo, hi = c * WIDE, min((c + 1) * WIDE, PROJ)
        for r in HALVES:
            value = mm_nn(self.xn1[r, :], columns(self.wm.at[c], 0, hi - lo))
            for ref, at, first, last in self.pieces(lo, hi):
                ref[r, at : at + last - first] = value[:, first:last].astype(ref.dtype)

    def pieces(self, lo, hi):
        found = []
        for ref, start, end, at in (
            (self.proj, 0, V_AT, 0),
            (self.pval, V_AT, G_AT, 0),
            (self.proj, G_AT, PROJ, GATE_AT),
        ):
            a, b = max(lo, start), min(hi, end)
            if a < b:
                found.append((ref, at + a - start, a - lo, b - lo))
        return found

    def gates(self, r):
        lane = iota((SEQ, MISC), 1)
        lowrank = low_type(jnp.where(lane < RANK, self.proj[r, 0:MISC], 0.0))
        logits = mm_nn(lowrank, self.wf[...]) + self.bias[0:1, :]
        forget = (jnp.minimum(logits, 0.0) - jnp.log1p(jnp.exp(-jnp.abs(logits)))) * (1.0 / 16.0)
        row, col = iota((SEQ, SEQ), 0), iota((SEQ, SEQ), 1)
        same = row // BLOCK == col // BLOCK
        causal = same & (col <= row)
        running = exact_sum(low_type(jnp.where(causal, 1.0, 0.0)), forget)
        tails = [running[b * BLOCK + BLOCK - 1 : (b + 1) * BLOCK] for b in range(BLOCKS)]
        tail = jnp.concatenate(
            [jnp.broadcast_to(one, (BLOCK, KEY_WIDE)) for one in tails], axis=0
        )
        return (lowrank, logits, running, tails, tail, same, causal)

    def attend(self, i):
        r = self.rows(i)
        _, _, running, tails, tail, _, causal = self.gates(r)
        grow = jnp.exp(running)
        fade = jnp.exp(-running)
        late = jnp.exp(tail - running)
        for h in range(HEADS):
            k = slice(h * HEAD_KEY, (h + 1) * HEAD_KEY)
            queries = self.proj[r, Q_AT + h * HEAD_KEY : Q_AT + (h + 1) * HEAD_KEY]
            key_rows = self.proj[r, K_AT + h * HEAD_KEY : K_AT + (h + 1) * HEAD_KEY]
            values = self.pval[r, h * HEAD_VAL : (h + 1) * HEAD_VAL]
            q_gate = low_type(queries * SCALE * grow[:, k])
            k_back = low_type(key_rows * fade[:, k])
            k_tail = low_type(key_rows * late[:, k])
            probs = low_type(jnp.where(causal, mm_nt(q_gate, k_back), 0.0))
            mixed = mm_nn(probs, values)
            state = mm_tn(values[0:BLOCK], k_tail[0:BLOCK])
            parts = [mixed[0:BLOCK]]
            for b in range(1, BLOCKS):
                cut = slice(b * BLOCK, (b + 1) * BLOCK)
                parts.append(mixed[cut] + mm_nt(q_gate[cut], low_type(state)))
                if b + 1 < BLOCKS:
                    state = state * jnp.exp(tails[b][:, k]) + mm_tn(values[cut], k_tail[cut])
            self.mixed[r, h * HEAD_VAL : (h + 1) * HEAD_VAL] = jnp.concatenate(parts, axis=0)

    def gate_rows(self, i):
        r = self.rows(i)
        for h in range(HEADS):
            v = slice(h * HEAD_VAL, (h + 1) * HEAD_VAL)
            mixed = self.mixed[r, v]
            gate = self.proj[r, GATE_AT + h * HEAD_VAL : GATE_AT + (h + 1) * HEAD_VAL]
            normed = mixed * row_rsqrt(mixed, HEAD_EPS) * self.ghead[0:1, :]
            self.gated[r, v] = low_type(normed * (gate * jax.nn.sigmoid(gate)))

    def mix_out(self):
        cut = WIDE - O_AT % WIDE
        first = O_AT // WIDE
        lo = O_AT % WIDE
        for i in range(SEQS):
            r = pl.ds(i * SEQ, SEQ)
            self.out_sum[r, 0:cut] = wide_type(self.x[r, 0:cut]) + mm_nn(
                self.gated[r, :], columns(self.wm.at[first], lo, WIDE)
            )
            self.out_sum[r, cut:D] = wide_type(self.x[r, cut:D]) + mm_nn(
                self.gated[r, :], columns(self.wl, 0, D - cut)
            )

    def second_norm(self):
        for i in range(SEQS):
            r = pl.ds(i * SEQ, SEQ)
            value = self.out_sum[r, :]
            self.xn2[r, :] = low_type(value * row_rsqrt(value, EPS) * self.gains[1:2, :])
        self.dx_sum[...] = jnp.zeros_like(self.dx_sum)
        self.turn(self.xn2, self.turn_a)
        self.turn(self.cot, self.turn_b)

    def turn(self, src, dst):
        for i in range(LIVE // 256):
            dst[:, i * 256 : (i + 1) * 256] = src[i * 256 : (i + 1) * 256, :].T

    def ffn(self, w_ref, g_ref):
        c = FF_CUT
        for r in HALVES:
            pre = mm_nn(self.xn2[r, :], columns(w_ref, 0, 2 * c))
            d_hidden = mm_nn(self.cot[r, :], columns(w_ref, 2 * c, 3 * c))
            pre_gate, pre_up = pre[:, 0:c], pre[:, c : 2 * c]
            sig = jax.nn.sigmoid(pre_gate)
            silu = pre_gate * sig
            self.hid[r, :] = low_type(silu * pre_up)
            self.dpre[r, 0:c] = low_type(d_hidden * pre_up * sig * (1.0 + pre_gate * (1.0 - sig)))
            self.dpre[r, c : 2 * c] = low_type(d_hidden * silu)
            self.out_sum[r, :] += mm_nt(self.hid[r, :], columns(w_ref, 2 * c, 3 * c))
            self.dx_sum[r, :] += mm_nt(self.dpre[r, :], columns(w_ref, 0, 2 * c))
        put_columns(g_ref, 0, 2 * c, low_type(mm_nn(self.turn_a[...], self.dpre[...])))
        put_columns(g_ref, 2 * c, 3 * c, low_type(mm_nn(self.turn_b[...], self.hid[...])))

    def norm_back(self, value, d_out, gain, eps):
        rs = row_rsqrt(value, eps)
        scaled = gain * d_out
        mean = jnp.mean(value * scaled, axis=-1, keepdims=True)
        d_gain = jnp.sum(d_out * value * rs, axis=0, keepdims=True)
        return (rs * scaled - value * (rs * rs * rs * mean), d_gain)

    def after_ffn(self):
        cut = WIDE - O_AT % WIDE
        first = O_AT // WIDE
        lo = O_AT % WIDE
        total = jnp.zeros((1, D), jnp.float32)
        for i in range(SEQS):
            r = pl.ds(i * SEQ, SEQ)
            resid = wide_type(self.x[r, :]) + jnp.concatenate(
                [
                    mm_nn(self.gated[r, :], columns(self.wm.at[first], lo, WIDE)),
                    mm_nn(self.gated[r, :], columns(self.wl, 0, D - cut)),
                ],
                axis=1,
            )
            d_val, d_gain = self.norm_back(
                resid, self.dx_sum[r, :], self.gains[1:2, :], EPS
            )
            total += d_gain
            d_resid = wide_type(self.cot[r, :]) + d_val
            self.dx_sum[r, :] = d_resid
            self.xn2[r, :] = low_type(d_resid)
        self.dgains[1:2, :] = total
        self.turn(self.gated, self.turn_a)
        self.turn(self.xn1, self.turn_b)
        self.gated[...] = low_type(self.out_sum[...])
        self.dwf[...] = jnp.zeros_like(self.dwf)
        self.dbias[...] = jnp.zeros_like(self.dbias)
        self.dghead[...] = jnp.zeros_like(self.dghead)

    def retreat(self, i):
        r = self.rows(i)
        cut = WIDE - O_AT % WIDE
        first = O_AT // WIDE
        lo = O_AT % WIDE
        d_attn = self.xn2[r, :]
        d_gated = mm_nt(d_attn[:, 0:cut], columns(self.wm.at[first], lo, WIDE))
        d_gated += mm_nt(d_attn[:, cut:D], columns(self.wl, 0, D - cut))
        lowrank, logits, running, tails, tail, same, causal = self.gates(r)
        grow = jnp.exp(running)
        fade = jnp.exp(-running)
        late = jnp.exp(tail - running)
        d_forget_parts = []
        tail_parts = []
        d_ghead = jnp.zeros((1, HEAD_VAL), jnp.float32)
        for h in range(HEADS):
            k = slice(h * HEAD_KEY, (h + 1) * HEAD_KEY)
            v = slice(h * HEAD_VAL, (h + 1) * HEAD_VAL)
            q_cols = slice(Q_AT + h * HEAD_KEY, Q_AT + (h + 1) * HEAD_KEY)
            k_cols = slice(K_AT + h * HEAD_KEY, K_AT + (h + 1) * HEAD_KEY)
            g_cols = slice(GATE_AT + h * HEAD_VAL, GATE_AT + (h + 1) * HEAD_VAL)
            mixed = self.mixed[r, v]
            gate = self.proj[r, g_cols]
            sig = jax.nn.sigmoid(gate)
            act = gate * sig
            rs = row_rsqrt(mixed, HEAD_EPS)
            unit = mixed * rs
            gain = self.ghead[0:1, :]
            d_out = d_gated[:, v]
            d_normed = d_out * act
            d_gate = d_out * (unit * gain) * sig * (1.0 + gate * (1.0 - sig))
            self.proj[r, g_cols] = wide_type(low_type(d_gate))
            d_ghead += jnp.sum(d_normed * unit, axis=0, keepdims=True)
            scaled = gain * d_normed
            mean = jnp.mean(mixed * scaled, axis=-1, keepdims=True)
            d_mixed = low_type(rs * scaled - mixed * (rs * rs * rs * mean))

            q_full = self.proj[r, q_cols] * SCALE * grow[:, k]
            key_rows = self.proj[r, k_cols]
            kb_full = key_rows * fade[:, k]
            kt_full = key_rows * late[:, k]
            values = self.pval[r, v]
            q_gate, k_back, k_tail = low_type(q_full), low_type(kb_full), low_type(kt_full)
            probs = low_type(jnp.where(causal, mm_nt(q_gate, k_back), 0.0))
            d_probs = low_type(jnp.where(causal, mm_nt(d_mixed, values), 0.0))
            d_q = mm_nn(d_probs, k_back)
            d_kb = mm_tn(d_probs, q_gate)
            d_v = mm_tn(probs, d_mixed)
            cuts = [slice(b * BLOCK, (b + 1) * BLOCK) for b in range(BLOCKS)]
            before = [None, mm_tn(values[cuts[0]], k_tail[cuts[0]])]
            decay = [jnp.exp(tails[b][:, k]) for b in range(BLOCKS)]
            for b in range(2, BLOCKS):
                before.append(
                    before[b - 1] * decay[b - 1] + mm_tn(values[cuts[b - 1]], k_tail[cuts[b - 1]])
                )
            after = [None] * BLOCKS
            for b in range(BLOCKS - 1, 0, -1):
                d_before = mm_tn(d_mixed[cuts[b]], q_gate[cuts[b]])
                after[b - 1] = d_before if after[b] is None else d_before + decay[b] * after[b]
            q_parts, t_parts, v_parts, e_parts = [], [], [], []
            for b in range(BLOCKS):
                cut_b = cuts[b]
                part = d_q[cut_b]
                if b > 0:
                    part = part + mm_nn(d_mixed[cut_b], low_type(before[b]))
                q_parts.append(part)
                if after[b] is None:
                    t_parts.append(jnp.zeros((BLOCK, HEAD_KEY), jnp.float32))
                    v_parts.append(d_v[cut_b])
                    e_parts.append(jnp.zeros((1, HEAD_KEY), jnp.float32))
                    continue
                after_low = low_type(after[b])
                d_kt = mm_nn(values[cut_b], after_low)
                t_parts.append(d_kt)
                v_parts.append(d_v[cut_b] + mm_nt(k_tail[cut_b], after_low))
                extra = jnp.sum(d_kt * kt_full[cut_b], axis=0, keepdims=True)
                if b > 0:
                    extra += jnp.sum(after[b] * before[b], axis=0, keepdims=True) * decay[b]
                e_parts.append(extra)
            d_q = jnp.concatenate(q_parts, axis=0)
            d_kt = jnp.concatenate(t_parts, axis=0)
            d_v = jnp.concatenate(v_parts, axis=0)
            self.pval[r, v] = low_type(d_v)
            self.proj[r, q_cols] = wide_type(low_type(d_q * SCALE * grow[:, k]))
            self.proj[r, k_cols] = wide_type(low_type(d_kb * fade[:, k] + d_kt * late[:, k]))
            d_forget_parts.append(d_q * q_full - d_kb * kb_full - d_kt * kt_full)
            tail_parts.append(
                jnp.concatenate(
                    [jnp.broadcast_to(one, (BLOCK, HEAD_KEY)) for one in e_parts], axis=0
                )
            )
        self.dghead[0:1, :] += d_ghead
        d_running = jnp.concatenate(d_forget_parts, axis=1)
        row, col = iota((SEQ, SEQ), 0), iota((SEQ, SEQ), 1)
        later = low_type(jnp.where(same & (col >= row), 1.0, 0.0))
        d_forget = exact_sum(later, d_running) + jnp.concatenate(tail_parts, axis=1)
        d_logits = d_forget * jax.nn.sigmoid(-logits) * (1.0 / 16.0)
        self.dbias[0:1, :] += jnp.sum(d_logits, axis=0, keepdims=True)
        d_logit_low = low_type(d_logits)
        self.dwf[...] += mm_tn(lowrank, d_logit_low)
        self.proj[r, 0:MISC] = wide_type(low_type(mm_nt(d_logit_low, self.wf[...])))

    def d_proj(self, c, rows=slice(None)):
        lo, hi = c * WIDE, min((c + 1) * WIDE, PROJ)
        parts = [
            low_type(ref[rows, at : at + last - first])
            for ref, at, first, last in self.pieces(lo, hi)
        ]
        return parts[0] if len(parts) == 1 else jnp.concatenate(parts, axis=1)

    def first_norm_back(self):
        for c in range(-(-PROJ // WIDE)):
            for r in HALVES:
                d_proj = self.d_proj(c, r)
                part = mm_nt(d_proj, columns(self.wm.at[c], 0, d_proj.shape[1]))
                self.out_sum[r, :] = part if c == 0 else self.out_sum[r, :] + part
        total = jnp.zeros((1, D), jnp.float32)
        for i in range(SEQS):
            r = pl.ds(i * SEQ, SEQ)
            d_val, d_gain = self.norm_back(
                wide_type(self.x[r, :]), self.out_sum[r, :], self.gains[0:1, :], EPS
            )
            total += d_gain
            self.xn1[r, :] = low_type(self.dx_sum[r, :] + d_val)
        self.dgains[0:1, :] = total

    def mixer_grad(self, c, g_ref):
        first = O_AT // WIDE
        lo = O_AT % WIDE
        cut = WIDE - lo
        if c == first + 1:
            put_columns(g_ref, 0, D - cut, low_type(mm_nn(self.turn_a[...], self.xn2[:, cut:D])))
            return
        d_proj = self.d_proj(c)
        grad = mm_nn(self.turn_b[...], d_proj)
        if c == first:
            put_columns(g_ref, lo, WIDE, low_type(mm_nn(self.turn_a[...], self.xn2[:, 0:cut])))
            put_columns(g_ref, 0, lo, low_type(grad))
            return
        if c > 0:
            put_columns(g_ref, 0, WIDE, low_type(grad))
            return
        zero = jnp.zeros
        gains = jnp.concatenate(
            [zero((RANK, D), jnp.float32), self.dgains[...], zero((MISC - RANK - 8, D), jnp.float32)],
            axis=0,
        )
        small = mm_tn(low_type(gains), unit_matrix(MISC))
        keyed = jnp.concatenate(
            [
                zero((32, KEY_WIDE), jnp.float32),
                self.dwf[0:RANK, :],
                self.dbias[...],
                zero((MISC - 56, KEY_WIDE), jnp.float32),
            ],
            axis=0,
        )
        small += mm_nt(place_matrix(KEY_WIDE // DEVICES, KEY_WIDE), low_type(keyed))
        lane = iota((MISC, HEAD_VAL), 0)
        headed = jnp.where(lane == 18, jnp.broadcast_to(self.dghead[0:1, :], (MISC, HEAD_VAL)), 0.0)
        small += mm_nt(place_matrix(HEAD_VAL // DEVICES, HEAD_VAL), low_type(headed))
        put_columns(g_ref, 0, MISC, low_type(grad[:, 0:MISC] + small))
        put_columns(g_ref, MISC, WIDE, low_type(grad[:, MISC:WIDE]))


LAYER_SCRATCH = (
    ("small", (MISC, ROWS), jnp.float32),
    ("x", (LIVE, D), jnp.bfloat16),
    ("cot", (LIVE, D), jnp.bfloat16),
    ("xn1", (LIVE, D), jnp.bfloat16),
    ("proj", (LIVE, GATE_AT + VAL_WIDE), jnp.float32),
    ("pval", (LIVE, VAL_WIDE), jnp.bfloat16),
    ("wm", (MIX_CHUNKS - 1, GRP, SQUARE, CORES, ROWS, WIDE), jnp.bfloat16),
    ("wl", (GRP, SQUARE, CORES, ROWS, LAST_WIDE), jnp.bfloat16),
    ("gains", (8, D), jnp.float32),
    ("wf", (MISC, KEY_WIDE), jnp.bfloat16),
    ("bias", (8, KEY_WIDE), jnp.float32),
    ("ghead", (8, HEAD_VAL), jnp.float32),
    ("mixed", (LIVE, D), jnp.float32),
    ("gated", (LIVE, D), jnp.bfloat16),
    ("xn2", (LIVE, D), jnp.bfloat16),
    ("out_sum", (LIVE, D), jnp.float32),
    ("dx_sum", (LIVE, D), jnp.float32),
    ("turn_a", (D, LIVE), jnp.bfloat16),
    ("turn_b", (D, LIVE), jnp.bfloat16),
    ("hid", (LIVE, FF_CUT), jnp.bfloat16),
    ("dpre", (LIVE, 2 * FF_CUT), jnp.bfloat16),
    ("dgains", (8, D), jnp.float32),
    ("dwf", (MISC, KEY_WIDE), jnp.float32),
    ("dbias", (8, KEY_WIDE), jnp.float32),
    ("dghead", (8, HEAD_VAL), jnp.float32),
    ("wb", (2, GRP, SQUARE, CORES, ROWS, WIDE), jnp.bfloat16),
    ("gb", (2, GRP, SQUARE, CORES, ROWS, WIDE), jnp.bfloat16),
)


def fill_parts(parts, small, held):
    lowrank_t, g_attn, g_ffn, g_head, w_forget, b_forget = parts[:6]
    mats = parts[6:]
    small[...] = jnp.zeros_like(small)
    small[0:RANK, :] = wide_type(lowrank_t[...])
    small[RANK : RANK + 1, :] = wide_type(g_attn[...])
    small[RANK + 1 : RANK + 2, :] = wide_type(g_ffn[...])
    small[18:19, 0 : HEAD_VAL // DEVICES] = wide_type(g_head[...])
    small[32 : 32 + RANK, 0 : KEY_WIDE // DEVICES] = wide_type(w_forget[...])
    small[48:49, 0 : KEY_WIDE // DEVICES] = wide_type(b_forget[...])
    held[0, 0, 0, :, 0:MISC] = low_type(mm_tn(low_type(small[...]), unit_matrix(MISC)))
    at = MISC
    for ref in mats[:5]:
        end = at + ref.shape[1]
        for c in range(MIX_CHUNKS):
            lo, hi = max(at, c * WIDE), min(end, (c + 1) * WIDE)
            if lo < hi:
                held[0, c // SQUARE, c % SQUARE, :, lo - c * WIDE : hi - c * WIDE] = ref[
                    :, lo - at : hi - at
                ]
        at = end
    c = MIX_CHUNKS - 1
    held[0, c // SQUARE, c % SQUARE, :, LAST_WIDE:WIDE] = jnp.zeros(
        (ROWS, WIDE - LAST_WIDE), jnp.bfloat16
    )
    for f in range(FF_CHUNKS):
        c = MIX_CHUNKS + f
        for i, ref in enumerate(mats[5:]):
            held[c // 16, c % 16 // SQUARE, c % SQUARE, :, i * FF_CUT : (i + 1) * FF_CUT] = ref[
                :, f * FF_CUT : (f + 1) * FF_CUT
            ]


def layer_kernel(*refs):
    parts, refs = refs[:14], refs[14:]
    (x_in, cot_in, lengths, dealing), refs = refs[:4], refs[4:]
    (out, grad, red, full, grads), scratch = refs[:5], refs[5:]
    count = len(LAYER_SCRATCH)
    refs = {name: ref for (name, _, _), ref in zip(LAYER_SCRATCH, scratch[:count])}
    scratch = scratch[count:]
    g_sems, scratch = scratch[:9], scratch[9:]
    load_sem, store_sem, out_sem = scratch[:3]
    bufs, r_sems = scratch[3:9], scratch[9:]

    place = Place()
    barrier, greeted = place.greet()
    gather = Gather(place, bufs[0], full, g_sems)
    red_op = Reduce(place, grads, red, bufs, r_sems)
    work = Layer(refs)
    x_copy = pltpu.make_async_copy(x_in, work.x, out_sem.at[0])
    cot_copy = pltpu.make_async_copy(cot_in, work.cot, out_sem.at[1])

    def load(c, ref, k):
        return pltpu.make_async_copy(full.at[c], ref, load_sem.at[k])

    def load_ffn(f):
        k = f % 2 if isinstance(f, int) else lax.rem(f, 2)
        return load(MIX_CHUNKS + f, work.wb.at[k], k)

    def load_mixer(c):
        if c == MIX_CHUNKS - 1:
            half = pl.ds(0, LAST_WIDE)
            return pltpu.make_async_copy(
                full.at[c, :, :, :, :, half], work.wl, load_sem.at[0]
            )
        return load(c, work.wm.at[c], 0)

    def store(o, k):
        if isinstance(o, int) and o == CHUNKS - 1:
            half = pl.ds(0, LAST_WIDE)
            return pltpu.make_async_copy(
                work.gb.at[k, :, :, :, :, half], grads.at[o, :, :, :, :, half], store_sem.at[k]
            )
        return pltpu.make_async_copy(work.gb.at[k], grads.at[o], store_sem.at[k])

    def fetch_mixer(c):
        copy = load_mixer(c)
        copy.start()
        copy.wait()

    fill_parts(parts, work.small, bufs[0])
    own_copies = gather.locals()
    start_all(own_copies)
    x_copy.start()
    cot_copy.start()
    work.dgains[...] = jnp.zeros_like(work.dgains)
    pl.semaphore_wait(barrier, greeted)
    for c in SPREAD:
        gather.spread_first(c)
    for c in range(AHEAD):
        gather.line_out(c)
    for copy in own_copies:
        copy.wait()
    gather.step(0)
    x_copy.wait()
    cot_copy.wait()
    first_seq = (place.z * SHARD + place.s) * SEQS
    work.mask(lengths, dealing, first_seq)
    for t in range(1, 4):
        gather.step(t)
    fetch_mixer(0)
    work.prepare()
    work.project(0)
    for c in (1, 2, 3):
        gather.step(3 + c)
        fetch_mixer(c)
        work.project(c)
    work.attend(0)
    work.attend(1)
    gather.step(7)
    fetch_mixer(4)
    work.project(4)
    work.attend(2)
    work.attend(3)
    gather.step(8)
    fetch_mixer(5)
    for i in range(SEQS):
        work.gate_rows(i)
    work.mix_out()
    gather.step(9)
    load_ffn(0).start()
    work.second_norm()

    def ffn_step(f, reduce_too):
        k = lax.rem(f, 2)
        if reduce_too:
            gather.late_step(10 + f)
        else:
            gather.mid_step(10 + f)
        load_ffn(f).wait()
        when(f + 1 < FF_CHUNKS, lambda: load_ffn(f + 1).start())
        when(f >= 2, lambda: store(f - 2, k).wait())
        work.ffn(work.wb.at[k], work.gb.at[k])
        store(f, k).start()
        if reduce_too:
            red_op.step(f - RED_FROM)
        return 0

    def ffn_first(f, carry):
        return ffn_step(f, False)

    def ffn_last(f, carry):
        return ffn_step(f, True)

    lax.fori_loop(0, RED_FROM, ffn_first, 0)
    gather.drain_parts()
    red_op.enter(0)
    lax.fori_loop(RED_FROM, FF_CHUNKS, ffn_last, 0)
    for f in (FF_CHUNKS - 2, FF_CHUNKS - 1):
        store(f, f % 2).wait()
    steps = list(range(FF_CHUNKS - RED_FROM, CHUNKS + 3))

    def reduce_step(ready):
        if steps and steps[0] + 1 < ready:
            red_op.step(steps.pop(0))

    work.after_ffn()
    out_copy = pltpu.make_async_copy(work.gated, out, out_sem.at[0])
    out_copy.start()
    reduce_step(FF_CHUNKS)
    for i in range(SEQS):
        work.retreat(i)
        reduce_step(FF_CHUNKS)
    work.first_norm_back()
    grad_copy = pltpu.make_async_copy(work.xn1, grad, out_sem.at[1])
    grad_copy.start()
    reduce_step(FF_CHUNKS)
    for n, c in enumerate((4, 3, 2, 1, 0, 5)):
        work.mixer_grad(c, work.gb.at[n % 2])
        copy = store(FF_CHUNKS + n, n % 2)
        copy.start()
        copy.wait()
        reduce_step(FF_CHUNKS + n + 1)
        reduce_step(FF_CHUNKS + n + 1)
    while steps:
        red_op.step(steps.pop(0))
    out_copy.wait()
    grad_copy.wait()
    for c in range(CHUNKS):
        gather.drain(c)
    for c in range(CHUNKS - SLOTS, CHUNKS):
        red_op.drain(c)
        red_op.leave(c).wait()


def layer_call(parts, x, cot, lengths, dealing):
    any_spec = pl.BlockSpec(memory_space=pl.ANY)
    vmem = pl.BlockSpec(memory_space=pltpu.VMEM)
    chunk = (CHUNKS, GRP, SQUARE, CORES, ROWS, WIDE)
    rows = jax.ShapeDtypeStruct((LIVE, D), jnp.bfloat16)
    scratch = [pltpu.VMEM(shape, kind) for _, shape, kind in LAYER_SCRATCH]
    scratch += [DMA((5,))] + [DMA((CHUNKS, 3))] * 2 + [DMA((CHUNKS, 2))] * 4 + [DMA((CHUNKS,))] * 2
    scratch += [DMA((2,)), DMA((2,)), DMA((2,))]
    scratch += reduce_scratch()
    result = pl.pallas_call(
        layer_kernel,
        out_shape=(
            rows,
            rows,
            jax.ShapeDtypeStruct((CHUNKS, ROWS, WIDE), jnp.float32),
            jax.ShapeDtypeStruct(chunk, jnp.bfloat16),
            jax.ShapeDtypeStruct(chunk, jnp.bfloat16),
        ),
        in_specs=[vmem] * 14 + [any_spec] * 2 + [vmem] * 2,
        out_specs=(any_spec,) * 5,
        scratch_shapes=scratch,
        compiler_params=pltpu.CompilerParams(
            collective_id=0, has_side_effects=True, vmem_limit_bytes=VMEM_LIMIT
        ),
    )(*parts, x, cot, lengths, dealing)
    return result[:3]


def chunk_place(c):
    return FF_CHUNKS + (4, 3, 2, 1, 0, 5).index(c)


def finish_kernel(red, out_in, grad_in, *outs):
    outs[0][...] = out_in[...]
    outs[1][...] = grad_in[...]
    (
        g_attn,
        w_query,
        w_key,
        w_value,
        w_outgate,
        w_lowrank,
        w_forget,
        b_forget,
        g_head,
        w_output,
        g_ffn,
        w_gate,
        w_up,
        w_down,
    ) = outs[2:]
    misc = red[chunk_place(0), :, 0:MISC]
    turned = misc.T
    w_lowrank[...] = turned[0:RANK]
    g_attn[...] = turned[RANK : RANK + 1]
    g_ffn[...] = turned[RANK + 1 : RANK + 2]
    g_head[...] = turned[18:19, 0 : HEAD_VAL // DEVICES]
    w_forget[...] = turned[32 : 32 + RANK, 0 : KEY_WIDE // DEVICES]
    b_forget[...] = turned[48:49, 0 : KEY_WIDE // DEVICES]
    at = MISC
    for ref in (w_query, w_key, w_value, w_outgate, w_output):
        end = at + ref.shape[1]
        for c in range(MIX_CHUNKS):
            lo, hi = max(at, c * WIDE), min(end, (c + 1) * WIDE)
            if lo < hi:
                ref[:, lo - at : hi - at] = red[chunk_place(c), :, lo - c * WIDE : hi - c * WIDE]
        at = end
    for f in range(FF_CHUNKS):
        cut = slice(f * FF_CUT, (f + 1) * FF_CUT)
        w_gate[:, cut] = red[f, :, 0:FF_CUT]
        w_up[:, cut] = red[f, :, FF_CUT : 2 * FF_CUT]
        w_down[:, cut] = red[f, :, 2 * FF_CUT : 3 * FF_CUT]


def finish_call(red, out_rows, grad_rows, shapes):
    vmem = pl.BlockSpec(memory_space=pltpu.VMEM)
    rows = jax.ShapeDtypeStruct(out_rows.shape, out_rows.dtype)
    return pl.pallas_call(
        finish_kernel,
        out_shape=(rows, rows) + tuple(jax.ShapeDtypeStruct(one, jnp.float32) for one in shapes),
        in_specs=[vmem] * 3,
        out_specs=(vmem,) * (2 + len(shapes)),
        compiler_params=pltpu.CompilerParams(vmem_limit_bytes=VMEM_LIMIT),
    )(red, out_rows, grad_rows)


def plain_shards(
    inputs,
    cotangent,
    lengths,
    dealing,
    g_attn,
    w_query,
    w_key,
    w_value,
    w_outgate,
    w_lowrank,
    w_forget,
    b_forget,
    g_head,
    w_output,
    g_ffn,
    w_gate,
    w_up,
    w_down,
):
    axes = ("grp", "shard")
    shard_count = lax.axis_size("shard")
    self_index = lax.axis_index("grp") * shard_count + lax.axis_index("shard")
    seq_dev, max_len, _ = inputs.shape
    own_given = self_index * seq_dev + jnp.arange(seq_dev, dtype=jnp.int32)
    own_len = jnp.sum(jnp.where(dealing[None, :] == own_given[:, None], lengths[None, :], 0), axis=1)
    live = jnp.arange(max_len, dtype=jnp.int32)[None, :] < own_len[:, None]
    zero_low = jnp.zeros((), jnp.bfloat16)
    rows_in = jnp.where(live[..., None], inputs, zero_low).reshape(seq_dev * max_len, D)
    back_in = jnp.where(live[..., None], cotangent, zero_low).reshape(seq_dev * max_len, D)
    shard_weights = (
        g_attn,
        w_query,
        w_key,
        w_value,
        w_outgate,
        w_lowrank,
        w_forget,
        b_forget,
        g_head,
        w_output,
        g_ffn,
        w_gate,
        w_up,
        w_down,
    )
    grad_dims = (0, 0, 0, 0, 0, 0, 1, 0, 0, 0, 0, 0, 0, 1)
    gathered = tuple(
        lax.all_gather(weight, axes, axis=dim, tiled=True)
        for weight, dim in zip(shard_weights, grad_dims)
    )
    out_rows, grad_rows, grads = layer_pass(gathered, rows_in, back_in, seq_dev)
    reduced = tuple(
        lax.psum_scatter(
            grad.astype(jnp.bfloat16), axes, scatter_dimension=dim, tiled=True
        ).astype(jnp.float32)
        for grad, dim in zip(grads, grad_dims)
    )
    return (out_rows.reshape(inputs.shape), grad_rows.reshape(inputs.shape)) + reduced


def kernel_shards(
    inputs,
    cotangent,
    lengths,
    dealing,
    g_attn,
    w_query,
    w_key,
    w_value,
    w_outgate,
    w_lowrank,
    w_forget,
    b_forget,
    g_head,
    w_output,
    g_ffn,
    w_gate,
    w_up,
    w_down,
):
    seq_dev, max_len, _ = inputs.shape
    rows = (seq_dev * max_len, D)
    parts = (
        w_lowrank.T,
        g_attn.reshape(1, -1),
        g_ffn.reshape(1, -1),
        g_head.reshape(1, -1),
        w_forget,
        b_forget.reshape(1, -1),
        w_query,
        w_key,
        w_value,
        w_outgate,
        w_output,
        w_gate,
        w_up,
        w_down.T,
    )
    out_rows, grad_rows, red = layer_call(
        parts,
        inputs.reshape(rows),
        cotangent.reshape(rows),
        lengths.reshape(1, -1),
        dealing.reshape(1, -1),
    )
    weights = (
        g_attn,
        w_query,
        w_key,
        w_value,
        w_outgate,
        w_lowrank,
        w_forget,
        b_forget,
        g_head,
        w_output,
        g_ffn,
        w_gate,
        w_up,
        w_down,
    )
    shapes = [one.shape if one.ndim == 2 else (1,) + one.shape for one in weights]
    turned = (5, 13)
    for i in turned:
        shapes[i] = shapes[i][::-1]
    result = finish_call(red, out_rows, grad_rows, shapes)
    sums = tuple(
        one.T if i in turned else one.reshape(like.shape)
        for i, (one, like) in enumerate(zip(result[2:], weights))
    )
    return (result[0].reshape(inputs.shape), result[1].reshape(inputs.shape)) + sums


def solution(mesh):
    small = mesh.shape["grp"] == GRP and mesh.shape["shard"] == SHARD
    return jax.shard_map(
        kernel_shards if small else plain_shards,
        mesh=mesh,
        in_specs=(
            P(("grp", "shard"), None, None),
            P(("grp", "shard"), None, None),
            P(),
            P(),
            P(("grp", "shard")),
            P(("grp", "shard"), None),
            P(("grp", "shard"), None),
            P(("grp", "shard"), None),
            P(("grp", "shard"), None),
            P(("grp", "shard"), None),
            P(None, ("grp", "shard")),
            P(("grp", "shard")),
            P(("grp", "shard")),
            P(("grp", "shard"), None),
            P(("grp", "shard")),
            P(("grp", "shard"), None),
            P(("grp", "shard"), None),
            P(None, ("grp", "shard")),
        ),
        out_specs=(
            P(("grp", "shard"), None, None),
            P(("grp", "shard"), None, None),
            P(("grp", "shard")),
            P(("grp", "shard"), None),
            P(("grp", "shard"), None),
            P(("grp", "shard"), None),
            P(("grp", "shard"), None),
            P(("grp", "shard"), None),
            P(None, ("grp", "shard")),
            P(("grp", "shard")),
            P(("grp", "shard")),
            P(("grp", "shard"), None),
            P(("grp", "shard")),
            P(("grp", "shard"), None),
            P(("grp", "shard"), None),
            P(None, ("grp", "shard")),
        ),
        check_vma=False,
    )
```

```python
import jax
import jax.numpy as jnp
from jax import lax
from jax.experimental import pallas as pl
from jax.experimental.pallas import tpu as pltpu
from jax.sharding import PartitionSpec as P

D = 1024
HEADS = 4
BLOCK = 64


EPS = 1e-05
HEAD_EPS = 1.0

MESH = pl.DeviceIdType.MESH
DMA = pltpu.SemaphoreType.DMA
GRP = 4
SHARD = 8
ROWS = 32
WIDE = 768
FF_CUT = 256
SLOTS = 4
MISC = 128
DEVICES = 32
RANK = 16
KEY_WIDE = 512
VAL_WIDE = 1024
HEAD_KEY = 128
HEAD_VAL = 256
SCALE = 128 ** (-0.5)
SEQS = 4
SEQ = 192
BLOCKS = 3
LIVE = SEQS * SEQ
Q_AT = MISC
K_AT = Q_AT + KEY_WIDE
V_AT = K_AT + KEY_WIDE
G_AT = V_AT + VAL_WIDE
O_AT = G_AT + VAL_WIDE
PROJ = O_AT
GATE_AT = V_AT
MIX_CHUNKS = 6
FF_CHUNKS = 11
CHUNKS = MIX_CHUNKS + FF_CHUNKS
LAST_WIDE = O_AT + D - (MIX_CHUNKS - 1) * WIDE
MIX_ORDER = (5, 4, 3, 2, 1, 0)
NARROW = FF_CHUNKS + MIX_ORDER.index(MIX_CHUNKS - 1)
AHEAD = 4
SPREAD_AT = (7, 9)
PASS_AT = (13, 15)
RED_FROM = 5
SQUARE = 4
CORES = 2
SPREAD = (15, 16)
LINES = 15
VMEM_LIMIT = 63 << 20
HALVES = (slice(0, LIVE // 2), slice(LIVE // 2, LIVE))


def matmul(left_mat, right_mat):
    return jnp.dot(left_mat, right_mat, preferred_element_type=jnp.float32)


def rows_contract(left_mat, right_mat):
    return lax.dot_general(
        left_mat, right_mat, (((0,), (0,)), ((), ())), preferred_element_type=jnp.float32
    )


def right_transpose(left_mat, right_mat):
    return lax.dot_general(
        left_mat, right_mat, (((1,), (1,)), ((), ())), preferred_element_type=jnp.float32
    )


def scaled_rows(rows_in, gain_vec):
    return rows_in * lax.rsqrt(jnp.mean(rows_in * rows_in, axis=-1, keepdims=True) + EPS) * gain_vec


def head_rows(rows_in, gain_vec):
    return (
        rows_in
        * lax.rsqrt(jnp.mean(rows_in * rows_in, axis=-1, keepdims=True) + HEAD_EPS)
        * gain_vec
    )


def forget_rate(logits):
    return jax.nn.log_sigmoid(logits) / 16.0


def swiglu_core(pre_gate, pre_up):
    return jax.nn.silu(pre_gate) * pre_up


def head_gate(mixed_out, gate_out, head_gain):
    normed = head_rows(mixed_out, head_gain)
    active = gate_out * jax.nn.sigmoid(gate_out)
    return normed.reshape(active.shape) * active


def block_gates(queries, key_rows, forget):
    running = jnp.cumsum(forget, axis=1)
    tail_sum = running[:, -1:]
    q_gate = queries * queries.shape[-1] ** (-0.5) * jnp.exp(running)
    k_back = key_rows * jnp.exp(-running)
    k_tail = key_rows * jnp.exp(tail_sum - running)
    return (q_gate, k_back, k_tail, jnp.exp(tail_sum[:, 0]))


def layer_pass(weights, rows_in, back_in, seq_count):
    (
        g_attn,
        w_query,
        w_key,
        w_value,
        w_outgate,
        w_lowrank,
        w_forget,
        b_forget,
        g_head,
        w_output,
        g_ffn,
        w_gate,
        w_up,
        w_down,
    ) = weights
    row_count = rows_in.shape[0]
    blocks = row_count // BLOCK
    key_dim = w_query.shape[1] // HEADS
    val_dim = w_value.shape[1] // HEADS
    key_shape = (blocks, BLOCK, HEADS, key_dim)
    val_shape = (blocks, BLOCK, HEADS, val_dim)
    flat_rows = rows_in.astype(jnp.float32)
    norm_one, pull_one = jax.vjp(scaled_rows, flat_rows, g_attn.astype(jnp.float32))
    xn_one = norm_one.astype(jnp.bfloat16)
    queries = matmul(xn_one, w_query)
    key_rows = matmul(xn_one, w_key)
    values = matmul(xn_one, w_value).astype(jnp.bfloat16)
    gate_out = matmul(xn_one, w_outgate)
    lowrank = matmul(xn_one, w_lowrank).astype(jnp.bfloat16)
    logits = matmul(lowrank, w_forget) + b_forget.astype(jnp.float32)
    forget, pull_forget = jax.vjp(forget_rate, logits)
    gate_vals, pull_gates = jax.vjp(
        block_gates,
        queries.reshape(key_shape),
        key_rows.reshape(key_shape),
        forget.reshape(key_shape),
    )
    q_gate = gate_vals[0].astype(jnp.bfloat16)
    k_back = gate_vals[1].astype(jnp.bfloat16)
    k_tail = gate_vals[2].astype(jnp.bfloat16)
    decays = gate_vals[3]
    val_blocks = values.reshape(val_shape)
    spot_ids = jnp.arange(BLOCK)
    causal = (spot_ids[:, None] >= spot_ids[None, :]).astype(jnp.float32)
    scores = jnp.einsum("cthd,cshd->chts", q_gate, k_back, preferred_element_type=jnp.float32)
    attn_probs = (scores * causal).astype(jnp.bfloat16)
    intra_out = jnp.einsum(
        "chts,cshe->cthe", attn_probs, val_blocks, preferred_element_type=jnp.float32
    )
    update = jnp.einsum("cthd,cthe->chde", k_tail, val_blocks, preferred_element_type=jnp.float32)

    per_seq = blocks // seq_count
    seq_blocks = (seq_count, per_seq) + update.shape[1:]
    upd_seq = update.reshape(seq_blocks)
    decay_seq = decays.reshape((seq_count, per_seq) + decays.shape[1:])
    carried = jnp.zeros_like(upd_seq[:, 0])
    before_list = []
    for idx in range(per_seq):
        before_list.append(carried)
        carried = decay_seq[:, idx][..., None] * carried + upd_seq[:, idx]
    before_seq = jnp.stack(before_list, axis=1)
    before_low = before_seq.reshape(update.shape).astype(jnp.bfloat16)
    inter_out = jnp.einsum(
        "cthd,chde->cthe", q_gate, before_low, preferred_element_type=jnp.float32
    )
    mixed_out = (intra_out + inter_out).reshape(row_count, HEADS, val_dim)
    gated_f, pull_head = jax.vjp(head_gate, mixed_out, gate_out, g_head.astype(jnp.float32))
    gated_out = gated_f.astype(jnp.bfloat16)
    resid_one = flat_rows + matmul(gated_out, w_output)
    norm_two, pull_two = jax.vjp(scaled_rows, resid_one, g_ffn.astype(jnp.float32))
    xn_two = norm_two.astype(jnp.bfloat16)
    pre_gate = matmul(xn_two, w_gate)
    pre_up = matmul(xn_two, w_up)
    hidden_f, pull_ffn = jax.vjp(swiglu_core, pre_gate, pre_up)
    hidden = hidden_f.astype(jnp.bfloat16)
    output = (resid_one + matmul(hidden, w_down)).astype(jnp.bfloat16)
    back_f = back_in.astype(jnp.float32)
    dw_down = rows_contract(hidden, back_in)
    d_hidden = right_transpose(back_in, w_down)
    d_pre_gate, d_pre_up = pull_ffn(d_hidden)
    d_gate_low = d_pre_gate.astype(jnp.bfloat16)
    d_up_low = d_pre_up.astype(jnp.bfloat16)
    dw_gate = rows_contract(xn_two, d_gate_low)
    dw_up = rows_contract(xn_two, d_up_low)
    d_norm_two = right_transpose(d_gate_low, w_gate) + right_transpose(d_up_low, w_up)
    d_resid_part, dg_ffn = pull_two(d_norm_two)
    d_resid = back_f + d_resid_part
    d_attn = d_resid.astype(jnp.bfloat16)
    dw_output = rows_contract(gated_out, d_attn)
    d_gated = right_transpose(d_attn, w_output)
    d_mixed_f, d_gate_out_f, dg_head = pull_head(d_gated)
    d_mixed = d_mixed_f.astype(jnp.bfloat16).reshape(val_shape)
    d_scores = jnp.einsum(
        "cthe,cshe->chts", d_mixed, val_blocks, preferred_element_type=jnp.float32
    )
    d_probs = (d_scores * causal).astype(jnp.bfloat16)
    d_q_gate = jnp.einsum(
        "chts,cshd->cthd", d_probs, k_back, preferred_element_type=jnp.float32
    ) + jnp.einsum("cthe,chde->cthd", d_mixed, before_low, preferred_element_type=jnp.float32)
    d_k_back = jnp.einsum("chts,cthd->cshd", d_probs, q_gate, preferred_element_type=jnp.float32)
    d_val_intra = jnp.einsum(
        "chts,cthe->cshe", attn_probs, d_mixed, preferred_element_type=jnp.float32
    )
    d_before = jnp.einsum("cthd,cthe->chde", q_gate, d_mixed, preferred_element_type=jnp.float32)

    d_before_seq = d_before.reshape(seq_blocks)
    d_after = jnp.zeros_like(upd_seq[:, 0])
    d_update_list = []
    d_decay_list = []
    for idx in reversed(range(per_seq)):
        d_update_list.append(d_after)
        d_decay_list.append(jnp.sum(d_after * before_seq[:, idx], axis=-1))
        d_after = d_before_seq[:, idx] + decay_seq[:, idx][..., None] * d_after
    d_update = jnp.stack(d_update_list[::-1], axis=1).reshape(update.shape)
    d_decays = jnp.stack(d_decay_list[::-1], axis=1).reshape(decays.shape)
    d_update_low = d_update.astype(jnp.bfloat16)
    d_k_tail = jnp.einsum(
        "cthe,chde->cthd", val_blocks, d_update_low, preferred_element_type=jnp.float32
    )
    d_values = (
        (
            d_val_intra
            + jnp.einsum(
                "cthd,chde->cthe", k_tail, d_update_low, preferred_element_type=jnp.float32
            )
        )
        .reshape(row_count, -1)
        .astype(jnp.bfloat16)
    )
    d_query_f, d_key_f, d_forget = pull_gates((d_q_gate, d_k_back, d_k_tail, d_decays))
    d_queries = d_query_f.reshape(row_count, -1).astype(jnp.bfloat16)
    d_keys = d_key_f.reshape(row_count, -1).astype(jnp.bfloat16)
    (d_logits,) = pull_forget(d_forget.reshape(row_count, -1))
    db_forget = jnp.sum(d_logits, axis=0)
    d_logit_low = d_logits.astype(jnp.bfloat16)
    dw_forget = rows_contract(lowrank, d_logit_low)
    d_lowrank = right_transpose(d_logit_low, w_forget).astype(jnp.bfloat16)
    d_gate_out = d_gate_out_f.astype(jnp.bfloat16)
    dw_query = rows_contract(xn_one, d_queries)
    dw_key = rows_contract(xn_one, d_keys)
    dw_value = rows_contract(xn_one, d_values)
    dw_outgate = rows_contract(xn_one, d_gate_out)
    dw_lowrank = rows_contract(xn_one, d_lowrank)
    d_norm_one = (
        right_transpose(d_queries, w_query)
        + right_transpose(d_keys, w_key)
        + right_transpose(d_values, w_value)
        + right_transpose(d_gate_out, w_outgate)
        + right_transpose(d_lowrank, w_lowrank)
    )
    d_flat, dg_attn = pull_one(d_norm_one)
    grad_rows = (d_resid + d_flat).astype(jnp.bfloat16)
    grads = (
        dg_attn,
        dw_query,
        dw_key,
        dw_value,
        dw_outgate,
        dw_lowrank,
        dw_forget,
        db_forget,
        dg_head,
        dw_output,
        dg_ffn,
        dw_gate,
        dw_up,
        dw_down,
    )
    return (output, grad_rows, grads)


def when(cond, do):
    if isinstance(cond, bool):
        if cond:
            do()
    else:
        pl.when(cond)(do)


def columns(ref, lo, hi):
    return ref[:, :, :, :, lo:hi].reshape(D, hi - lo)


def put_columns(ref, lo, hi, value):
    ref[:, :, :, :, lo:hi] = value.reshape(GRP, SQUARE, CORES, ROWS, hi - lo)


def flip(index, bit):
    return index + bit - 2 * bit * lax.rem(index // bit, 2)


def remote(src, dst, send_sem, recv_sem, device):
    return pltpu.make_async_remote_copy(
        src_ref=src,
        dst_ref=dst,
        send_sem=send_sem,
        recv_sem=recv_sem,
        device_id=device,
        device_id_type=MESH,
    )


def start_all(copies):
    for copy in copies:
        copy.start()


def recv_all(copies):
    for copy in copies:
        copy.wait_recv()


def sent_all(copies):
    for copy in copies:
        copy.wait_send()


class Place:
    def __init__(self):
        self.z = lax.axis_index("grp")
        self.s = lax.axis_index("shard")
        self.core = lax.rem(self.s, CORES)
        self.q = self.s // CORES
        self.qx = flip(self.q, 1)
        self.qy = flip(self.q, 2)
        self.qd = flip(self.qx, 2)
        self.z_peers = [lax.rem(self.z + step, GRP) for step in range(1, GRP)]
        self.z_from = [lax.rem(self.z + GRP - step, GRP) for step in range(1, GRP)]
        self.line_to = [(peer, self.s) for peer in self.z_peers]
        self.middle = (self.z == 1) | (self.z == 2)
        self.near = [self.z != GRP - 1, True, self.z != 0]
        self.pass_from = lax.rem(self.z + 2, GRP)
        self.pass_to = jnp.where(self.z == 1, 0, GRP - 1)
        self.pass_slot = jnp.where(self.z == 1, 0, 2)
        self.sib = (self.z, flip(self.s, 1))
        self.xn = (self.z, flip(self.s, CORES))
        self.yn = (self.z, flip(self.s, 2 * CORES))

    def greet(self):
        barrier = pltpu.get_barrier_semaphore()
        peers = self.line_to + [self.sib, self.xn, self.yn]
        for peer in peers:
            pl.semaphore_signal(barrier, inc=1, device_id=peer, device_id_type=MESH)
        return (barrier, len(peers))


class Gather:
    def __init__(self, place, parts, full, sems):
        self.p = place
        self.parts = parts
        self.full = full
        (
            self.ls,
            self.zs,
            self.zr,
            self.fs,
            self.xs,
            self.xr,
            self.ds,
            self.dr,
            self.ss,
            self.sr,
        ) = sems

    def cols(self, c):
        narrow = isinstance(c, int) and c == MIX_CHUNKS - 1
        return pl.ds(0, LAST_WIDE if narrow else WIDE)

    def mine(self, c):
        return self.parts.at[c // 16, c % 16 // SQUARE, c % SQUARE, :, self.cols(c)]

    def locals(self):
        p = self.p
        groups = [(g, pl.ds(g * SQUARE, SQUARE)) for g in range(16 // SQUARE)]
        copies = [
            pltpu.make_async_copy(
                self.parts.at[0, g], self.full.at[chunks, p.z, p.q, p.core], self.ls.at[g]
            )
            for g, chunks in groups
        ]
        last = pltpu.make_async_copy(
            self.parts.at[1, 0, 0], self.full.at[16, p.z, p.q, p.core], self.ls.at[4]
        )
        return copies + [last]

    def view(self, c, z, q):
        return self.full.at[c, z, q, self.p.core, :, self.cols(c)]

    def line(self, c):
        p = self.p
        there = self.view(c, p.z, p.q)
        return [
            remote(self.mine(c), there, self.zs.at[c, k], self.zr.at[c, k], p.line_to[k])
            for k in range(GRP - 1)
        ]

    def held(self, c, z):
        if isinstance(c, int) and c in SPREAD:
            return self.full.at[c, z, :, self.p.core]
        return self.view(c, z, self.p.q)

    def line_in(self, c, k):
        view = self.held(c, self.p.z_from[k])
        remote(view, view, self.zs.at[c, k], self.zr.at[c, k], self.p.line_to[k]).wait_recv()

    def passed(self, c):
        p = self.p
        view = self.held(c, p.pass_from)
        to = (p.pass_to, p.s)
        return remote(view, view, self.fs.at[c], self.zr.at[c, p.pass_slot], to)

    def near_all(self, copies, do):
        for copy, near in zip(copies, self.p.near):
            when(near, lambda copy=copy: do(copy))

    def pass_on(self, c):
        def middle():
            self.line_in(c, 1)
            self.passed(c).start()

        pl.when(self.p.middle)(middle)

    def line_end(self, c):
        self.line_in(c, 0)
        pl.when(jnp.logical_not(self.p.middle))(lambda: self.line_in(c, 1))
        self.line_in(c, 2)

    def line_sent(self, c):
        copies = self.spread(c) if isinstance(c, int) and c in SPREAD else self.line(c)
        self.near_all(copies, lambda copy: copy.wait_send())
        pl.when(self.p.middle)(lambda: self.passed(c).wait_send())

    def z_part(self, c):
        return self.p.z if isinstance(c, int) and c in SPREAD else pl.ds(0, GRP)

    def plane(self, c):
        p = self.p
        there = self.view(c, self.z_part(c), p.q)
        here = self.mine(c) if isinstance(c, int) and c in SPREAD else there
        return [
            remote(here, there, self.xs.at[c, k], self.xr.at[c, k], to)
            for k, to in enumerate((p.xn, p.yn))
        ]

    def plane_in(self, c):
        p = self.p
        return [
            remote(view, view, self.xs.at[c, k], self.xr.at[c, k], to)
            for k, (view, to) in enumerate(
                (
                    (self.view(c, self.z_part(c), p.qx), p.xn),
                    (self.view(c, self.z_part(c), p.qy), p.yn),
                )
            )
        ]

    def halves(self, c, q_low, q_high):
        if isinstance(c, int) and c in SPREAD:
            half = ROWS // 2
            return (
                self.full.at[c, self.p.z, q_low, self.p.core, pl.ds(0, half)],
                self.full.at[c, self.p.z, q_high, self.p.core, pl.ds(half, half)],
            )
        return (self.view(c, pl.ds(0, 2), q_low), self.view(c, pl.ds(2, 2), q_high))

    def corner(self, c):
        p = self.p
        low, high = self.halves(c, p.qx, p.qy)
        return [
            remote(low, low, self.ds.at[c, 0], self.dr.at[c, 0], p.yn),
            remote(high, high, self.ds.at[c, 1], self.dr.at[c, 1], p.xn),
        ]

    def corner_in(self, c):
        p = self.p
        low, high = self.halves(c, p.qd, p.qd)
        return [
            remote(low, low, self.ds.at[c, 0], self.dr.at[c, 0], p.yn),
            remote(high, high, self.ds.at[c, 1], self.dr.at[c, 1], p.xn),
        ]

    def spread(self, c):
        p = self.p
        own = self.full.at[c, p.z, :, p.core]
        return [
            remote(own, own, self.zs.at[c, k], self.zr.at[c, k], p.line_to[k])
            for k in range(GRP - 1)
        ]

    def other(self, c, core):
        view = self.full.at[c, :, :, core, :, self.cols(c)]
        return remote(view, view, self.ss.at[c], self.sr.at[c], self.p.sib)

    def other_in(self, c):
        self.other(c, 1 - self.p.core).wait_recv()

    def other_out(self, c):
        self.other(c, self.p.core).start()

    def line_out(self, c):
        self.near_all(self.line(c), lambda copy: copy.start())

    def line_stage(self, c):
        self.line_end(c)
        start_all(self.plane(c))

    def plane_stage(self, c):
        recv_all(self.plane_in(c))
        start_all(self.corner(c))

    def corner_stage(self, c):
        recv_all(self.corner_in(c))
        self.other_out(c)

    def spread_first(self, c):
        start_all(self.plane(c))

    def spread_out(self, c):
        recv_all(self.corner_in(c))
        self.near_all(self.spread(c), lambda copy: copy.start())

    def spread_last(self, c):
        self.line_end(c)
        self.other_out(c)

    def step(self, t):
        def some(c, do):
            when(0 <= c < LINES, lambda: do(c))

        some(t + AHEAD, self.line_out)
        some(t + 1, self.pass_on)
        some(t, self.line_stage)
        some(t - 1, self.plane_stage)
        some(t - 2, self.corner_stage)
        some(t - 3, self.other_in)
        if t == 1:
            for c in SPREAD:
                self.plane_stage(c)
        for c, at in zip(SPREAD, SPREAD_AT):
            if t == at:
                self.spread_out(c)

    def spread_pass(self, t):
        for c, at in zip(SPREAD, PASS_AT):
            when(t == at, lambda c=c: self.pass_on(c))

    def mid_step(self, t):
        when(t + AHEAD < LINES, lambda: self.line_out(t + AHEAD))
        when(t + 1 < LINES, lambda: self.pass_on(t + 1))
        self.line_stage(t)
        self.plane_stage(t - 1)
        self.corner_stage(t - 2)
        self.other_in(t - 3)
        self.spread_pass(t)

    def late_step(self, t):
        self.spread_pass(t)
        when(t == LINES, lambda: self.plane_stage(LINES - 1))
        when(t <= LINES + 1, lambda: self.corner_stage(t - 2))
        when(t <= LINES + 2, lambda: self.other_in(t - 3))
        when(t == LINES + 2, lambda: self.spread_last(SPREAD[0]))
        when(t == LINES + 3, lambda: self.other_in(SPREAD[0]))
        when(t == LINES + 3, lambda: self.spread_last(SPREAD[1]))
        when(t == LINES + 4, lambda: self.other_in(SPREAD[1]))

    def drain_parts(self):
        for c in range(LINES):
            self.line_sent(c)
        for c in SPREAD:
            sent_all(self.plane(c))

    def drain(self, c):
        if c in SPREAD:
            self.line_sent(c)
        else:
            sent_all(self.plane(c))
        sent_all(self.corner(c) + [self.other(c, self.p.core)])


class Reduce:
    def __init__(self, place, src, out, bufs, sems):
        self.p = place
        self.src = src
        self.out = out
        self.own, self.b1, self.b2, self.b3, self.b4, self.stage = bufs
        (
            self.ls,
            self.s1,
            self.r1,
            self.s2,
            self.r2,
            self.s3,
            self.r3,
            self.s4,
            self.r4,
            self.out_sem,
        ) = sems

    def slot(self, c):
        return c % SLOTS if isinstance(c, int) else lax.rem(c, SLOTS)

    def wide(self, c):
        return LAST_WIDE if isinstance(c, int) and c == NARROW else WIDE

    def local(self, c):
        k, n = self.slot(c), pl.ds(0, self.wide(c))
        return pltpu.make_async_copy(
            self.src.at[c, :, :, self.p.core, :, n], self.own.at[k, :, :, :, n], self.ls.at[k]
        )

    def other(self, c):
        k, n = self.slot(c), pl.ds(0, self.wide(c))
        return remote(
            self.src.at[c, :, :, 1 - self.p.core, :, n],
            self.b1.at[k, :, :, :, n],
            self.s1.at[k],
            self.r1.at[k],
            self.p.sib,
        )

    def corner(self, c):
        p, k, n = self.p, self.slot(c), pl.ds(0, self.wide(c))
        return [
            remote(
                self.own.at[k, pl.ds(2 * i, 2), p.qd, :, n],
                self.b2.at[k, i, :, :, n],
                self.s2.at[k, i],
                self.r2.at[k, i],
                to,
            )
            for i, to in enumerate((p.xn, p.yn))
        ]

    def plane(self, c):
        p, k, n = self.p, self.slot(c), pl.ds(0, self.wide(c))
        return [
            remote(
                self.own.at[k, :, q, :, n],
                self.b3.at[k, i, :, :, n],
                self.s3.at[k, i],
                self.r3.at[k, i],
                to,
            )
            for i, (q, to) in enumerate(((p.qx, p.xn), (p.qy, p.yn)))
        ]

    def line(self, c):
        p, k, n = self.p, self.slot(c), pl.ds(0, self.wide(c))
        return [
            remote(
                self.own.at[k, p.z_peers[i], p.q, :, n],
                self.b4.at[k, i, :, n],
                self.s4.at[k, i],
                self.r4.at[k, i],
                p.line_to[i],
            )
            for i in range(GRP - 1)
        ]

    def drain(self, c):
        sent_all([self.other(c)] + self.corner(c) + self.plane(c) + self.line(c))

    def enter(self, c):
        when(c >= SLOTS, lambda: self.drain(c - SLOTS))
        self.local(c).start()
        self.other(c).start()

    def add_other(self, c):
        p, k, n = self.p, self.slot(c), slice(0, self.wide(c))
        self.local(c).wait()
        self.other(c).wait_recv()
        for q in (p.qd, p.qx, p.qy, p.q):
            self.own[k, :, q, :, n] = self.own[k, :, q, :, n] + self.b1[k, :, q, :, n]
            if q is p.qd:
                start_all(self.corner(c))

    def add_corner(self, c):
        p, k, n = self.p, self.slot(c), slice(0, self.wide(c))
        recv_all(self.corner(c))
        for q, cut, i in ((p.qy, slice(0, 2), 0), (p.qx, slice(2, 4), 1)):
            self.own[k, cut, q, :, n] = self.own[k, cut, q, :, n] + self.b2[k, i, :, :, n]
        start_all(self.plane(c))

    def add_plane(self, c):
        p, k, n = self.p, self.slot(c), slice(0, self.wide(c))
        recv_all(self.plane(c))
        total = wide_type(self.own[k, :, p.q, :, n])
        total += wide_type(self.b3[k, 0, :, :, n])
        total += wide_type(self.b3[k, 1, :, :, n])
        self.own[k, :, p.q, :, n] = low_type(total)
        start_all(self.line(c))

    def finish(self, c):
        p, k, n = self.p, self.slot(c), slice(0, self.wide(c))
        recv_all(self.line(c))
        total = wide_type(self.own[k, p.z, p.q, :, n])
        for i in range(GRP - 1):
            total += wide_type(self.b4[k, i, :, n])
        when(c >= SLOTS, lambda: self.leave(c - SLOTS).wait())
        self.stage[k, :, n] = total
        self.leave(c).start()

    def leave(self, c):
        k, n = self.slot(c), pl.ds(0, self.wide(c))
        return pltpu.make_async_copy(
            self.stage.at[k, :, n], self.out.at[c, :, n], self.out_sem.at[k]
        )

    def step(self, t):
        def some(c, do):
            if isinstance(c, int):
                when(0 <= c < CHUNKS, lambda: do(c))
            else:
                when(c >= 0, lambda: do(c))

        some(t - 3, self.finish)
        some(t + 1, self.enter)
        some(t, self.add_other)
        some(t - 1, self.add_corner)
        some(t - 2, self.add_plane)


def reduce_scratch():
    def buf(*shape):
        return pltpu.VMEM((SLOTS,) + shape + (ROWS, WIDE), jnp.bfloat16)

    bufs = [buf(GRP, SQUARE), buf(GRP, SQUARE), buf(2, 2), buf(2, GRP), buf(GRP - 1)]
    bufs.append(pltpu.VMEM((SLOTS, ROWS, WIDE), jnp.float32))
    sems = [DMA((SLOTS,))] * 3 + [DMA((SLOTS, count)) for count in (2, 2, 2, 2, 3, 3)]
    return bufs + sems + [DMA((SLOTS,))]


def mm_nn(left_mat, right_mat):
    return jnp.dot(left_mat, right_mat, preferred_element_type=jnp.float32)


def mm_nt(left_mat, right_mat):
    return right_transpose(left_mat, right_mat)


def mm_tn(left_mat, right_mat):
    return rows_contract(left_mat, right_mat)


def low_type(value):
    return value.astype(jnp.bfloat16)


def wide_type(value):
    return value.astype(jnp.float32)


def exact_sum(zero_one, value):
    high = low_type(value)
    rest = value - wide_type(high)
    mid = low_type(rest)
    last = low_type(rest - wide_type(mid))
    return mm_nn(zero_one, high) + mm_nn(zero_one, mid) + mm_nn(zero_one, last)


def iota(shape, dim):
    return lax.broadcasted_iota(jnp.int32, shape, dim)


def place_matrix(keep, columns):
    row = iota((D, columns), 0)
    col = iota((D, columns), 1)
    hit = (row // ROWS == col // keep) & (row % ROWS == col % keep)
    return low_type(jnp.where(hit, 1.0, 0.0))


def unit_matrix(size):
    return low_type(jnp.where(iota((size, size), 0) == iota((size, size), 1), 1.0, 0.0))


def row_rsqrt(value, eps):
    return lax.rsqrt(jnp.mean(value * value, axis=-1, keepdims=True) + eps)


class Layer:
    def __init__(self, refs):
        self.__dict__.update(refs)

    def rows(self, i):
        return pl.ds(pl.multiple_of(i * SEQ, SEQ), SEQ)

    def mask(self, lengths, dealing, first_seq):
        held = wide_type(lengths[...])
        for i in range(SEQS):
            r = pl.ds(i * SEQ, SEQ)
            match = dealing[...] == first_seq + i
            length = jnp.sum(jnp.where(match, held, 0.0), axis=1, keepdims=True)
            live = wide_type(iota((SEQ, 1), 0)) < length
            self.x[r, :] = jnp.where(live, self.x[r, :], jnp.zeros((), jnp.bfloat16))
            self.cot[r, :] = jnp.where(live, self.cot[r, :], jnp.zeros((), jnp.bfloat16))

    def prepare(self):
        misc = columns(self.wm.at[0], 0, MISC)
        turned = mm_nt(unit_matrix(MISC), misc)
        self.gains[0:1, :] = turned[RANK : RANK + 1]
        self.gains[1:2, :] = turned[RANK + 1 : RANK + 2]
        picked = mm_tn(misc, place_matrix(KEY_WIDE // DEVICES, KEY_WIDE))
        self.wf[...] = jnp.zeros_like(self.wf)
        self.wf[0:RANK, :] = low_type(picked[32 : 32 + RANK])
        self.bias[0:1, :] = picked[48:49]
        heads = mm_tn(misc, place_matrix(HEAD_VAL // DEVICES, HEAD_VAL))
        self.ghead[0:1, :] = heads[18:19]
        for i in range(SEQS):
            r = pl.ds(i * SEQ, SEQ)
            value = wide_type(self.x[r, :])
            self.xn1[r, :] = low_type(value * row_rsqrt(value, EPS) * self.gains[0:1, :])

    def project(self, c):
        lo, hi = c * WIDE, min((c + 1) * WIDE, PROJ)
        for r in HALVES:
            value = mm_nn(self.xn1[r, :], columns(self.wm.at[c], 0, hi - lo))
            for ref, at, first, last in self.pieces(lo, hi):
                ref[r, at : at + last - first] = value[:, first:last].astype(ref.dtype)

    def pieces(self, lo, hi):
        found = []
        for ref, start, end, at in (
            (self.proj, 0, V_AT, 0),
            (self.pval, V_AT, G_AT, 0),
            (self.proj, G_AT, PROJ, GATE_AT),
        ):
            a, b = max(lo, start), min(hi, end)
            if a < b:
                found.append((ref, at + a - start, a - lo, b - lo))
        return found

    def gates(self, r):
        lane = iota((SEQ, MISC), 1)
        lowrank = low_type(jnp.where(lane < RANK, self.proj[r, 0:MISC], 0.0))
        logits = mm_nn(lowrank, self.wf[...]) + self.bias[0:1, :]
        forget = (jnp.minimum(logits, 0.0) - jnp.log1p(jnp.exp(-jnp.abs(logits)))) * (1.0 / 16.0)
        row, col = iota((SEQ, SEQ), 0), iota((SEQ, SEQ), 1)
        same = row // BLOCK == col // BLOCK
        causal = same & (col <= row)
        running = exact_sum(low_type(jnp.where(causal, 1.0, 0.0)), forget)
        tails = [running[b * BLOCK + BLOCK - 1 : (b + 1) * BLOCK] for b in range(BLOCKS)]
        tail = jnp.concatenate(
            [jnp.broadcast_to(one, (BLOCK, KEY_WIDE)) for one in tails], axis=0
        )
        return (lowrank, logits, running, tails, tail, same, causal)

    def attend(self, i):
        r = self.rows(i)
        _, _, running, tails, tail, _, causal = self.gates(r)
        grow = jnp.exp(running)
        fade = jnp.exp(-running)
        late = jnp.exp(tail - running)
        for h in range(HEADS):
            k = slice(h * HEAD_KEY, (h + 1) * HEAD_KEY)
            queries = self.proj[r, Q_AT + h * HEAD_KEY : Q_AT + (h + 1) * HEAD_KEY]
            key_rows = self.proj[r, K_AT + h * HEAD_KEY : K_AT + (h + 1) * HEAD_KEY]
            values = self.pval[r, h * HEAD_VAL : (h + 1) * HEAD_VAL]
            q_gate = low_type(queries * SCALE * grow[:, k])
            k_back = low_type(key_rows * fade[:, k])
            k_tail = low_type(key_rows * late[:, k])
            probs = low_type(jnp.where(causal, mm_nt(q_gate, k_back), 0.0))
            mixed = mm_nn(probs, values)
            state = mm_tn(values[0:BLOCK], k_tail[0:BLOCK])
            parts = [mixed[0:BLOCK]]
            for b in range(1, BLOCKS):
                cut = slice(b * BLOCK, (b + 1) * BLOCK)
                parts.append(mixed[cut] + mm_nt(q_gate[cut], low_type(state)))
                if b + 1 < BLOCKS:
                    state = state * jnp.exp(tails[b][:, k]) + mm_tn(values[cut], k_tail[cut])
            self.mixed[r, h * HEAD_VAL : (h + 1) * HEAD_VAL] = jnp.concatenate(parts, axis=0)

    def gate_rows(self, i):
        r = self.rows(i)
        for h in range(HEADS):
            v = slice(h * HEAD_VAL, (h + 1) * HEAD_VAL)
            mixed = self.mixed[r, v]
            gate = self.proj[r, GATE_AT + h * HEAD_VAL : GATE_AT + (h + 1) * HEAD_VAL]
            normed = mixed * row_rsqrt(mixed, HEAD_EPS) * self.ghead[0:1, :]
            self.gated[r, v] = low_type(normed * (gate * jax.nn.sigmoid(gate)))

    def mix_out(self):
        cut = WIDE - O_AT % WIDE
        first = O_AT // WIDE
        lo = O_AT % WIDE
        for i in range(SEQS):
            r = pl.ds(i * SEQ, SEQ)
            self.out_sum[r, 0:cut] = wide_type(self.x[r, 0:cut]) + mm_nn(
                self.gated[r, :], columns(self.wm.at[first], lo, WIDE)
            )
            self.out_sum[r, cut:D] = wide_type(self.x[r, cut:D]) + mm_nn(
                self.gated[r, :], columns(self.wl, 0, D - cut)
            )

    def second_norm(self):
        for i in range(SEQS):
            r = pl.ds(i * SEQ, SEQ)
            value = self.out_sum[r, :]
            self.xn2[r, :] = low_type(value * row_rsqrt(value, EPS) * self.gains[1:2, :])
        self.dx_sum[...] = jnp.zeros_like(self.dx_sum)
        self.turn(self.xn2, self.turn_a)

    def turn(self, src, dst):
        for i in range(LIVE // 256):
            dst[:, i * 256 : (i + 1) * 256] = src[i * 256 : (i + 1) * 256, :].T

    def ffn(self, w_ref, g_ref):
        c = FF_CUT
        for r in HALVES:
            pre = mm_nn(self.xn2[r, :], columns(w_ref, 0, 2 * c))
            d_hidden = mm_nn(self.cot[r, :], columns(w_ref, 2 * c, 3 * c))
            pre_gate, pre_up = pre[:, 0:c], pre[:, c : 2 * c]
            sig = jax.nn.sigmoid(pre_gate)
            silu = pre_gate * sig
            self.hid[r, :] = low_type(silu * pre_up)
            self.dpre[r, 0:c] = low_type(d_hidden * pre_up * sig * (1.0 + pre_gate * (1.0 - sig)))
            self.dpre[r, c : 2 * c] = low_type(d_hidden * silu)
            self.out_sum[r, :] += mm_nt(self.hid[r, :], columns(w_ref, 2 * c, 3 * c))
            self.dx_sum[r, :] += mm_nt(self.dpre[r, :], columns(w_ref, 0, 2 * c))
        put_columns(g_ref, 0, 2 * c, low_type(mm_nn(self.turn_a[...], self.dpre[...])))
        put_columns(g_ref, 2 * c, 3 * c, low_type(mm_nn(self.turn_b[...], self.hid[...])))

    def norm_back(self, value, d_out, gain, eps):
        rs = row_rsqrt(value, eps)
        scaled = gain * d_out
        mean = jnp.mean(value * scaled, axis=-1, keepdims=True)
        d_gain = jnp.sum(d_out * value * rs, axis=0, keepdims=True)
        return (rs * scaled - value * (rs * rs * rs * mean), d_gain)

    def after_ffn(self):
        cut = WIDE - O_AT % WIDE
        first = O_AT // WIDE
        lo = O_AT % WIDE
        total = jnp.zeros((1, D), jnp.float32)
        for i in range(SEQS):
            r = pl.ds(i * SEQ, SEQ)
            resid = wide_type(self.x[r, :]) + jnp.concatenate(
                [
                    mm_nn(self.gated[r, :], columns(self.wm.at[first], lo, WIDE)),
                    mm_nn(self.gated[r, :], columns(self.wl, 0, D - cut)),
                ],
                axis=1,
            )
            d_val, d_gain = self.norm_back(
                resid, self.dx_sum[r, :], self.gains[1:2, :], EPS
            )
            total += d_gain
            d_resid = wide_type(self.cot[r, :]) + d_val
            self.dx_sum[r, :] = d_resid
            self.xn2[r, :] = low_type(d_resid)
        self.dgains[1:2, :] = total
        self.turn(self.gated, self.turn_a)
        self.turn(self.xn1, self.turn_b)
        self.gated[...] = low_type(self.out_sum[...])
        self.dwf[...] = jnp.zeros_like(self.dwf)
        self.dbias[...] = jnp.zeros_like(self.dbias)
        self.dghead[...] = jnp.zeros_like(self.dghead)

    def retreat(self, i):
        r = self.rows(i)
        cut = WIDE - O_AT % WIDE
        first = O_AT // WIDE
        lo = O_AT % WIDE
        d_attn = self.xn2[r, :]
        d_gated = mm_nt(d_attn[:, 0:cut], columns(self.wm.at[first], lo, WIDE))
        d_gated += mm_nt(d_attn[:, cut:D], columns(self.wl, 0, D - cut))
        lowrank, logits, running, tails, tail, same, causal = self.gates(r)
        grow = jnp.exp(running)
        fade = jnp.exp(-running)
        late = jnp.exp(tail - running)
        d_forget_parts = []
        tail_parts = []
        d_ghead = jnp.zeros((1, HEAD_VAL), jnp.float32)
        for h in range(HEADS):
            k = slice(h * HEAD_KEY, (h + 1) * HEAD_KEY)
            v = slice(h * HEAD_VAL, (h + 1) * HEAD_VAL)
            q_cols = slice(Q_AT + h * HEAD_KEY, Q_AT + (h + 1) * HEAD_KEY)
            k_cols = slice(K_AT + h * HEAD_KEY, K_AT + (h + 1) * HEAD_KEY)
            g_cols = slice(GATE_AT + h * HEAD_VAL, GATE_AT + (h + 1) * HEAD_VAL)
            mixed = self.mixed[r, v]
            gate = self.proj[r, g_cols]
            sig = jax.nn.sigmoid(gate)
            act = gate * sig
            rs = row_rsqrt(mixed, HEAD_EPS)
            unit = mixed * rs
            gain = self.ghead[0:1, :]
            d_out = d_gated[:, v]
            d_normed = d_out * act
            d_gate = d_out * (unit * gain) * sig * (1.0 + gate * (1.0 - sig))
            self.proj[r, g_cols] = wide_type(low_type(d_gate))
            d_ghead += jnp.sum(d_normed * unit, axis=0, keepdims=True)
            scaled = gain * d_normed
            mean = jnp.mean(mixed * scaled, axis=-1, keepdims=True)
            d_mixed = low_type(rs * scaled - mixed * (rs * rs * rs * mean))

            q_full = self.proj[r, q_cols] * SCALE * grow[:, k]
            key_rows = self.proj[r, k_cols]
            kb_full = key_rows * fade[:, k]
            kt_full = key_rows * late[:, k]
            values = self.pval[r, v]
            q_gate, k_back, k_tail = low_type(q_full), low_type(kb_full), low_type(kt_full)
            probs = low_type(jnp.where(causal, mm_nt(q_gate, k_back), 0.0))
            d_probs = low_type(jnp.where(causal, mm_nt(d_mixed, values), 0.0))
            d_q = mm_nn(d_probs, k_back)
            d_kb = mm_tn(d_probs, q_gate)
            d_v = mm_tn(probs, d_mixed)
            cuts = [slice(b * BLOCK, (b + 1) * BLOCK) for b in range(BLOCKS)]
            before = [None, mm_tn(values[cuts[0]], k_tail[cuts[0]])]
            decay = [jnp.exp(tails[b][:, k]) for b in range(BLOCKS)]
            for b in range(2, BLOCKS):
                before.append(
                    before[b - 1] * decay[b - 1] + mm_tn(values[cuts[b - 1]], k_tail[cuts[b - 1]])
                )
            after = [None] * BLOCKS
            for b in range(BLOCKS - 1, 0, -1):
                d_before = mm_tn(d_mixed[cuts[b]], q_gate[cuts[b]])
                after[b - 1] = d_before if after[b] is None else d_before + decay[b] * after[b]
            q_parts, t_parts, v_parts, e_parts = [], [], [], []
            for b in range(BLOCKS):
                cut_b = cuts[b]
                part = d_q[cut_b]
                if b > 0:
                    part = part + mm_nn(d_mixed[cut_b], low_type(before[b]))
                q_parts.append(part)
                if after[b] is None:
                    t_parts.append(jnp.zeros((BLOCK, HEAD_KEY), jnp.float32))
                    v_parts.append(d_v[cut_b])
                    e_parts.append(jnp.zeros((1, HEAD_KEY), jnp.float32))
                    continue
                after_low = low_type(after[b])
                d_kt = mm_nn(values[cut_b], after_low)
                t_parts.append(d_kt)
                v_parts.append(d_v[cut_b] + mm_nt(k_tail[cut_b], after_low))
                extra = jnp.sum(d_kt * kt_full[cut_b], axis=0, keepdims=True)
                if b > 0:
                    extra += jnp.sum(after[b] * before[b], axis=0, keepdims=True) * decay[b]
                e_parts.append(extra)
            d_q = jnp.concatenate(q_parts, axis=0)
            d_kt = jnp.concatenate(t_parts, axis=0)
            d_v = jnp.concatenate(v_parts, axis=0)
            self.pval[r, v] = low_type(d_v)
            self.proj[r, q_cols] = wide_type(low_type(d_q * SCALE * grow[:, k]))
            self.proj[r, k_cols] = wide_type(low_type(d_kb * fade[:, k] + d_kt * late[:, k]))
            d_forget_parts.append(d_q * q_full - d_kb * kb_full - d_kt * kt_full)
            tail_parts.append(
                jnp.concatenate(
                    [jnp.broadcast_to(one, (BLOCK, HEAD_KEY)) for one in e_parts], axis=0
                )
            )
        self.dghead[0:1, :] += d_ghead
        d_running = jnp.concatenate(d_forget_parts, axis=1)
        row, col = iota((SEQ, SEQ), 0), iota((SEQ, SEQ), 1)
        later = low_type(jnp.where(same & (col >= row), 1.0, 0.0))
        d_forget = exact_sum(later, d_running) + jnp.concatenate(tail_parts, axis=1)
        d_logits = d_forget * jax.nn.sigmoid(-logits) * (1.0 / 16.0)
        self.dbias[0:1, :] += jnp.sum(d_logits, axis=0, keepdims=True)
        d_logit_low = low_type(d_logits)
        self.dwf[...] += mm_tn(lowrank, d_logit_low)
        self.proj[r, 0:MISC] = wide_type(low_type(mm_nt(d_logit_low, self.wf[...])))

    def d_proj(self, c, rows=slice(None)):
        lo, hi = c * WIDE, min((c + 1) * WIDE, PROJ)
        parts = [
            low_type(ref[rows, at : at + last - first])
            for ref, at, first, last in self.pieces(lo, hi)
        ]
        return parts[0] if len(parts) == 1 else jnp.concatenate(parts, axis=1)

    def first_norm_back(self):
        for c in range(-(-PROJ // WIDE)):
            for r in HALVES:
                d_proj = self.d_proj(c, r)
                part = mm_nt(d_proj, columns(self.wm.at[c], 0, d_proj.shape[1]))
                self.out_sum[r, :] = part if c == 0 else self.out_sum[r, :] + part
        total = jnp.zeros((1, D), jnp.float32)
        for i in range(SEQS):
            r = pl.ds(i * SEQ, SEQ)
            d_val, d_gain = self.norm_back(
                wide_type(self.x[r, :]), self.out_sum[r, :], self.gains[0:1, :], EPS
            )
            total += d_gain
            self.xn1[r, :] = low_type(self.dx_sum[r, :] + d_val)
        self.dgains[0:1, :] = total

    def mixer_grad(self, c, g_ref):
        first = O_AT // WIDE
        lo = O_AT % WIDE
        cut = WIDE - lo
        if c == first + 1:
            put_columns(g_ref, 0, D - cut, low_type(mm_nn(self.turn_a[...], self.xn2[:, cut:D])))
            return
        d_proj = self.d_proj(c)
        grad = mm_nn(self.turn_b[...], d_proj)
        if c == first:
            put_columns(g_ref, lo, WIDE, low_type(mm_nn(self.turn_a[...], self.xn2[:, 0:cut])))
            put_columns(g_ref, 0, lo, low_type(grad))
            return
        if c > 0:
            put_columns(g_ref, 0, WIDE, low_type(grad))
            return
        zero = jnp.zeros
        gains = jnp.concatenate(
            [zero((RANK, D), jnp.float32), self.dgains[...], zero((MISC - RANK - 8, D), jnp.float32)],
            axis=0,
        )
        small = mm_tn(low_type(gains), unit_matrix(MISC))
        keyed = jnp.concatenate(
            [
                zero((32, KEY_WIDE), jnp.float32),
                self.dwf[0:RANK, :],
                self.dbias[...],
                zero((MISC - 56, KEY_WIDE), jnp.float32),
            ],
            axis=0,
        )
        small += mm_nt(place_matrix(KEY_WIDE // DEVICES, KEY_WIDE), low_type(keyed))
        lane = iota((MISC, HEAD_VAL), 0)
        headed = jnp.where(lane == 18, jnp.broadcast_to(self.dghead[0:1, :], (MISC, HEAD_VAL)), 0.0)
        small += mm_nt(place_matrix(HEAD_VAL // DEVICES, HEAD_VAL), low_type(headed))
        put_columns(g_ref, 0, MISC, low_type(grad[:, 0:MISC] + small))
        put_columns(g_ref, MISC, WIDE, low_type(grad[:, MISC:WIDE]))


LAYER_SCRATCH = (
    ("small", (MISC, ROWS), jnp.float32),
    ("x", (LIVE, D), jnp.bfloat16),
    ("cot", (LIVE, D), jnp.bfloat16),
    ("xn1", (LIVE, D), jnp.bfloat16),
    ("proj", (LIVE, GATE_AT + VAL_WIDE), jnp.float32),
    ("pval", (LIVE, VAL_WIDE), jnp.bfloat16),
    ("wm", (MIX_CHUNKS - 1, GRP, SQUARE, CORES, ROWS, WIDE), jnp.bfloat16),
    ("wl", (GRP, SQUARE, CORES, ROWS, LAST_WIDE), jnp.bfloat16),
    ("gains", (8, D), jnp.float32),
    ("wf", (MISC, KEY_WIDE), jnp.bfloat16),
    ("bias", (8, KEY_WIDE), jnp.float32),
    ("ghead", (8, HEAD_VAL), jnp.float32),
    ("mixed", (LIVE, D), jnp.float32),
    ("gated", (LIVE, D), jnp.bfloat16),
    ("xn2", (LIVE, D), jnp.bfloat16),
    ("out_sum", (LIVE, D), jnp.float32),
    ("dx_sum", (LIVE, D), jnp.float32),
    ("turn_a", (D, LIVE), jnp.bfloat16),
    ("turn_b", (D, LIVE), jnp.bfloat16),
    ("hid", (LIVE, FF_CUT), jnp.bfloat16),
    ("dpre", (LIVE, 2 * FF_CUT), jnp.bfloat16),
    ("dgains", (8, D), jnp.float32),
    ("dwf", (MISC, KEY_WIDE), jnp.float32),
    ("dbias", (8, KEY_WIDE), jnp.float32),
    ("dghead", (8, HEAD_VAL), jnp.float32),
    ("wb", (2, GRP, SQUARE, CORES, ROWS, WIDE), jnp.bfloat16),
    ("gb", (2, GRP, SQUARE, CORES, ROWS, WIDE), jnp.bfloat16),
)


def fill_parts(parts, small, held):
    lowrank_t, g_attn, g_ffn, g_head, w_forget, b_forget = parts[:6]
    mats = parts[6:]
    small[...] = jnp.zeros_like(small)
    small[0:RANK, :] = wide_type(lowrank_t[...])
    small[RANK : RANK + 1, :] = wide_type(g_attn[...])
    small[RANK + 1 : RANK + 2, :] = wide_type(g_ffn[...])
    small[18:19, 0 : HEAD_VAL // DEVICES] = wide_type(g_head[...])
    small[32 : 32 + RANK, 0 : KEY_WIDE // DEVICES] = wide_type(w_forget[...])
    small[48:49, 0 : KEY_WIDE // DEVICES] = wide_type(b_forget[...])
    held[0, 0, 0, :, 0:MISC] = low_type(mm_tn(low_type(small[...]), unit_matrix(MISC)))
    at = MISC
    for ref in mats[:5]:
        end = at + ref.shape[1]
        for c in range(MIX_CHUNKS):
            lo, hi = max(at, c * WIDE), min(end, (c + 1) * WIDE)
            if lo < hi:
                held[0, c // SQUARE, c % SQUARE, :, lo - c * WIDE : hi - c * WIDE] = ref[
                    :, lo - at : hi - at
                ]
        at = end
    c = MIX_CHUNKS - 1
    held[0, c // SQUARE, c % SQUARE, :, LAST_WIDE:WIDE] = jnp.zeros(
        (ROWS, WIDE - LAST_WIDE), jnp.bfloat16
    )
    for f in range(FF_CHUNKS):
        c = MIX_CHUNKS + f
        for i, ref in enumerate(mats[5:]):
            held[c // 16, c % 16 // SQUARE, c % SQUARE, :, i * FF_CUT : (i + 1) * FF_CUT] = ref[
                :, f * FF_CUT : (f + 1) * FF_CUT
            ]


def layer_kernel(*refs):
    parts, refs = refs[:14], refs[14:]
    (x_in, cot_in, lengths, dealing), refs = refs[:4], refs[4:]
    (out, grad, red, full, grads), scratch = refs[:5], refs[5:]
    count = len(LAYER_SCRATCH)
    refs = {name: ref for (name, _, _), ref in zip(LAYER_SCRATCH, scratch[:count])}
    scratch = scratch[count:]
    g_sems, scratch = scratch[:10], scratch[10:]
    load_sem, store_sem, out_sem = scratch[:3]
    bufs, r_sems = scratch[3:9], scratch[9:]

    place = Place()
    barrier, greeted = place.greet()
    gather = Gather(place, bufs[0], full, g_sems)
    red_op = Reduce(place, grads, red, bufs, r_sems)
    work = Layer(refs)
    x_copy = pltpu.make_async_copy(x_in, work.x, out_sem.at[0])
    cot_copy = pltpu.make_async_copy(cot_in, work.cot, out_sem.at[1])

    def load(c, ref, k):
        return pltpu.make_async_copy(full.at[c], ref, load_sem.at[k])

    def load_ffn(f):
        k = f % 2 if isinstance(f, int) else lax.rem(f, 2)
        return load(MIX_CHUNKS + f, work.wb.at[k], k)

    def load_mixer(c):
        if c == MIX_CHUNKS - 1:
            half = pl.ds(0, LAST_WIDE)
            return pltpu.make_async_copy(
                full.at[c, :, :, :, :, half], work.wl, load_sem.at[0]
            )
        return load(c, work.wm.at[c], 0)

    def store(o, k):
        if isinstance(o, int) and o == NARROW:
            half = pl.ds(0, LAST_WIDE)
            return pltpu.make_async_copy(
                work.gb.at[k, :, :, :, :, half], grads.at[o, :, :, :, :, half], store_sem.at[k]
            )
        return pltpu.make_async_copy(work.gb.at[k], grads.at[o], store_sem.at[k])

    def fetch_mixer(c):
        copy = load_mixer(c)
        copy.start()
        copy.wait()

    fill_parts(parts, work.small, bufs[0])
    own_copies = gather.locals()
    start_all(own_copies)
    x_copy.start()
    cot_copy.start()
    work.dgains[...] = jnp.zeros_like(work.dgains)
    pl.semaphore_wait(barrier, greeted)
    for c in SPREAD:
        gather.spread_first(c)
    for c in range(AHEAD):
        gather.line_out(c)
    gather.pass_on(0)
    for copy in own_copies:
        copy.wait()
    gather.step(0)
    x_copy.wait()
    cot_copy.wait()
    first_seq = (place.z * SHARD + place.s) * SEQS
    work.mask(lengths, dealing, first_seq)
    work.turn(work.cot, work.turn_b)
    for t in range(1, 4):
        gather.step(t)
    fetch_mixer(0)
    work.prepare()
    work.project(0)
    for c in (1, 2, 3):
        gather.step(3 + c)
        fetch_mixer(c)
        work.project(c)
    work.attend(0)
    work.attend(1)
    gather.step(7)
    fetch_mixer(4)
    work.project(4)
    work.attend(2)
    work.attend(3)
    gather.step(8)
    fetch_mixer(5)
    for i in range(SEQS):
        work.gate_rows(i)
    work.mix_out()
    gather.step(9)
    load_ffn(0).start()
    work.second_norm()

    def ffn_step(f, reduce_too):
        k = lax.rem(f, 2)
        if reduce_too:
            gather.late_step(10 + f)
        else:
            gather.mid_step(10 + f)
        load_ffn(f).wait()
        when(f + 1 < FF_CHUNKS, lambda: load_ffn(f + 1).start())
        when(f >= 2, lambda: store(f - 2, k).wait())
        work.ffn(work.wb.at[k], work.gb.at[k])
        store(f, k).start()
        if reduce_too:
            red_op.step(f - RED_FROM)
        return 0

    def ffn_first(f, carry):
        return ffn_step(f, False)

    def ffn_last(f, carry):
        return ffn_step(f, True)

    lax.fori_loop(0, RED_FROM, ffn_first, 0)
    gather.drain_parts()
    red_op.enter(0)
    lax.fori_loop(RED_FROM, FF_CHUNKS, ffn_last, 0)
    for f in (FF_CHUNKS - 2, FF_CHUNKS - 1):
        store(f, f % 2).wait()
    steps = list(range(FF_CHUNKS - RED_FROM, CHUNKS + 3))

    def reduce_step(ready):
        if steps and steps[0] + 1 < ready:
            red_op.step(steps.pop(0))

    def hand_over(n):
        work.mixer_grad(MIX_ORDER[n], work.gb.at[n % 2])
        copy = store(FF_CHUNKS + n, n % 2)
        copy.start()
        copy.wait()
        reduce_step(FF_CHUNKS + n + 1)

    work.after_ffn()
    out_copy = pltpu.make_async_copy(work.gated, out, out_sem.at[0])
    out_copy.start()
    reduce_step(FF_CHUNKS)
    hand_over(0)
    for i in range(SEQS):
        work.retreat(i)
        reduce_step(FF_CHUNKS + 1)
    for n in range(1, MIX_CHUNKS - 1):
        hand_over(n)
        reduce_step(FF_CHUNKS + n + 1)
    work.first_norm_back()
    grad_copy = pltpu.make_async_copy(work.xn1, grad, out_sem.at[1])
    grad_copy.start()
    reduce_step(CHUNKS - 1)
    hand_over(MIX_CHUNKS - 1)
    while steps:
        red_op.step(steps.pop(0))
    out_copy.wait()
    grad_copy.wait()
    for c in range(CHUNKS):
        gather.drain(c)
    for c in range(CHUNKS - SLOTS, CHUNKS):
        red_op.drain(c)
        red_op.leave(c).wait()


def layer_call(parts, x, cot, lengths, dealing):
    any_spec = pl.BlockSpec(memory_space=pl.ANY)
    vmem = pl.BlockSpec(memory_space=pltpu.VMEM)
    chunk = (CHUNKS, GRP, SQUARE, CORES, ROWS, WIDE)
    rows = jax.ShapeDtypeStruct((LIVE, D), jnp.bfloat16)
    scratch = [pltpu.VMEM(shape, kind) for _, shape, kind in LAYER_SCRATCH]
    scratch += [DMA((5,))] + [DMA((CHUNKS, 3))] * 2 + [DMA((CHUNKS,))] + [DMA((CHUNKS, 2))] * 4 + [DMA((CHUNKS,))] * 2
    scratch += [DMA((2,)), DMA((2,)), DMA((2,))]
    scratch += reduce_scratch()
    result = pl.pallas_call(
        layer_kernel,
        out_shape=(
            rows,
            rows,
            jax.ShapeDtypeStruct((CHUNKS, ROWS, WIDE), jnp.float32),
            jax.ShapeDtypeStruct(chunk, jnp.bfloat16),
            jax.ShapeDtypeStruct(chunk, jnp.bfloat16),
        ),
        in_specs=[vmem] * 14 + [any_spec] * 2 + [vmem] * 2,
        out_specs=(any_spec,) * 5,
        scratch_shapes=scratch,
        compiler_params=pltpu.CompilerParams(
            collective_id=0, has_side_effects=True, vmem_limit_bytes=VMEM_LIMIT
        ),
    )(*parts, x, cot, lengths, dealing)
    return result[:3]


def chunk_place(c):
    return FF_CHUNKS + MIX_ORDER.index(c)


def finish_kernel(red, out_in, grad_in, *outs):
    outs[0][...] = out_in[...]
    outs[1][...] = grad_in[...]
    (
        g_attn,
        w_query,
        w_key,
        w_value,
        w_outgate,
        w_lowrank,
        w_forget,
        b_forget,
        g_head,
        w_output,
        g_ffn,
        w_gate,
        w_up,
        w_down,
    ) = outs[2:]
    misc = red[chunk_place(0), :, 0:MISC]
    turned = misc.T
    w_lowrank[...] = turned[0:RANK]
    g_attn[...] = turned[RANK : RANK + 1]
    g_ffn[...] = turned[RANK + 1 : RANK + 2]
    g_head[...] = turned[18:19, 0 : HEAD_VAL // DEVICES]
    w_forget[...] = turned[32 : 32 + RANK, 0 : KEY_WIDE // DEVICES]
    b_forget[...] = turned[48:49, 0 : KEY_WIDE // DEVICES]
    at = MISC
    for ref in (w_query, w_key, w_value, w_outgate, w_output):
        end = at + ref.shape[1]
        for c in range(MIX_CHUNKS):
            lo, hi = max(at, c * WIDE), min(end, (c + 1) * WIDE)
            if lo < hi:
                ref[:, lo - at : hi - at] = red[chunk_place(c), :, lo - c * WIDE : hi - c * WIDE]
        at = end
    for f in range(FF_CHUNKS):
        cut = slice(f * FF_CUT, (f + 1) * FF_CUT)
        w_gate[:, cut] = red[f, :, 0:FF_CUT]
        w_up[:, cut] = red[f, :, FF_CUT : 2 * FF_CUT]
        w_down[:, cut] = red[f, :, 2 * FF_CUT : 3 * FF_CUT]


def finish_call(red, out_rows, grad_rows, shapes):
    vmem = pl.BlockSpec(memory_space=pltpu.VMEM)
    rows = jax.ShapeDtypeStruct(out_rows.shape, out_rows.dtype)
    return pl.pallas_call(
        finish_kernel,
        out_shape=(rows, rows) + tuple(jax.ShapeDtypeStruct(one, jnp.float32) for one in shapes),
        in_specs=[vmem] * 3,
        out_specs=(vmem,) * (2 + len(shapes)),
        compiler_params=pltpu.CompilerParams(vmem_limit_bytes=VMEM_LIMIT),
    )(red, out_rows, grad_rows)


def plain_shards(
    inputs,
    cotangent,
    lengths,
    dealing,
    g_attn,
    w_query,
    w_key,
    w_value,
    w_outgate,
    w_lowrank,
    w_forget,
    b_forget,
    g_head,
    w_output,
    g_ffn,
    w_gate,
    w_up,
    w_down,
):
    axes = ("grp", "shard")
    shard_count = lax.axis_size("shard")
    self_index = lax.axis_index("grp") * shard_count + lax.axis_index("shard")
    seq_dev, max_len, _ = inputs.shape
    own_given = self_index * seq_dev + jnp.arange(seq_dev, dtype=jnp.int32)
    own_len = jnp.sum(jnp.where(dealing[None, :] == own_given[:, None], lengths[None, :], 0), axis=1)
    live = jnp.arange(max_len, dtype=jnp.int32)[None, :] < own_len[:, None]
    zero_low = jnp.zeros((), jnp.bfloat16)
    rows_in = jnp.where(live[..., None], inputs, zero_low).reshape(seq_dev * max_len, D)
    back_in = jnp.where(live[..., None], cotangent, zero_low).reshape(seq_dev * max_len, D)
    shard_weights = (
        g_attn,
        w_query,
        w_key,
        w_value,
        w_outgate,
        w_lowrank,
        w_forget,
        b_forget,
        g_head,
        w_output,
        g_ffn,
        w_gate,
        w_up,
        w_down,
    )
    grad_dims = (0, 0, 0, 0, 0, 0, 1, 0, 0, 0, 0, 0, 0, 1)
    gathered = tuple(
        lax.all_gather(weight, axes, axis=dim, tiled=True)
        for weight, dim in zip(shard_weights, grad_dims)
    )
    out_rows, grad_rows, grads = layer_pass(gathered, rows_in, back_in, seq_dev)
    reduced = tuple(
        lax.psum_scatter(
            grad.astype(jnp.bfloat16), axes, scatter_dimension=dim, tiled=True
        ).astype(jnp.float32)
        for grad, dim in zip(grads, grad_dims)
    )
    return (out_rows.reshape(inputs.shape), grad_rows.reshape(inputs.shape)) + reduced


def kernel_shards(
    inputs,
    cotangent,
    lengths,
    dealing,
    g_attn,
    w_query,
    w_key,
    w_value,
    w_outgate,
    w_lowrank,
    w_forget,
    b_forget,
    g_head,
    w_output,
    g_ffn,
    w_gate,
    w_up,
    w_down,
):
    seq_dev, max_len, _ = inputs.shape
    rows = (seq_dev * max_len, D)
    parts = (
        w_lowrank.T,
        g_attn.reshape(1, -1),
        g_ffn.reshape(1, -1),
        g_head.reshape(1, -1),
        w_forget,
        b_forget.reshape(1, -1),
        w_query,
        w_key,
        w_value,
        w_outgate,
        w_output,
        w_gate,
        w_up,
        w_down.T,
    )
    out_rows, grad_rows, red = layer_call(
        parts,
        inputs.reshape(rows),
        cotangent.reshape(rows),
        lengths.reshape(1, -1),
        dealing.reshape(1, -1),
    )
    weights = (
        g_attn,
        w_query,
        w_key,
        w_value,
        w_outgate,
        w_lowrank,
        w_forget,
        b_forget,
        g_head,
        w_output,
        g_ffn,
        w_gate,
        w_up,
        w_down,
    )
    shapes = [one.shape if one.ndim == 2 else (1,) + one.shape for one in weights]
    turned = (5, 13)
    for i in turned:
        shapes[i] = shapes[i][::-1]
    result = finish_call(red, out_rows, grad_rows, shapes)
    sums = tuple(
        one.T if i in turned else one.reshape(like.shape)
        for i, (one, like) in enumerate(zip(result[2:], weights))
    )
    return (result[0].reshape(inputs.shape), result[1].reshape(inputs.shape)) + sums


def solution(mesh):
    small = mesh.shape["grp"] == GRP and mesh.shape["shard"] == SHARD
    return jax.shard_map(
        kernel_shards if small else plain_shards,
        mesh=mesh,
        in_specs=(
            P(("grp", "shard"), None, None),
            P(("grp", "shard"), None, None),
            P(),
            P(),
            P(("grp", "shard")),
            P(("grp", "shard"), None),
            P(("grp", "shard"), None),
            P(("grp", "shard"), None),
            P(("grp", "shard"), None),
            P(("grp", "shard"), None),
            P(None, ("grp", "shard")),
            P(("grp", "shard")),
            P(("grp", "shard")),
            P(("grp", "shard"), None),
            P(("grp", "shard")),
            P(("grp", "shard"), None),
            P(("grp", "shard"), None),
            P(None, ("grp", "shard")),
        ),
        out_specs=(
            P(("grp", "shard"), None, None),
            P(("grp", "shard"), None, None),
            P(("grp", "shard")),
            P(("grp", "shard"), None),
            P(("grp", "shard"), None),
            P(("grp", "shard"), None),
            P(("grp", "shard"), None),
            P(("grp", "shard"), None),
            P(None, ("grp", "shard")),
            P(("grp", "shard")),
            P(("grp", "shard")),
            P(("grp", "shard"), None),
            P(("grp", "shard")),
            P(("grp", "shard"), None),
            P(("grp", "shard"), None),
            P(None, ("grp", "shard")),
        ),
        check_vma=False,
    )
```

```python
import jax
import jax.numpy as jnp
from jax import lax
from jax.experimental import pallas as pl
from jax.experimental.pallas import tpu as pltpu
from jax.sharding import PartitionSpec as P

D = 1024
HEADS = 4
BLOCK = 64


EPS = 1e-05
HEAD_EPS = 1.0

MESH = pl.DeviceIdType.MESH
DMA = pltpu.SemaphoreType.DMA
GRP = 4
SHARD = 8
ROWS = 32
WIDE = 768
FF_CUT = 256
SLOTS = 4
MISC = 128
DEVICES = 32
RANK = 16
KEY_WIDE = 512
VAL_WIDE = 1024
HEAD_KEY = 128
HEAD_VAL = 256
SCALE = 128 ** (-0.5)
SEQS = 4
SEQ = 192
BLOCKS = 3
LIVE = SEQS * SEQ
Q_AT = MISC
K_AT = Q_AT + KEY_WIDE
V_AT = K_AT + KEY_WIDE
G_AT = V_AT + VAL_WIDE
O_AT = G_AT + VAL_WIDE
PROJ = O_AT
GATE_AT = V_AT
MIX_CHUNKS = 6
FF_CHUNKS = 11
CHUNKS = MIX_CHUNKS + FF_CHUNKS
LAST_WIDE = O_AT + D - (MIX_CHUNKS - 1) * WIDE
MIX_ORDER = (5, 4, 3, 2, 1, 0)
NARROW = FF_CHUNKS + MIX_ORDER.index(MIX_CHUNKS - 1)
AHEAD = 4
EARLY = (0, 1)
SPREAD_AT = (7, 9)
PASS_AT = (13, 15)
RED_FROM = 4
SQUARE = 4
CORES = 2
SPREAD = (15, 16)
LINES = 15
VMEM_LIMIT = 63 << 20
HALVES = (slice(0, LIVE // 2), slice(LIVE // 2, LIVE))


def matmul(left_mat, right_mat):
    return jnp.dot(left_mat, right_mat, preferred_element_type=jnp.float32)


def rows_contract(left_mat, right_mat):
    return lax.dot_general(
        left_mat, right_mat, (((0,), (0,)), ((), ())), preferred_element_type=jnp.float32
    )


def right_transpose(left_mat, right_mat):
    return lax.dot_general(
        left_mat, right_mat, (((1,), (1,)), ((), ())), preferred_element_type=jnp.float32
    )


def scaled_rows(rows_in, gain_vec):
    return rows_in * lax.rsqrt(jnp.mean(rows_in * rows_in, axis=-1, keepdims=True) + EPS) * gain_vec


def head_rows(rows_in, gain_vec):
    return (
        rows_in
        * lax.rsqrt(jnp.mean(rows_in * rows_in, axis=-1, keepdims=True) + HEAD_EPS)
        * gain_vec
    )


def forget_rate(logits):
    return jax.nn.log_sigmoid(logits) / 16.0


def swiglu_core(pre_gate, pre_up):
    return jax.nn.silu(pre_gate) * pre_up


def head_gate(mixed_out, gate_out, head_gain):
    normed = head_rows(mixed_out, head_gain)
    active = gate_out * jax.nn.sigmoid(gate_out)
    return normed.reshape(active.shape) * active


def block_gates(queries, key_rows, forget):
    running = jnp.cumsum(forget, axis=1)
    tail_sum = running[:, -1:]
    q_gate = queries * queries.shape[-1] ** (-0.5) * jnp.exp(running)
    k_back = key_rows * jnp.exp(-running)
    k_tail = key_rows * jnp.exp(tail_sum - running)
    return (q_gate, k_back, k_tail, jnp.exp(tail_sum[:, 0]))


def layer_pass(weights, rows_in, back_in, seq_count):
    (
        g_attn,
        w_query,
        w_key,
        w_value,
        w_outgate,
        w_lowrank,
        w_forget,
        b_forget,
        g_head,
        w_output,
        g_ffn,
        w_gate,
        w_up,
        w_down,
    ) = weights
    row_count = rows_in.shape[0]
    blocks = row_count // BLOCK
    key_dim = w_query.shape[1] // HEADS
    val_dim = w_value.shape[1] // HEADS
    key_shape = (blocks, BLOCK, HEADS, key_dim)
    val_shape = (blocks, BLOCK, HEADS, val_dim)
    flat_rows = rows_in.astype(jnp.float32)
    norm_one, pull_one = jax.vjp(scaled_rows, flat_rows, g_attn.astype(jnp.float32))
    xn_one = norm_one.astype(jnp.bfloat16)
    queries = matmul(xn_one, w_query)
    key_rows = matmul(xn_one, w_key)
    values = matmul(xn_one, w_value).astype(jnp.bfloat16)
    gate_out = matmul(xn_one, w_outgate)
    lowrank = matmul(xn_one, w_lowrank).astype(jnp.bfloat16)
    logits = matmul(lowrank, w_forget) + b_forget.astype(jnp.float32)
    forget, pull_forget = jax.vjp(forget_rate, logits)
    gate_vals, pull_gates = jax.vjp(
        block_gates,
        queries.reshape(key_shape),
        key_rows.reshape(key_shape),
        forget.reshape(key_shape),
    )
    q_gate = gate_vals[0].astype(jnp.bfloat16)
    k_back = gate_vals[1].astype(jnp.bfloat16)
    k_tail = gate_vals[2].astype(jnp.bfloat16)
    decays = gate_vals[3]
    val_blocks = values.reshape(val_shape)
    spot_ids = jnp.arange(BLOCK)
    causal = (spot_ids[:, None] >= spot_ids[None, :]).astype(jnp.float32)
    scores = jnp.einsum("cthd,cshd->chts", q_gate, k_back, preferred_element_type=jnp.float32)
    attn_probs = (scores * causal).astype(jnp.bfloat16)
    intra_out = jnp.einsum(
        "chts,cshe->cthe", attn_probs, val_blocks, preferred_element_type=jnp.float32
    )
    update = jnp.einsum("cthd,cthe->chde", k_tail, val_blocks, preferred_element_type=jnp.float32)

    per_seq = blocks // seq_count
    seq_blocks = (seq_count, per_seq) + update.shape[1:]
    upd_seq = update.reshape(seq_blocks)
    decay_seq = decays.reshape((seq_count, per_seq) + decays.shape[1:])
    carried = jnp.zeros_like(upd_seq[:, 0])
    before_list = []
    for idx in range(per_seq):
        before_list.append(carried)
        carried = decay_seq[:, idx][..., None] * carried + upd_seq[:, idx]
    before_seq = jnp.stack(before_list, axis=1)
    before_low = before_seq.reshape(update.shape).astype(jnp.bfloat16)
    inter_out = jnp.einsum(
        "cthd,chde->cthe", q_gate, before_low, preferred_element_type=jnp.float32
    )
    mixed_out = (intra_out + inter_out).reshape(row_count, HEADS, val_dim)
    gated_f, pull_head = jax.vjp(head_gate, mixed_out, gate_out, g_head.astype(jnp.float32))
    gated_out = gated_f.astype(jnp.bfloat16)
    resid_one = flat_rows + matmul(gated_out, w_output)
    norm_two, pull_two = jax.vjp(scaled_rows, resid_one, g_ffn.astype(jnp.float32))
    xn_two = norm_two.astype(jnp.bfloat16)
    pre_gate = matmul(xn_two, w_gate)
    pre_up = matmul(xn_two, w_up)
    hidden_f, pull_ffn = jax.vjp(swiglu_core, pre_gate, pre_up)
    hidden = hidden_f.astype(jnp.bfloat16)
    output = (resid_one + matmul(hidden, w_down)).astype(jnp.bfloat16)
    back_f = back_in.astype(jnp.float32)
    dw_down = rows_contract(hidden, back_in)
    d_hidden = right_transpose(back_in, w_down)
    d_pre_gate, d_pre_up = pull_ffn(d_hidden)
    d_gate_low = d_pre_gate.astype(jnp.bfloat16)
    d_up_low = d_pre_up.astype(jnp.bfloat16)
    dw_gate = rows_contract(xn_two, d_gate_low)
    dw_up = rows_contract(xn_two, d_up_low)
    d_norm_two = right_transpose(d_gate_low, w_gate) + right_transpose(d_up_low, w_up)
    d_resid_part, dg_ffn = pull_two(d_norm_two)
    d_resid = back_f + d_resid_part
    d_attn = d_resid.astype(jnp.bfloat16)
    dw_output = rows_contract(gated_out, d_attn)
    d_gated = right_transpose(d_attn, w_output)
    d_mixed_f, d_gate_out_f, dg_head = pull_head(d_gated)
    d_mixed = d_mixed_f.astype(jnp.bfloat16).reshape(val_shape)
    d_scores = jnp.einsum(
        "cthe,cshe->chts", d_mixed, val_blocks, preferred_element_type=jnp.float32
    )
    d_probs = (d_scores * causal).astype(jnp.bfloat16)
    d_q_gate = jnp.einsum(
        "chts,cshd->cthd", d_probs, k_back, preferred_element_type=jnp.float32
    ) + jnp.einsum("cthe,chde->cthd", d_mixed, before_low, preferred_element_type=jnp.float32)
    d_k_back = jnp.einsum("chts,cthd->cshd", d_probs, q_gate, preferred_element_type=jnp.float32)
    d_val_intra = jnp.einsum(
        "chts,cthe->cshe", attn_probs, d_mixed, preferred_element_type=jnp.float32
    )
    d_before = jnp.einsum("cthd,cthe->chde", q_gate, d_mixed, preferred_element_type=jnp.float32)

    d_before_seq = d_before.reshape(seq_blocks)
    d_after = jnp.zeros_like(upd_seq[:, 0])
    d_update_list = []
    d_decay_list = []
    for idx in reversed(range(per_seq)):
        d_update_list.append(d_after)
        d_decay_list.append(jnp.sum(d_after * before_seq[:, idx], axis=-1))
        d_after = d_before_seq[:, idx] + decay_seq[:, idx][..., None] * d_after
    d_update = jnp.stack(d_update_list[::-1], axis=1).reshape(update.shape)
    d_decays = jnp.stack(d_decay_list[::-1], axis=1).reshape(decays.shape)
    d_update_low = d_update.astype(jnp.bfloat16)
    d_k_tail = jnp.einsum(
        "cthe,chde->cthd", val_blocks, d_update_low, preferred_element_type=jnp.float32
    )
    d_values = (
        (
            d_val_intra
            + jnp.einsum(
                "cthd,chde->cthe", k_tail, d_update_low, preferred_element_type=jnp.float32
            )
        )
        .reshape(row_count, -1)
        .astype(jnp.bfloat16)
    )
    d_query_f, d_key_f, d_forget = pull_gates((d_q_gate, d_k_back, d_k_tail, d_decays))
    d_queries = d_query_f.reshape(row_count, -1).astype(jnp.bfloat16)
    d_keys = d_key_f.reshape(row_count, -1).astype(jnp.bfloat16)
    (d_logits,) = pull_forget(d_forget.reshape(row_count, -1))
    db_forget = jnp.sum(d_logits, axis=0)
    d_logit_low = d_logits.astype(jnp.bfloat16)
    dw_forget = rows_contract(lowrank, d_logit_low)
    d_lowrank = right_transpose(d_logit_low, w_forget).astype(jnp.bfloat16)
    d_gate_out = d_gate_out_f.astype(jnp.bfloat16)
    dw_query = rows_contract(xn_one, d_queries)
    dw_key = rows_contract(xn_one, d_keys)
    dw_value = rows_contract(xn_one, d_values)
    dw_outgate = rows_contract(xn_one, d_gate_out)
    dw_lowrank = rows_contract(xn_one, d_lowrank)
    d_norm_one = (
        right_transpose(d_queries, w_query)
        + right_transpose(d_keys, w_key)
        + right_transpose(d_values, w_value)
        + right_transpose(d_gate_out, w_outgate)
        + right_transpose(d_lowrank, w_lowrank)
    )
    d_flat, dg_attn = pull_one(d_norm_one)
    grad_rows = (d_resid + d_flat).astype(jnp.bfloat16)
    grads = (
        dg_attn,
        dw_query,
        dw_key,
        dw_value,
        dw_outgate,
        dw_lowrank,
        dw_forget,
        db_forget,
        dg_head,
        dw_output,
        dg_ffn,
        dw_gate,
        dw_up,
        dw_down,
    )
    return (output, grad_rows, grads)


def when(cond, do):
    if isinstance(cond, bool):
        if cond:
            do()
    else:
        pl.when(cond)(do)


def columns(ref, lo, hi):
    return ref[:, :, :, :, lo:hi].reshape(D, hi - lo)


def put_columns(ref, lo, hi, value):
    ref[:, :, :, :, lo:hi] = value.reshape(GRP, SQUARE, CORES, ROWS, hi - lo)


def flip(index, bit):
    return index + bit - 2 * bit * lax.rem(index // bit, 2)


def remote(src, dst, send_sem, recv_sem, device):
    return pltpu.make_async_remote_copy(
        src_ref=src,
        dst_ref=dst,
        send_sem=send_sem,
        recv_sem=recv_sem,
        device_id=device,
        device_id_type=MESH,
    )


def start_all(copies):
    for copy in copies:
        copy.start()


def recv_all(copies):
    for copy in copies:
        copy.wait_recv()


def sent_all(copies):
    for copy in copies:
        copy.wait_send()


class Place:
    def __init__(self):
        self.z = lax.axis_index("grp")
        self.s = lax.axis_index("shard")
        self.core = lax.rem(self.s, CORES)
        self.q = self.s // CORES
        self.qx = flip(self.q, 1)
        self.qy = flip(self.q, 2)
        self.qd = flip(self.qx, 2)
        self.z_peers = [lax.rem(self.z + step, GRP) for step in range(1, GRP)]
        self.z_from = [lax.rem(self.z + GRP - step, GRP) for step in range(1, GRP)]
        self.line_to = [(peer, self.s) for peer in self.z_peers]
        self.middle = (self.z == 1) | (self.z == 2)
        self.near = [self.z != GRP - 1, True, self.z != 0]
        self.pass_from = lax.rem(self.z + 2, GRP)
        self.pass_to = jnp.where(self.z == 1, 0, GRP - 1)
        self.pass_slot = jnp.where(self.z == 1, 0, 2)
        self.sib = (self.z, flip(self.s, 1))
        self.xn = (self.z, flip(self.s, CORES))
        self.yn = (self.z, flip(self.s, 2 * CORES))

    def greet(self):
        barrier = pltpu.get_barrier_semaphore()
        peers = self.line_to + [self.sib, self.xn, self.yn]
        for peer in peers:
            pl.semaphore_signal(barrier, inc=1, device_id=peer, device_id_type=MESH)
        return (barrier, len(peers))


class Gather:
    def __init__(self, place, parts, full, sems):
        self.p = place
        self.parts = parts
        self.full = full
        (
            self.ls,
            self.zs,
            self.zr,
            self.fs,
            self.xs,
            self.xr,
            self.ds,
            self.dr,
            self.ss,
            self.sr,
            self.es,
            self.er,
        ) = sems

    def cols(self, c):
        narrow = isinstance(c, int) and c == MIX_CHUNKS - 1
        return pl.ds(0, LAST_WIDE if narrow else WIDE)

    def mine(self, c):
        return self.parts.at[c // 16, c % 16 // SQUARE, c % SQUARE, :, self.cols(c)]

    def locals(self):
        p = self.p
        groups = [(g, pl.ds(g * SQUARE, SQUARE)) for g in range(16 // SQUARE)]
        copies = [
            pltpu.make_async_copy(
                self.parts.at[0, g], self.full.at[chunks, p.z, p.q, p.core], self.ls.at[g]
            )
            for g, chunks in groups
        ]
        last = pltpu.make_async_copy(
            self.parts.at[1, 0, 0], self.full.at[16, p.z, p.q, p.core], self.ls.at[4]
        )
        return copies + [last]

    def view(self, c, z, q):
        return self.full.at[c, z, q, self.p.core, :, self.cols(c)]

    def line(self, c):
        p = self.p
        there = self.view(c, p.z, p.q)
        return [
            remote(self.mine(c), there, self.zs.at[c, k], self.zr.at[c, k], p.line_to[k])
            for k in range(GRP - 1)
        ]

    def held(self, c, z):
        if isinstance(c, int) and c in SPREAD:
            return self.full.at[c, z, :, self.p.core]
        return self.view(c, z, self.p.q)

    def line_in(self, c, k):
        view = self.held(c, self.p.z_from[k])
        remote(view, view, self.zs.at[c, k], self.zr.at[c, k], self.p.line_to[k]).wait_recv()

    def passed(self, c):
        p = self.p
        view = self.held(c, p.pass_from)
        to = (p.pass_to, p.s)
        return remote(view, view, self.fs.at[c], self.zr.at[c, p.pass_slot], to)

    def near_all(self, copies, do):
        for copy, near in zip(copies, self.p.near):
            when(near, lambda copy=copy: do(copy))

    def pass_on(self, c):
        def middle():
            self.line_in(c, 1)
            self.passed(c).start()

        pl.when(self.p.middle)(middle)

    def line_end(self, c):
        self.line_in(c, 0)
        pl.when(jnp.logical_not(self.p.middle))(lambda: self.line_in(c, 1))
        self.line_in(c, 2)

    def line_sent(self, c):
        copies = self.spread(c) if isinstance(c, int) and c in SPREAD else self.line(c)
        self.near_all(copies, lambda copy: copy.wait_send())
        pl.when(self.p.middle)(lambda: self.passed(c).wait_send())

    def z_part(self, c):
        return self.p.z if isinstance(c, int) and c in SPREAD else pl.ds(0, GRP)

    def plane(self, c):
        p = self.p
        there = self.view(c, self.z_part(c), p.q)
        here = self.mine(c) if isinstance(c, int) and c in SPREAD else there
        return [
            remote(here, there, self.xs.at[c, k], self.xr.at[c, k], to)
            for k, to in enumerate((p.xn, p.yn))
        ]

    def plane_in(self, c):
        p = self.p
        return [
            remote(view, view, self.xs.at[c, k], self.xr.at[c, k], to)
            for k, (view, to) in enumerate(
                (
                    (self.view(c, self.z_part(c), p.qx), p.xn),
                    (self.view(c, self.z_part(c), p.qy), p.yn),
                )
            )
        ]

    def halves(self, c, q_low, q_high):
        if isinstance(c, int) and c in SPREAD:
            half = ROWS // 2
            return (
                self.full.at[c, self.p.z, q_low, self.p.core, pl.ds(0, half)],
                self.full.at[c, self.p.z, q_high, self.p.core, pl.ds(half, half)],
            )
        return (self.view(c, pl.ds(0, 2), q_low), self.view(c, pl.ds(2, 2), q_high))

    def corner(self, c):
        p = self.p
        low, high = self.halves(c, p.qx, p.qy)
        return [
            remote(low, low, self.ds.at[c, 0], self.dr.at[c, 0], p.yn),
            remote(high, high, self.ds.at[c, 1], self.dr.at[c, 1], p.xn),
        ]

    def corner_in(self, c):
        p = self.p
        low, high = self.halves(c, p.qd, p.qd)
        return [
            remote(low, low, self.ds.at[c, 0], self.dr.at[c, 0], p.yn),
            remote(high, high, self.ds.at[c, 1], self.dr.at[c, 1], p.xn),
        ]

    def spread(self, c):
        p = self.p
        own = self.full.at[c, p.z, :, p.core]
        return [
            remote(own, own, self.zs.at[c, k], self.zr.at[c, k], p.line_to[k])
            for k in range(GRP - 1)
        ]

    def other(self, c, core):
        view = self.full.at[c, :, :, core, :, self.cols(c)]
        return remote(view, view, self.ss.at[c], self.sr.at[c], self.p.sib)

    def other_in(self, c):
        self.other(c, 1 - self.p.core).wait_recv()

    def other_out(self, c):
        self.other(c, self.p.core).start()

    def line_out(self, c):
        self.near_all(self.line(c), lambda copy: copy.start())

    def line_stage(self, c):
        if isinstance(c, int) and c in EARLY:
            self.line_in(c, 0)
            start_all(self.early(c, 1))
            pl.when(jnp.logical_not(self.p.middle))(lambda: self.line_in(c, 1))
            start_all(self.early(c, 2))
            self.line_in(c, 2)
            start_all(self.early(c, 3))
            return
        self.line_end(c)
        start_all(self.plane(c))

    def early(self, c, j):
        p = self.p
        there = self.view(c, ([p.z] + p.z_from)[j], p.q)
        here = self.mine(c) if j == 0 else there
        return [
            remote(here, there, self.es.at[c, j, k], self.er.at[c, j, k], to)
            for k, to in enumerate((p.xn, p.yn))
        ]

    def early_in(self, c):
        p = self.p
        for j, z in enumerate([p.z] + p.z_from):
            for k, (q, to) in enumerate(((p.qx, p.xn), (p.qy, p.yn))):
                view = self.view(c, z, q)
                remote(view, view, self.es.at[c, j, k], self.er.at[c, j, k], to).wait_recv()

    def plane_stage(self, c):
        if isinstance(c, int) and c in EARLY:
            self.early_in(c)
        else:
            recv_all(self.plane_in(c))
        start_all(self.corner(c))

    def corner_stage(self, c):
        recv_all(self.corner_in(c))
        self.other_out(c)

    def spread_first(self, c):
        start_all(self.plane(c))

    def spread_out(self, c):
        recv_all(self.corner_in(c))
        self.near_all(self.spread(c), lambda copy: copy.start())

    def spread_last(self, c):
        self.line_end(c)
        self.other_out(c)

    def step(self, t):
        def some(c, do):
            when(0 <= c < LINES, lambda: do(c))

        some(t + AHEAD, self.line_out)
        some(t + 1, self.pass_on)
        some(t, self.line_stage)
        some(t - 1, self.plane_stage)
        some(t - 2, self.corner_stage)
        some(t - 3, self.other_in)
        if t == 1:
            for c in SPREAD:
                self.plane_stage(c)
        for c, at in zip(SPREAD, SPREAD_AT):
            if t == at:
                self.spread_out(c)

    def spread_pass(self, t):
        for c, at in zip(SPREAD, PASS_AT):
            when(t == at, lambda c=c: self.pass_on(c))

    def mid_step(self, t):
        when(t + AHEAD < LINES, lambda: self.line_out(t + AHEAD))
        when(t + 1 < LINES, lambda: self.pass_on(t + 1))
        self.line_stage(t)
        self.plane_stage(t - 1)
        self.corner_stage(t - 2)
        self.other_in(t - 3)
        self.spread_pass(t)

    def late_step(self, t):
        self.spread_pass(t)
        when(t == LINES - 1, lambda: self.line_stage(LINES - 1))
        when(t <= LINES, lambda: self.plane_stage(t - 1))
        when(t <= LINES + 1, lambda: self.corner_stage(t - 2))
        when(t <= LINES + 2, lambda: self.other_in(t - 3))
        when(t == LINES + 2, lambda: self.spread_last(SPREAD[0]))
        when(t == LINES + 3, lambda: self.other_in(SPREAD[0]))
        when(t == LINES + 3, lambda: self.spread_last(SPREAD[1]))
        when(t == LINES + 4, lambda: self.other_in(SPREAD[1]))

    def drain_parts(self):
        for c in range(LINES):
            self.line_sent(c)
        for c in SPREAD:
            sent_all(self.plane(c))
        for c in EARLY:
            sent_all(self.early(c, 0))

    def drain(self, c):
        if c in SPREAD:
            self.line_sent(c)
        elif c in EARLY:
            for j in range(1, GRP):
                sent_all(self.early(c, j))
        else:
            sent_all(self.plane(c))
        sent_all(self.corner(c) + [self.other(c, self.p.core)])


class Reduce:
    def __init__(self, place, src, out, bufs, sems):
        self.p = place
        self.src = src
        self.out = out
        self.own, self.b1, self.b2, self.b3, self.b4, self.stage = bufs
        (
            self.ls,
            self.s1,
            self.r1,
            self.s2,
            self.r2,
            self.s3,
            self.r3,
            self.s4,
            self.r4,
            self.out_sem,
        ) = sems

    def slot(self, c):
        return c % SLOTS if isinstance(c, int) else lax.rem(c, SLOTS)

    def wide(self, c):
        return LAST_WIDE if isinstance(c, int) and c == NARROW else WIDE

    def local(self, c):
        k, n = self.slot(c), pl.ds(0, self.wide(c))
        return pltpu.make_async_copy(
            self.src.at[c, :, :, self.p.core, :, n], self.own.at[k, :, :, :, n], self.ls.at[k]
        )

    def other(self, c):
        k, n = self.slot(c), pl.ds(0, self.wide(c))
        return remote(
            self.src.at[c, :, :, 1 - self.p.core, :, n],
            self.b1.at[k, :, :, :, n],
            self.s1.at[k],
            self.r1.at[k],
            self.p.sib,
        )

    def corner(self, c):
        p, k, n = self.p, self.slot(c), pl.ds(0, self.wide(c))
        return [
            remote(
                self.own.at[k, pl.ds(2 * i, 2), p.qd, :, n],
                self.b2.at[k, i, :, :, n],
                self.s2.at[k, i],
                self.r2.at[k, i],
                to,
            )
            for i, to in enumerate((p.xn, p.yn))
        ]

    def plane(self, c):
        p, k, n = self.p, self.slot(c), pl.ds(0, self.wide(c))
        return [
            remote(
                self.own.at[k, :, q, :, n],
                self.b3.at[k, i, :, :, n],
                self.s3.at[k, i],
                self.r3.at[k, i],
                to,
            )
            for i, (q, to) in enumerate(((p.qx, p.xn), (p.qy, p.yn)))
        ]

    def line(self, c):
        p, k, n = self.p, self.slot(c), pl.ds(0, self.wide(c))
        return [
            remote(
                self.own.at[k, p.z_peers[i], p.q, :, n],
                self.b4.at[k, i, :, n],
                self.s4.at[k, i],
                self.r4.at[k, i],
                p.line_to[i],
            )
            for i in range(GRP - 1)
        ]

    def drain(self, c):
        sent_all([self.other(c)] + self.corner(c) + self.plane(c) + self.line(c))

    def enter(self, c):
        when(c >= SLOTS, lambda: self.drain(c - SLOTS))
        self.local(c).start()
        self.other(c).start()

    def add_other(self, c):
        p, k, n = self.p, self.slot(c), slice(0, self.wide(c))
        self.local(c).wait()
        self.other(c).wait_recv()
        for q in (p.qd, p.qx, p.qy, p.q):
            self.own[k, :, q, :, n] = self.own[k, :, q, :, n] + self.b1[k, :, q, :, n]
            if q is p.qd:
                start_all(self.corner(c))

    def add_corner(self, c):
        p, k, n = self.p, self.slot(c), slice(0, self.wide(c))
        recv_all(self.corner(c))
        for q, cut, i in ((p.qy, slice(0, 2), 0), (p.qx, slice(2, 4), 1)):
            self.own[k, cut, q, :, n] = self.own[k, cut, q, :, n] + self.b2[k, i, :, :, n]
        start_all(self.plane(c))

    def add_plane(self, c):
        p, k, n = self.p, self.slot(c), slice(0, self.wide(c))
        recv_all(self.plane(c))
        total = wide_type(self.own[k, :, p.q, :, n])
        total += wide_type(self.b3[k, 0, :, :, n])
        total += wide_type(self.b3[k, 1, :, :, n])
        self.own[k, :, p.q, :, n] = low_type(total)
        start_all(self.line(c))

    def finish(self, c):
        p, k, n = self.p, self.slot(c), slice(0, self.wide(c))
        recv_all(self.line(c))
        total = wide_type(self.own[k, p.z, p.q, :, n])
        for i in range(GRP - 1):
            total += wide_type(self.b4[k, i, :, n])
        when(c >= SLOTS, lambda: self.leave(c - SLOTS).wait())
        self.stage[k, :, n] = total
        self.leave(c).start()

    def leave(self, c):
        k, n = self.slot(c), pl.ds(0, self.wide(c))
        return pltpu.make_async_copy(
            self.stage.at[k, :, n], self.out.at[c, :, n], self.out_sem.at[k]
        )

    def step(self, t):
        def some(c, do):
            if isinstance(c, int):
                when(0 <= c < CHUNKS, lambda: do(c))
            else:
                when(c >= 0, lambda: do(c))

        some(t - 3, self.finish)
        some(t + 1, self.enter)
        some(t, self.add_other)
        some(t - 1, self.add_corner)
        some(t - 2, self.add_plane)


def reduce_scratch():
    def buf(*shape):
        return pltpu.VMEM((SLOTS,) + shape + (ROWS, WIDE), jnp.bfloat16)

    bufs = [buf(GRP, SQUARE), buf(GRP, SQUARE), buf(2, 2), buf(2, GRP), buf(GRP - 1)]
    bufs.append(pltpu.VMEM((SLOTS, ROWS, WIDE), jnp.float32))
    sems = [DMA((SLOTS,))] * 3 + [DMA((SLOTS, count)) for count in (2, 2, 2, 2, 3, 3)]
    return bufs + sems + [DMA((SLOTS,))]


def mm_nn(left_mat, right_mat):
    return jnp.dot(left_mat, right_mat, preferred_element_type=jnp.float32)


def mm_nt(left_mat, right_mat):
    return right_transpose(left_mat, right_mat)


def mm_tn(left_mat, right_mat):
    return rows_contract(left_mat, right_mat)


def low_type(value):
    return value.astype(jnp.bfloat16)


def wide_type(value):
    return value.astype(jnp.float32)


def exact_sum(zero_one, value):
    high = low_type(value)
    rest = value - wide_type(high)
    mid = low_type(rest)
    last = low_type(rest - wide_type(mid))
    return mm_nn(zero_one, high) + mm_nn(zero_one, mid) + mm_nn(zero_one, last)


def iota(shape, dim):
    return lax.broadcasted_iota(jnp.int32, shape, dim)


def place_matrix(keep, columns):
    row = iota((D, columns), 0)
    col = iota((D, columns), 1)
    hit = (row // ROWS == col // keep) & (row % ROWS == col % keep)
    return low_type(jnp.where(hit, 1.0, 0.0))


def unit_matrix(size):
    return low_type(jnp.where(iota((size, size), 0) == iota((size, size), 1), 1.0, 0.0))


def row_rsqrt(value, eps):
    return lax.rsqrt(jnp.mean(value * value, axis=-1, keepdims=True) + eps)


class Layer:
    def __init__(self, refs):
        self.__dict__.update(refs)

    def rows(self, i):
        return pl.ds(pl.multiple_of(i * SEQ, SEQ), SEQ)

    def mask(self, lengths, dealing, first_seq):
        held = wide_type(lengths[...])
        for i in range(SEQS):
            r = pl.ds(i * SEQ, SEQ)
            match = dealing[...] == first_seq + i
            length = jnp.sum(jnp.where(match, held, 0.0), axis=1, keepdims=True)
            live = wide_type(iota((SEQ, 1), 0)) < length
            self.x[r, :] = jnp.where(live, self.x[r, :], jnp.zeros((), jnp.bfloat16))
            self.cot[r, :] = jnp.where(live, self.cot[r, :], jnp.zeros((), jnp.bfloat16))

    def prepare(self):
        misc = columns(self.wm.at[0], 0, MISC)
        turned = mm_nt(unit_matrix(MISC), misc)
        self.gains[0:1, :] = turned[RANK : RANK + 1]
        self.gains[1:2, :] = turned[RANK + 1 : RANK + 2]
        picked = mm_tn(misc, place_matrix(KEY_WIDE // DEVICES, KEY_WIDE))
        self.wf[...] = jnp.zeros_like(self.wf)
        self.wf[0:RANK, :] = low_type(picked[32 : 32 + RANK])
        self.bias[0:1, :] = picked[48:49]
        heads = mm_tn(misc, place_matrix(HEAD_VAL // DEVICES, HEAD_VAL))
        self.ghead[0:1, :] = heads[18:19]
        for i in range(SEQS):
            r = pl.ds(i * SEQ, SEQ)
            value = wide_type(self.x[r, :])
            self.xn1[r, :] = low_type(value * row_rsqrt(value, EPS) * self.gains[0:1, :])

    def project(self, c):
        lo, hi = c * WIDE, min((c + 1) * WIDE, PROJ)
        for r in HALVES:
            value = mm_nn(self.xn1[r, :], columns(self.wm.at[c], 0, hi - lo))
            for ref, at, first, last in self.pieces(lo, hi):
                ref[r, at : at + last - first] = value[:, first:last].astype(ref.dtype)

    def pieces(self, lo, hi):
        found = []
        for ref, start, end, at in (
            (self.proj, 0, V_AT, 0),
            (self.pval, V_AT, G_AT, 0),
            (self.proj, G_AT, PROJ, GATE_AT),
        ):
            a, b = max(lo, start), min(hi, end)
            if a < b:
                found.append((ref, at + a - start, a - lo, b - lo))
        return found

    def gates(self, r):
        lane = iota((SEQ, MISC), 1)
        lowrank = low_type(jnp.where(lane < RANK, self.proj[r, 0:MISC], 0.0))
        logits = mm_nn(lowrank, self.wf[...]) + self.bias[0:1, :]
        forget = (jnp.minimum(logits, 0.0) - jnp.log1p(jnp.exp(-jnp.abs(logits)))) * (1.0 / 16.0)
        row, col = iota((SEQ, SEQ), 0), iota((SEQ, SEQ), 1)
        same = row // BLOCK == col // BLOCK
        causal = same & (col <= row)
        running = exact_sum(low_type(jnp.where(causal, 1.0, 0.0)), forget)
        tails = [running[b * BLOCK + BLOCK - 1 : (b + 1) * BLOCK] for b in range(BLOCKS)]
        tail = jnp.concatenate(
            [jnp.broadcast_to(one, (BLOCK, KEY_WIDE)) for one in tails], axis=0
        )
        return (lowrank, logits, running, tails, tail, same, causal)

    def attend(self, i):
        r = self.rows(i)
        _, _, running, tails, tail, _, causal = self.gates(r)
        grow = jnp.exp(running)
        fade = jnp.exp(-running)
        late = jnp.exp(tail - running)
        for h in range(HEADS):
            k = slice(h * HEAD_KEY, (h + 1) * HEAD_KEY)
            queries = self.proj[r, Q_AT + h * HEAD_KEY : Q_AT + (h + 1) * HEAD_KEY]
            key_rows = self.proj[r, K_AT + h * HEAD_KEY : K_AT + (h + 1) * HEAD_KEY]
            values = self.pval[r, h * HEAD_VAL : (h + 1) * HEAD_VAL]
            q_gate = low_type(queries * SCALE * grow[:, k])
            k_back = low_type(key_rows * fade[:, k])
            k_tail = low_type(key_rows * late[:, k])
            probs = low_type(jnp.where(causal, mm_nt(q_gate, k_back), 0.0))
            mixed = mm_nn(probs, values)
            state = mm_tn(values[0:BLOCK], k_tail[0:BLOCK])
            parts = [mixed[0:BLOCK]]
            for b in range(1, BLOCKS):
                cut = slice(b * BLOCK, (b + 1) * BLOCK)
                parts.append(mixed[cut] + mm_nt(q_gate[cut], low_type(state)))
                if b + 1 < BLOCKS:
                    state = state * jnp.exp(tails[b][:, k]) + mm_tn(values[cut], k_tail[cut])
            self.mixed[r, h * HEAD_VAL : (h + 1) * HEAD_VAL] = jnp.concatenate(parts, axis=0)

    def gate_rows(self, i):
        r = self.rows(i)
        for h in range(HEADS):
            v = slice(h * HEAD_VAL, (h + 1) * HEAD_VAL)
            mixed = self.mixed[r, v]
            gate = self.proj[r, GATE_AT + h * HEAD_VAL : GATE_AT + (h + 1) * HEAD_VAL]
            normed = mixed * row_rsqrt(mixed, HEAD_EPS) * self.ghead[0:1, :]
            self.gated[r, v] = low_type(normed * (gate * jax.nn.sigmoid(gate)))

    def mix_out(self):
        cut = WIDE - O_AT % WIDE
        first = O_AT // WIDE
        lo = O_AT % WIDE
        for i in range(SEQS):
            r = pl.ds(i * SEQ, SEQ)
            self.out_sum[r, 0:cut] = wide_type(self.x[r, 0:cut]) + mm_nn(
                self.gated[r, :], columns(self.wm.at[first], lo, WIDE)
            )
            self.out_sum[r, cut:D] = wide_type(self.x[r, cut:D]) + mm_nn(
                self.gated[r, :], columns(self.wl, 0, D - cut)
            )

    def second_norm(self):
        for i in range(SEQS):
            r = pl.ds(i * SEQ, SEQ)
            value = self.out_sum[r, :]
            self.xn2[r, :] = low_type(value * row_rsqrt(value, EPS) * self.gains[1:2, :])
        self.dx_sum[...] = jnp.zeros_like(self.dx_sum)
        self.turn(self.xn2, self.turn_a)

    def turn(self, src, dst):
        for i in range(LIVE // 256):
            dst[:, i * 256 : (i + 1) * 256] = src[i * 256 : (i + 1) * 256, :].T

    def ffn(self, w_ref, g_ref):
        c = FF_CUT
        for r in HALVES:
            pre = mm_nn(self.xn2[r, :], columns(w_ref, 0, 2 * c))
            d_hidden = mm_nn(self.cot[r, :], columns(w_ref, 2 * c, 3 * c))
            pre_gate, pre_up = pre[:, 0:c], pre[:, c : 2 * c]
            sig = jax.nn.sigmoid(pre_gate)
            silu = pre_gate * sig
            self.hid[r, :] = low_type(silu * pre_up)
            self.dpre[r, 0:c] = low_type(d_hidden * pre_up * sig * (1.0 + pre_gate * (1.0 - sig)))
            self.dpre[r, c : 2 * c] = low_type(d_hidden * silu)
            self.out_sum[r, :] += mm_nt(self.hid[r, :], columns(w_ref, 2 * c, 3 * c))
            self.dx_sum[r, :] += mm_nt(self.dpre[r, :], columns(w_ref, 0, 2 * c))
        put_columns(g_ref, 0, 2 * c, low_type(mm_nn(self.turn_a[...], self.dpre[...])))
        put_columns(g_ref, 2 * c, 3 * c, low_type(mm_nn(self.turn_b[...], self.hid[...])))

    def norm_back(self, value, d_out, gain, eps):
        rs = row_rsqrt(value, eps)
        scaled = gain * d_out
        mean = jnp.mean(value * scaled, axis=-1, keepdims=True)
        d_gain = jnp.sum(d_out * value * rs, axis=0, keepdims=True)
        return (rs * scaled - value * (rs * rs * rs * mean), d_gain)

    def after_ffn(self):
        cut = WIDE - O_AT % WIDE
        first = O_AT // WIDE
        lo = O_AT % WIDE
        total = jnp.zeros((1, D), jnp.float32)
        for i in range(SEQS):
            r = pl.ds(i * SEQ, SEQ)
            resid = wide_type(self.x[r, :]) + jnp.concatenate(
                [
                    mm_nn(self.gated[r, :], columns(self.wm.at[first], lo, WIDE)),
                    mm_nn(self.gated[r, :], columns(self.wl, 0, D - cut)),
                ],
                axis=1,
            )
            d_val, d_gain = self.norm_back(
                resid, self.dx_sum[r, :], self.gains[1:2, :], EPS
            )
            total += d_gain
            d_resid = wide_type(self.cot[r, :]) + d_val
            self.dx_sum[r, :] = d_resid
            self.xn2[r, :] = low_type(d_resid)
        self.dgains[1:2, :] = total
        self.turn(self.gated, self.turn_a)
        self.turn(self.xn1, self.turn_b)
        self.gated[...] = low_type(self.out_sum[...])
        self.dwf[...] = jnp.zeros_like(self.dwf)
        self.dbias[...] = jnp.zeros_like(self.dbias)
        self.dghead[...] = jnp.zeros_like(self.dghead)

    def retreat(self, i):
        r = self.rows(i)
        cut = WIDE - O_AT % WIDE
        first = O_AT // WIDE
        lo = O_AT % WIDE
        d_attn = self.xn2[r, :]
        d_gated = mm_nt(d_attn[:, 0:cut], columns(self.wm.at[first], lo, WIDE))
        d_gated += mm_nt(d_attn[:, cut:D], columns(self.wl, 0, D - cut))
        lowrank, logits, running, tails, tail, same, causal = self.gates(r)
        grow = jnp.exp(running)
        fade = jnp.exp(-running)
        late = jnp.exp(tail - running)
        d_forget_parts = []
        tail_parts = []
        d_ghead = jnp.zeros((1, HEAD_VAL), jnp.float32)
        for h in range(HEADS):
            k = slice(h * HEAD_KEY, (h + 1) * HEAD_KEY)
            v = slice(h * HEAD_VAL, (h + 1) * HEAD_VAL)
            q_cols = slice(Q_AT + h * HEAD_KEY, Q_AT + (h + 1) * HEAD_KEY)
            k_cols = slice(K_AT + h * HEAD_KEY, K_AT + (h + 1) * HEAD_KEY)
            g_cols = slice(GATE_AT + h * HEAD_VAL, GATE_AT + (h + 1) * HEAD_VAL)
            mixed = self.mixed[r, v]
            gate = self.proj[r, g_cols]
            sig = jax.nn.sigmoid(gate)
            act = gate * sig
            rs = row_rsqrt(mixed, HEAD_EPS)
            unit = mixed * rs
            gain = self.ghead[0:1, :]
            d_out = d_gated[:, v]
            d_normed = d_out * act
            d_gate = d_out * (unit * gain) * sig * (1.0 + gate * (1.0 - sig))
            self.proj[r, g_cols] = wide_type(low_type(d_gate))
            d_ghead += jnp.sum(d_normed * unit, axis=0, keepdims=True)
            scaled = gain * d_normed
            mean = jnp.mean(mixed * scaled, axis=-1, keepdims=True)
            d_mixed = low_type(rs * scaled - mixed * (rs * rs * rs * mean))

            q_full = self.proj[r, q_cols] * SCALE * grow[:, k]
            key_rows = self.proj[r, k_cols]
            kb_full = key_rows * fade[:, k]
            kt_full = key_rows * late[:, k]
            values = self.pval[r, v]
            q_gate, k_back, k_tail = low_type(q_full), low_type(kb_full), low_type(kt_full)
            probs = low_type(jnp.where(causal, mm_nt(q_gate, k_back), 0.0))
            d_probs = low_type(jnp.where(causal, mm_nt(d_mixed, values), 0.0))
            d_q = mm_nn(d_probs, k_back)
            d_kb = mm_tn(d_probs, q_gate)
            d_v = mm_tn(probs, d_mixed)
            cuts = [slice(b * BLOCK, (b + 1) * BLOCK) for b in range(BLOCKS)]
            before = [None, mm_tn(values[cuts[0]], k_tail[cuts[0]])]
            decay = [jnp.exp(tails[b][:, k]) for b in range(BLOCKS)]
            for b in range(2, BLOCKS):
                before.append(
                    before[b - 1] * decay[b - 1] + mm_tn(values[cuts[b - 1]], k_tail[cuts[b - 1]])
                )
            after = [None] * BLOCKS
            for b in range(BLOCKS - 1, 0, -1):
                d_before = mm_tn(d_mixed[cuts[b]], q_gate[cuts[b]])
                after[b - 1] = d_before if after[b] is None else d_before + decay[b] * after[b]
            q_parts, t_parts, v_parts, e_parts = [], [], [], []
            for b in range(BLOCKS):
                cut_b = cuts[b]
                part = d_q[cut_b]
                if b > 0:
                    part = part + mm_nn(d_mixed[cut_b], low_type(before[b]))
                q_parts.append(part)
                if after[b] is None:
                    t_parts.append(jnp.zeros((BLOCK, HEAD_KEY), jnp.float32))
                    v_parts.append(d_v[cut_b])
                    e_parts.append(jnp.zeros((1, HEAD_KEY), jnp.float32))
                    continue
                after_low = low_type(after[b])
                d_kt = mm_nn(values[cut_b], after_low)
                t_parts.append(d_kt)
                v_parts.append(d_v[cut_b] + mm_nt(k_tail[cut_b], after_low))
                extra = jnp.sum(d_kt * kt_full[cut_b], axis=0, keepdims=True)
                if b > 0:
                    extra += jnp.sum(after[b] * before[b], axis=0, keepdims=True) * decay[b]
                e_parts.append(extra)
            d_q = jnp.concatenate(q_parts, axis=0)
            d_kt = jnp.concatenate(t_parts, axis=0)
            d_v = jnp.concatenate(v_parts, axis=0)
            self.pval[r, v] = low_type(d_v)
            self.proj[r, q_cols] = wide_type(low_type(d_q * SCALE * grow[:, k]))
            self.proj[r, k_cols] = wide_type(low_type(d_kb * fade[:, k] + d_kt * late[:, k]))
            d_forget_parts.append(d_q * q_full - d_kb * kb_full - d_kt * kt_full)
            tail_parts.append(
                jnp.concatenate(
                    [jnp.broadcast_to(one, (BLOCK, HEAD_KEY)) for one in e_parts], axis=0
                )
            )
        self.dghead[0:1, :] += d_ghead
        d_running = jnp.concatenate(d_forget_parts, axis=1)
        row, col = iota((SEQ, SEQ), 0), iota((SEQ, SEQ), 1)
        later = low_type(jnp.where(same & (col >= row), 1.0, 0.0))
        d_forget = exact_sum(later, d_running) + jnp.concatenate(tail_parts, axis=1)
        d_logits = d_forget * jax.nn.sigmoid(-logits) * (1.0 / 16.0)
        self.dbias[0:1, :] += jnp.sum(d_logits, axis=0, keepdims=True)
        d_logit_low = low_type(d_logits)
        self.dwf[...] += mm_tn(lowrank, d_logit_low)
        self.proj[r, 0:MISC] = wide_type(low_type(mm_nt(d_logit_low, self.wf[...])))

    def d_proj(self, c, rows=slice(None)):
        lo, hi = c * WIDE, min((c + 1) * WIDE, PROJ)
        parts = [
            low_type(ref[rows, at : at + last - first])
            for ref, at, first, last in self.pieces(lo, hi)
        ]
        return parts[0] if len(parts) == 1 else jnp.concatenate(parts, axis=1)

    def first_norm_back(self):
        for c in range(-(-PROJ // WIDE)):
            for r in HALVES:
                d_proj = self.d_proj(c, r)
                part = mm_nt(d_proj, columns(self.wm.at[c], 0, d_proj.shape[1]))
                self.out_sum[r, :] = part if c == 0 else self.out_sum[r, :] + part
        total = jnp.zeros((1, D), jnp.float32)
        for i in range(SEQS):
            r = pl.ds(i * SEQ, SEQ)
            d_val, d_gain = self.norm_back(
                wide_type(self.x[r, :]), self.out_sum[r, :], self.gains[0:1, :], EPS
            )
            total += d_gain
            self.xn1[r, :] = low_type(self.dx_sum[r, :] + d_val)
        self.dgains[0:1, :] = total

    def mixer_grad(self, c, g_ref):
        first = O_AT // WIDE
        lo = O_AT % WIDE
        cut = WIDE - lo
        if c == first + 1:
            put_columns(g_ref, 0, D - cut, low_type(mm_nn(self.turn_a[...], self.xn2[:, cut:D])))
            return
        d_proj = self.d_proj(c)
        grad = mm_nn(self.turn_b[...], d_proj)
        if c == first:
            put_columns(g_ref, lo, WIDE, low_type(mm_nn(self.turn_a[...], self.xn2[:, 0:cut])))
            put_columns(g_ref, 0, lo, low_type(grad))
            return
        if c > 0:
            put_columns(g_ref, 0, WIDE, low_type(grad))
            return
        zero = jnp.zeros
        gains = jnp.concatenate(
            [zero((RANK, D), jnp.float32), self.dgains[...], zero((MISC - RANK - 8, D), jnp.float32)],
            axis=0,
        )
        small = mm_tn(low_type(gains), unit_matrix(MISC))
        keyed = jnp.concatenate(
            [
                zero((32, KEY_WIDE), jnp.float32),
                self.dwf[0:RANK, :],
                self.dbias[...],
                zero((MISC - 56, KEY_WIDE), jnp.float32),
            ],
            axis=0,
        )
        small += mm_nt(place_matrix(KEY_WIDE // DEVICES, KEY_WIDE), low_type(keyed))
        lane = iota((MISC, HEAD_VAL), 0)
        headed = jnp.where(lane == 18, jnp.broadcast_to(self.dghead[0:1, :], (MISC, HEAD_VAL)), 0.0)
        small += mm_nt(place_matrix(HEAD_VAL // DEVICES, HEAD_VAL), low_type(headed))
        put_columns(g_ref, 0, MISC, low_type(grad[:, 0:MISC] + small))
        put_columns(g_ref, MISC, WIDE, low_type(grad[:, MISC:WIDE]))


LAYER_SCRATCH = (
    ("small", (MISC, ROWS), jnp.float32),
    ("x", (LIVE, D), jnp.bfloat16),
    ("cot", (LIVE, D), jnp.bfloat16),
    ("xn1", (LIVE, D), jnp.bfloat16),
    ("proj", (LIVE, GATE_AT + VAL_WIDE), jnp.float32),
    ("pval", (LIVE, VAL_WIDE), jnp.bfloat16),
    ("wm", (MIX_CHUNKS - 1, GRP, SQUARE, CORES, ROWS, WIDE), jnp.bfloat16),
    ("wl", (GRP, SQUARE, CORES, ROWS, LAST_WIDE), jnp.bfloat16),
    ("gains", (8, D), jnp.float32),
    ("wf", (MISC, KEY_WIDE), jnp.bfloat16),
    ("bias", (8, KEY_WIDE), jnp.float32),
    ("ghead", (8, HEAD_VAL), jnp.float32),
    ("mixed", (LIVE, D), jnp.float32),
    ("gated", (LIVE, D), jnp.bfloat16),
    ("xn2", (LIVE, D), jnp.bfloat16),
    ("out_sum", (LIVE, D), jnp.float32),
    ("dx_sum", (LIVE, D), jnp.float32),
    ("turn_a", (D, LIVE), jnp.bfloat16),
    ("turn_b", (D, LIVE), jnp.bfloat16),
    ("hid", (LIVE, FF_CUT), jnp.bfloat16),
    ("dpre", (LIVE, 2 * FF_CUT), jnp.bfloat16),
    ("dgains", (8, D), jnp.float32),
    ("dwf", (MISC, KEY_WIDE), jnp.float32),
    ("dbias", (8, KEY_WIDE), jnp.float32),
    ("dghead", (8, HEAD_VAL), jnp.float32),
    ("wb", (2, GRP, SQUARE, CORES, ROWS, WIDE), jnp.bfloat16),
    ("gb", (2, GRP, SQUARE, CORES, ROWS, WIDE), jnp.bfloat16),
)


def fill_parts(parts, small, held):
    lowrank_t, g_attn, g_ffn, g_head, w_forget, b_forget = parts[:6]
    mats = parts[6:]
    small[...] = jnp.zeros_like(small)
    small[0:RANK, :] = wide_type(lowrank_t[...])
    small[RANK : RANK + 1, :] = wide_type(g_attn[...])
    small[RANK + 1 : RANK + 2, :] = wide_type(g_ffn[...])
    small[18:19, 0 : HEAD_VAL // DEVICES] = wide_type(g_head[...])
    small[32 : 32 + RANK, 0 : KEY_WIDE // DEVICES] = wide_type(w_forget[...])
    small[48:49, 0 : KEY_WIDE // DEVICES] = wide_type(b_forget[...])
    held[0, 0, 0, :, 0:MISC] = low_type(mm_tn(low_type(small[...]), unit_matrix(MISC)))
    at = MISC
    for ref in mats[:5]:
        end = at + ref.shape[1]
        for c in range(MIX_CHUNKS):
            lo, hi = max(at, c * WIDE), min(end, (c + 1) * WIDE)
            if lo < hi:
                held[0, c // SQUARE, c % SQUARE, :, lo - c * WIDE : hi - c * WIDE] = ref[
                    :, lo - at : hi - at
                ]
        at = end
    c = MIX_CHUNKS - 1
    held[0, c // SQUARE, c % SQUARE, :, LAST_WIDE:WIDE] = jnp.zeros(
        (ROWS, WIDE - LAST_WIDE), jnp.bfloat16
    )
    for f in range(FF_CHUNKS):
        c = MIX_CHUNKS + f
        for i, ref in enumerate(mats[5:]):
            held[c // 16, c % 16 // SQUARE, c % SQUARE, :, i * FF_CUT : (i + 1) * FF_CUT] = ref[
                :, f * FF_CUT : (f + 1) * FF_CUT
            ]


def layer_kernel(*refs):
    parts, refs = refs[:14], refs[14:]
    (x_in, cot_in, lengths, dealing), refs = refs[:4], refs[4:]
    (out, grad, red, full, grads), scratch = refs[:5], refs[5:]
    count = len(LAYER_SCRATCH)
    refs = {name: ref for (name, _, _), ref in zip(LAYER_SCRATCH, scratch[:count])}
    scratch = scratch[count:]
    g_sems, scratch = scratch[:12], scratch[12:]
    load_sem, store_sem, out_sem = scratch[:3]
    bufs, r_sems = scratch[3:9], scratch[9:]

    place = Place()
    barrier, greeted = place.greet()
    gather = Gather(place, bufs[0], full, g_sems)
    red_op = Reduce(place, grads, red, bufs, r_sems)
    work = Layer(refs)
    x_copy = pltpu.make_async_copy(x_in, work.x, out_sem.at[0])
    cot_copy = pltpu.make_async_copy(cot_in, work.cot, out_sem.at[1])

    def load(c, ref, k):
        return pltpu.make_async_copy(full.at[c], ref, load_sem.at[k])

    def load_ffn(f):
        k = f % 2 if isinstance(f, int) else lax.rem(f, 2)
        return load(MIX_CHUNKS + f, work.wb.at[k], k)

    def load_mixer(c):
        if c == MIX_CHUNKS - 1:
            half = pl.ds(0, LAST_WIDE)
            return pltpu.make_async_copy(
                full.at[c, :, :, :, :, half], work.wl, load_sem.at[0]
            )
        return load(c, work.wm.at[c], 0)

    def store(o, k):
        if isinstance(o, int) and o == NARROW:
            half = pl.ds(0, LAST_WIDE)
            return pltpu.make_async_copy(
                work.gb.at[k, :, :, :, :, half], grads.at[o, :, :, :, :, half], store_sem.at[k]
            )
        return pltpu.make_async_copy(work.gb.at[k], grads.at[o], store_sem.at[k])

    fill_parts(parts, work.small, bufs[0])
    own_copies = gather.locals()
    start_all(own_copies)
    x_copy.start()
    cot_copy.start()
    work.dgains[...] = jnp.zeros_like(work.dgains)
    pl.semaphore_wait(barrier, greeted)
    for c in EARLY:
        start_all(gather.early(c, 0))
    for c in SPREAD:
        gather.spread_first(c)
    for c in range(AHEAD):
        gather.line_out(c)
    gather.pass_on(0)
    for copy in own_copies:
        copy.wait()
    gather.step(0)
    x_copy.wait()
    cot_copy.wait()
    first_seq = (place.z * SHARD + place.s) * SEQS
    work.mask(lengths, dealing, first_seq)
    work.turn(work.cot, work.turn_b)
    for t in range(1, 4):
        gather.step(t)
    load_mixer(0).start()
    load_mixer(0).wait()
    work.prepare()
    for c in range(4):
        gather.step(4 + c)
        load_mixer(c + 1).start()
        work.project(c)
        if c == 3:
            work.attend(0)
            work.attend(1)
        load_mixer(c + 1).wait()
    gather.step(8)
    load_mixer(5).start()
    work.project(4)
    work.attend(2)
    work.attend(3)
    load_mixer(5).wait()
    for i in range(SEQS):
        work.gate_rows(i)
    work.mix_out()
    gather.step(9)
    load_ffn(0).start()
    work.second_norm()

    def ffn_step(f, reduce_too):
        k = lax.rem(f, 2)
        if reduce_too:
            gather.late_step(10 + f)
        else:
            gather.mid_step(10 + f)
        load_ffn(f).wait()
        when(f + 1 < FF_CHUNKS, lambda: load_ffn(f + 1).start())
        when(f >= 2, lambda: store(f - 2, k).wait())
        work.ffn(work.wb.at[k], work.gb.at[k])
        store(f, k).start()
        if reduce_too:
            red_op.step(f - RED_FROM)
        return 0

    def ffn_first(f, carry):
        return ffn_step(f, False)

    def ffn_last(f, carry):
        return ffn_step(f, True)

    lax.fori_loop(0, RED_FROM, ffn_first, 0)
    gather.drain_parts()
    red_op.enter(0)
    lax.fori_loop(RED_FROM, FF_CHUNKS, ffn_last, 0)
    for f in (FF_CHUNKS - 2, FF_CHUNKS - 1):
        store(f, f % 2).wait()
    steps = list(range(FF_CHUNKS - RED_FROM, CHUNKS + 3))

    def reduce_step(ready):
        if steps and steps[0] + 1 < ready:
            red_op.step(steps.pop(0))

    def hand_over(n):
        work.mixer_grad(MIX_ORDER[n], work.gb.at[n % 2])
        copy = store(FF_CHUNKS + n, n % 2)
        copy.start()
        copy.wait()
        reduce_step(FF_CHUNKS + n + 1)

    work.after_ffn()
    out_copy = pltpu.make_async_copy(work.gated, out, out_sem.at[0])
    out_copy.start()
    reduce_step(FF_CHUNKS)
    hand_over(0)
    for i in range(SEQS):
        work.retreat(i)
        reduce_step(FF_CHUNKS + 1)
    for n in range(1, MIX_CHUNKS - 1):
        hand_over(n)
        reduce_step(FF_CHUNKS + n + 1)
    work.first_norm_back()
    grad_copy = pltpu.make_async_copy(work.xn1, grad, out_sem.at[1])
    grad_copy.start()
    reduce_step(CHUNKS - 1)
    hand_over(MIX_CHUNKS - 1)
    while steps:
        red_op.step(steps.pop(0))
    out_copy.wait()
    grad_copy.wait()
    for c in range(CHUNKS):
        gather.drain(c)
    for c in range(CHUNKS - SLOTS, CHUNKS):
        red_op.drain(c)
        red_op.leave(c).wait()


def layer_call(parts, x, cot, lengths, dealing):
    any_spec = pl.BlockSpec(memory_space=pl.ANY)
    vmem = pl.BlockSpec(memory_space=pltpu.VMEM)
    chunk = (CHUNKS, GRP, SQUARE, CORES, ROWS, WIDE)
    rows = jax.ShapeDtypeStruct((LIVE, D), jnp.bfloat16)
    scratch = [pltpu.VMEM(shape, kind) for _, shape, kind in LAYER_SCRATCH]
    scratch += [DMA((5,))] + [DMA((CHUNKS, 3))] * 2 + [DMA((CHUNKS,))] + [DMA((CHUNKS, 2))] * 4 + [DMA((CHUNKS,))] * 2
    scratch += [DMA((len(EARLY), GRP, 2))] * 2
    scratch += [DMA((2,)), DMA((2,)), DMA((2,))]
    scratch += reduce_scratch()
    result = pl.pallas_call(
        layer_kernel,
        out_shape=(
            rows,
            rows,
            jax.ShapeDtypeStruct((CHUNKS, ROWS, WIDE), jnp.float32),
            jax.ShapeDtypeStruct(chunk, jnp.bfloat16),
            jax.ShapeDtypeStruct(chunk, jnp.bfloat16),
        ),
        in_specs=[vmem] * 14 + [any_spec] * 2 + [vmem] * 2,
        out_specs=(any_spec,) * 5,
        scratch_shapes=scratch,
        compiler_params=pltpu.CompilerParams(
            collective_id=0, has_side_effects=True, vmem_limit_bytes=VMEM_LIMIT
        ),
    )(*parts, x, cot, lengths, dealing)
    return result[:3]


def chunk_place(c):
    return FF_CHUNKS + MIX_ORDER.index(c)


def finish_kernel(red, out_in, grad_in, *outs):
    outs[0][...] = out_in[...]
    outs[1][...] = grad_in[...]
    (
        g_attn,
        w_query,
        w_key,
        w_value,
        w_outgate,
        w_lowrank,
        w_forget,
        b_forget,
        g_head,
        w_output,
        g_ffn,
        w_gate,
        w_up,
        w_down,
    ) = outs[2:]
    misc = red[chunk_place(0), :, 0:MISC]
    turned = misc.T
    w_lowrank[...] = turned[0:RANK]
    g_attn[...] = turned[RANK : RANK + 1]
    g_ffn[...] = turned[RANK + 1 : RANK + 2]
    g_head[...] = turned[18:19, 0 : HEAD_VAL // DEVICES]
    w_forget[...] = turned[32 : 32 + RANK, 0 : KEY_WIDE // DEVICES]
    b_forget[...] = turned[48:49, 0 : KEY_WIDE // DEVICES]
    at = MISC
    for ref in (w_query, w_key, w_value, w_outgate, w_output):
        end = at + ref.shape[1]
        for c in range(MIX_CHUNKS):
            lo, hi = max(at, c * WIDE), min(end, (c + 1) * WIDE)
            if lo < hi:
                ref[:, lo - at : hi - at] = red[chunk_place(c), :, lo - c * WIDE : hi - c * WIDE]
        at = end
    for f in range(FF_CHUNKS):
        cut = slice(f * FF_CUT, (f + 1) * FF_CUT)
        w_gate[:, cut] = red[f, :, 0:FF_CUT]
        w_up[:, cut] = red[f, :, FF_CUT : 2 * FF_CUT]
        w_down[:, cut] = red[f, :, 2 * FF_CUT : 3 * FF_CUT]


def finish_call(red, out_rows, grad_rows, shapes):
    vmem = pl.BlockSpec(memory_space=pltpu.VMEM)
    rows = jax.ShapeDtypeStruct(out_rows.shape, out_rows.dtype)
    return pl.pallas_call(
        finish_kernel,
        out_shape=(rows, rows) + tuple(jax.ShapeDtypeStruct(one, jnp.float32) for one in shapes),
        in_specs=[vmem] * 3,
        out_specs=(vmem,) * (2 + len(shapes)),
        compiler_params=pltpu.CompilerParams(vmem_limit_bytes=VMEM_LIMIT),
    )(red, out_rows, grad_rows)


def plain_shards(
    inputs,
    cotangent,
    lengths,
    dealing,
    g_attn,
    w_query,
    w_key,
    w_value,
    w_outgate,
    w_lowrank,
    w_forget,
    b_forget,
    g_head,
    w_output,
    g_ffn,
    w_gate,
    w_up,
    w_down,
):
    axes = ("grp", "shard")
    shard_count = lax.axis_size("shard")
    self_index = lax.axis_index("grp") * shard_count + lax.axis_index("shard")
    seq_dev, max_len, _ = inputs.shape
    own_given = self_index * seq_dev + jnp.arange(seq_dev, dtype=jnp.int32)
    own_len = jnp.sum(jnp.where(dealing[None, :] == own_given[:, None], lengths[None, :], 0), axis=1)
    live = jnp.arange(max_len, dtype=jnp.int32)[None, :] < own_len[:, None]
    zero_low = jnp.zeros((), jnp.bfloat16)
    rows_in = jnp.where(live[..., None], inputs, zero_low).reshape(seq_dev * max_len, D)
    back_in = jnp.where(live[..., None], cotangent, zero_low).reshape(seq_dev * max_len, D)
    shard_weights = (
        g_attn,
        w_query,
        w_key,
        w_value,
        w_outgate,
        w_lowrank,
        w_forget,
        b_forget,
        g_head,
        w_output,
        g_ffn,
        w_gate,
        w_up,
        w_down,
    )
    grad_dims = (0, 0, 0, 0, 0, 0, 1, 0, 0, 0, 0, 0, 0, 1)
    gathered = tuple(
        lax.all_gather(weight, axes, axis=dim, tiled=True)
        for weight, dim in zip(shard_weights, grad_dims)
    )
    out_rows, grad_rows, grads = layer_pass(gathered, rows_in, back_in, seq_dev)
    reduced = tuple(
        lax.psum_scatter(
            grad.astype(jnp.bfloat16), axes, scatter_dimension=dim, tiled=True
        ).astype(jnp.float32)
        for grad, dim in zip(grads, grad_dims)
    )
    return (out_rows.reshape(inputs.shape), grad_rows.reshape(inputs.shape)) + reduced


def kernel_shards(
    inputs,
    cotangent,
    lengths,
    dealing,
    g_attn,
    w_query,
    w_key,
    w_value,
    w_outgate,
    w_lowrank,
    w_forget,
    b_forget,
    g_head,
    w_output,
    g_ffn,
    w_gate,
    w_up,
    w_down,
):
    seq_dev, max_len, _ = inputs.shape
    rows = (seq_dev * max_len, D)
    parts = (
        w_lowrank.T,
        g_attn.reshape(1, -1),
        g_ffn.reshape(1, -1),
        g_head.reshape(1, -1),
        w_forget,
        b_forget.reshape(1, -1),
        w_query,
        w_key,
        w_value,
        w_outgate,
        w_output,
        w_gate,
        w_up,
        w_down.T,
    )
    out_rows, grad_rows, red = layer_call(
        parts,
        inputs.reshape(rows),
        cotangent.reshape(rows),
        lengths.reshape(1, -1),
        dealing.reshape(1, -1),
    )
    weights = (
        g_attn,
        w_query,
        w_key,
        w_value,
        w_outgate,
        w_lowrank,
        w_forget,
        b_forget,
        g_head,
        w_output,
        g_ffn,
        w_gate,
        w_up,
        w_down,
    )
    shapes = [one.shape if one.ndim == 2 else (1,) + one.shape for one in weights]
    turned = (5, 13)
    for i in turned:
        shapes[i] = shapes[i][::-1]
    result = finish_call(red, out_rows, grad_rows, shapes)
    sums = tuple(
        one.T if i in turned else one.reshape(like.shape)
        for i, (one, like) in enumerate(zip(result[2:], weights))
    )
    return (result[0].reshape(inputs.shape), result[1].reshape(inputs.shape)) + sums


def solution(mesh):
    small = mesh.shape["grp"] == GRP and mesh.shape["shard"] == SHARD
    return jax.shard_map(
        kernel_shards if small else plain_shards,
        mesh=mesh,
        in_specs=(
            P(("grp", "shard"), None, None),
            P(("grp", "shard"), None, None),
            P(),
            P(),
            P(("grp", "shard")),
            P(("grp", "shard"), None),
            P(("grp", "shard"), None),
            P(("grp", "shard"), None),
            P(("grp", "shard"), None),
            P(("grp", "shard"), None),
            P(None, ("grp", "shard")),
            P(("grp", "shard")),
            P(("grp", "shard")),
            P(("grp", "shard"), None),
            P(("grp", "shard")),
            P(("grp", "shard"), None),
            P(("grp", "shard"), None),
            P(None, ("grp", "shard")),
        ),
        out_specs=(
            P(("grp", "shard"), None, None),
            P(("grp", "shard"), None, None),
            P(("grp", "shard")),
            P(("grp", "shard"), None),
            P(("grp", "shard"), None),
            P(("grp", "shard"), None),
            P(("grp", "shard"), None),
            P(("grp", "shard"), None),
            P(None, ("grp", "shard")),
            P(("grp", "shard")),
            P(("grp", "shard")),
            P(("grp", "shard"), None),
            P(("grp", "shard")),
            P(("grp", "shard"), None),
            P(("grp", "shard"), None),
            P(None, ("grp", "shard")),
        ),
        check_vma=False,
    )
```
